32 devices in a mesh: dp: 8 (over z, x), slot: 4 (over y, core).
Axes of the slice: x: 2, y: 2, z: 4, core: 2. Of those that a mesh axis runs over, the one named last changes fastest.
Arguments:
- inputs: float32 [16, 1024, 512], P('dp'), may hold values from -6 to 6
- starts: int32 [16, 1024], P('dp'), may hold values 0 or 1
- w_query: bfloat16 [512, 512], P(('dp', 'slot')), may hold values from -0.09375 to 0.09375
- w_key: bfloat16 [512, 512], P(('dp', 'slot')), may hold values from -0.25 to 0.25
- w_value: bfloat16 [512, 512], P(('dp', 'slot')), may hold values from -0.25 to 0.25
- w_out: bfloat16 [512, 512], P(('dp', 'slot')), may hold values from -1 to 1
- w_slot: bfloat16 [512, 512], P('dp', 'slot'), may hold values from -0.25 to 0.25
- w_up: bfloat16 [512, 2048], P('dp', 'slot'), may hold values from -0.25 to 0.25
- w_down: bfloat16 [2048, 512], P('slot', 'dp'), may hold values from -0.125 to 0.125
- gain_attn: bfloat16 [512], P(('dp', 'slot')), may hold values from 0.5 to 1.5
- gain_ffn: bfloat16 [512], P(('dp', 'slot')), may hold values from 0.5 to 1.5
- cotangent: float32 [16, 1024, 512], P('dp'), may hold values from -6 to 6
Outputs:
- output: float32 [16, 1024, 512], P('dp')
- grad_inputs: float32 [16, 1024, 512], P('dp')
- grad_query: float32 [512, 512], P(('dp', 'slot'))
- grad_key: float32 [512, 512], P(('dp', 'slot'))
- grad_value: float32 [512, 512], P(('dp', 'slot'))
- grad_out: float32 [512, 512], P(('dp', 'slot'))
- grad_slot: float32 [512, 512], P('dp', 'slot')
- grad_up: float32 [512, 2048], P('dp', 'slot')
- grad_down: float32 [2048, 512], P('slot', 'dp')
- grad_gain_attn: float32 [512], P(('dp', 'slot'))
- grad_gain_ffn: float32 [512], P(('dp', 'slot'))
The draws below stay inside these ranges and needn't reach their ends.
Inputs may be any that keep to these rules, and one draw needn't show every extreme that they name: A 1 starts a new document at that position; documents never cross rows.
All inputs are finite; a program needn't handle non-finite values. No bound on the sum of `starts` on one device may be relied on, other than what follows from the above.
Results may differ from the reference program's by a relative error of at most 0.022.
Values may be sent and summed in bfloat16 or wider, within the bound.
A program may use at most 192 MiB of HBM per device.

```python
import jax
import jax.numpy as jnp
from jax import lax

D = 512
HEADS = 8
DH = 64
SLOTS = 64
FF = 2048
SEQ = 1024
ROWS = 16


def set_ends(values, stream_key, low, top_value):
    place = [jax.random.randint(jax.random.fold_in(stream_key, axis), (), 0, length) for axis, length in enumerate(values.shape)]
    widest = values.shape.index(max(values.shape))
    neighbour = place[:widest] + [(place[widest] + 1) % values.shape[widest]] + place[widest + 1:]
    return values.at[tuple(place)].set(low).at[tuple(neighbour)].set(top_value)


def block_levels(key, extent, shards, low, largest):
    factor_of, own = 1.0, jax.random.fold_in(key, 6)
    for axis_at, blocks in shards:
        draws = jnp.exp(jax.random.uniform(jax.random.fold_in(own, axis_at), (blocks,), jnp.float32, low / len(shards), largest / len(shards)))
        factor_of = factor_of * jnp.repeat(draws, extent[axis_at] // blocks).reshape([-1 if axis == axis_at else 1 for axis in range(len(extent))])
    return factor_of


def normal_values(stream_key, dims, deviation, limit, pieces=(), kind=jnp.bfloat16):
    drawn = deviation * jax.random.normal(stream_key, dims, jnp.float32)
    if pieces:
        drawn = drawn * block_levels(stream_key, dims, pieces, -0.22, 0.18)
    return jnp.clip(drawn, -limit, limit).astype(kind)


def setup_inputs(seed: int = 0) -> dict:
    splits = jax.random.split(jax.random.key(seed), 13)
    return {
        "inputs": normal_values(splits[0], (ROWS, SEQ, D), 1.0, 6.0, ((0, 8),), jnp.float32),
        "starts": set_ends((jax.random.randint(splits[1], (ROWS, SEQ), 0, SEQ // 4) < 1).astype(jnp.int32), jax.random.fold_in(splits[1], 1), 0, 1),
        "w_query": normal_values(splits[2], (D, D), (8 * D) ** -0.5, 0.09375, ((0, 32),)),
        "w_key": normal_values(splits[3], (D, D), D ** -0.5, 0.25, ((0, 32),)),
        "w_value": normal_values(splits[4], (D, D), D ** -0.5, 0.25, ((0, 32),)),
        "w_out": normal_values(splits[5], (D, D), (D // 16) ** -0.5, 1.0, ((0, 32),)),
        "w_slot": normal_values(splits[6], (D, SLOTS * HEADS), D ** -0.5, 0.25, ((0, 8), (1, 4))),
        "w_up": normal_values(splits[7], (D, FF), D ** -0.5, 0.25, ((0, 8), (1, 4))),
        "w_down": normal_values(splits[8], (FF, D), FF ** -0.5, 0.125, ((0, 4), (1, 8))),
        "gain_attn": jnp.clip(1.0 + 0.1 * jax.random.normal(splits[9], (D,), jnp.float32), 0.5, 1.5).astype(jnp.bfloat16),
        "gain_ffn": jnp.clip(1.0 + 0.1 * jax.random.normal(splits[10], (D,), jnp.float32), 0.5, 1.5).astype(jnp.bfloat16),
        "cotangent": normal_values(splits[11], (ROWS, SEQ, D), 1.0, 6.0, ((0, 8),), jnp.float32),
    }


@jax.custom_vjp
def low(v):
    return lax.optimization_barrier(v.astype(jnp.bfloat16)).astype(jnp.float32)

@jax.custom_vjp
def low_back(v):
    return v

def low_keep(v):
    return (low(v), None)

def low_pass(kept, grad):
    return (grad,)

def back_keep(v):
    return (v, None)

def back_low(kept, grad):
    return (low(grad),)
low.defvjp(low_keep, low_pass)
low_back.defvjp(back_keep, back_low)
PRECISE_MODE = lax.Precision.HIGHEST

def round_both(value):
    return low(low_back(value))

def norm_rows(values, gain_row):
    center = values - lax.optimization_barrier(jnp.mean(values, axis=-1, keepdims=True))
    spread = lax.optimization_barrier(jnp.mean(center * center, axis=-1, keepdims=True))
    return center * lax.rsqrt(spread + 1e-05) * gain_row

def visibility(start_row):
    segment = jnp.cumsum(start_row)
    places = jnp.arange(start_row.shape[0], dtype=jnp.int32)
    allowed = (places[None, :] <= places[:, None]) & (segment[None, :] == segment[:, None])
    return allowed.astype(jnp.float32)

def heads_of(flat_rows):
    return flat_rows.reshape(SEQ, HEADS, DH).transpose(1, 0, 2)

def block_forward(values, visible, w_query, w_key, w_value, w_out, w_slot, w_up, w_down, gain_attn, gain_ffn):
    normed = low(norm_rows(values, gain_attn))
    query_matrix = heads_of(round_both(jnp.dot(normed, w_query, precision=PRECISE_MODE)))
    key_matrix = heads_of(round_both(jnp.dot(normed, w_key, precision=PRECISE_MODE)))
    value_matrix = heads_of(round_both(jnp.dot(normed, w_value, precision=PRECISE_MODE)))
    logits = low_back(jnp.dot(normed, w_slot, precision=PRECISE_MODE))
    slot_weight = round_both(jnp.exp(logits)).reshape(SEQ, SLOTS, HEADS).transpose(2, 0, 1)
    totals = low_back(jnp.einsum('lm,hmc->hlc', visible, slot_weight, precision=PRECISE_MODE))
    unscaled_score = jnp.einsum('qib,qzb->qiz', query_matrix, key_matrix, precision=PRECISE_MODE)
    cross_low = round_both(visible[None] * unscaled_score)
    numerator = low_back(jnp.einsum('hlm,hmc->hlc', cross_low, slot_weight, precision=PRECISE_MODE))
    slot_score = numerator / totals
    slot_top = lax.optimization_barrier(jnp.max(slot_score, axis=-1, keepdims=True))
    shifted = jnp.exp(slot_score - slot_top)
    slot_prob = shifted / lax.optimization_barrier(jnp.sum(shifted, axis=-1, keepdims=True))
    scaled = round_both(slot_prob / totals)
    mixture_narrow = round_both(visible[None] * jnp.einsum('hlc,hmc->hlm', scaled, slot_weight, precision=PRECISE_MODE))
    attended_rows = jnp.einsum('xgq,xqs->xgs', mixture_narrow, value_matrix, precision=PRECISE_MODE)
    merged = round_both(attended_rows.transpose(1, 0, 2).reshape(SEQ, D))
    middle = values + low_back(jnp.dot(merged, w_out, precision=PRECISE_MODE))
    normed_two = low(norm_rows(middle, gain_ffn))
    hidden = low_back(jnp.dot(normed_two, w_up, precision=PRECISE_MODE))
    active = low(jax.nn.gelu(hidden, approximate=False))
    return middle + low_back(jnp.dot(active, w_down, precision=PRECISE_MODE))

def reference(inputs, starts, w_query, w_key, w_value, w_out, w_slot, w_up, w_down, gain_attn, gain_ffn, cotangent):
    params = tuple((weight.astype(jnp.float32) for weight in (w_query, w_key, w_value, w_out, w_slot, w_up, w_down, gain_attn, gain_ffn)))

    def scan_step(carried, scan_item):
        values, start_row, grad_row = scan_item
        visible = visibility(start_row)

        def forward_row(values_in, *weights_in):
            return block_forward(values_in, visible, *weights_in)
        result, pull_back = jax.vjp(forward_row, values, *params)
        row_grads = pull_back(grad_row)
        updated = tuple((total + extra for total, extra in zip(carried, row_grads[1:])))
        return (updated, (result, row_grads[0]))
    zero_grads = tuple((jnp.zeros(weight.shape, jnp.float32) for weight in params))
    summed, (outputs, grad_inputs) = lax.scan(scan_step, zero_grads, (inputs, starts, cotangent))
    return (outputs, grad_inputs, summed[0], summed[1], summed[2], summed[3], summed[4], summed[5], summed[6], summed[7], summed[8])
```

```python
import functools

import jax
import jax.numpy as jnp
from jax import lax
from jax.experimental import pallas as pl
from jax.experimental.pallas import tpu as pltpu
from jax.sharding import PartitionSpec as P

HEADS = 8
EPSILON = 1e-05
NARROW = jnp.bfloat16
WIDE = jnp.float32
MESH = pl.DeviceIdType.MESH

WIDTH = 512
CHUNK = 128
PAIRS = 4
LANES = 128
EARLY = 272
LATE = 576


def dot(a, b):
    return lax.dot_general(a, b, (((1,), (0,)), ((), ())), preferred_element_type=WIDE)


def dot_nt(a, b):
    return lax.dot_general(a, b, (((1,), (1,)), ((), ())), preferred_element_type=WIDE)


def dot_tn(a, b):
    return lax.dot_general(a, b, (((0,), (0,)), ((), ())), preferred_element_type=WIDE)


def low(v):
    return v.astype(NARROW)


def iota2(shape, dim):
    return lax.broadcasted_iota(jnp.int32, shape, dim)


def row_mean(v):
    return jnp.sum(v, axis=-1, keepdims=True) * (1.0 / v.shape[-1])


def norm_parts(v):
    center = v - row_mean(v)
    inv = lax.rsqrt(row_mean(center * center) + EPSILON)
    return center * inv, inv


def norm_back(xhat, inv, gain, up):
    u = up * gain
    return (u - row_mean(u) - xhat * row_mean(u * xhat)) * inv


def owners():
    out = []
    for dp in range(8):
        for slot in range(4):
            z, x, y, c = dp // 2, dp % 2, slot // 2, slot % 2
            a, b = (y, x) if c == 0 else (x, y)
            out.append((dp * 4 + slot, c, a * 8 + b * 4 + z, dp, slot))
    return out


def block_kernel(linked, n_in, n_out, *refs):
    ins, outs, scr = refs[:n_in], refs[n_in : n_in + n_out], refs[n_in + n_out :]
    inputs_ref, starts_ref, cot_ref = ins[:3]
    out_ref, gin_ref = outs[:2]
    (x_v, cot_v, w_first, w_out_v, w_up_v, w_down_v, perm, gains, n1, n1t, proj, expo, score, prob,
     rtot, scaled, att, middle, n2, n2t, gf, gft, acc, gtwo, ga, gproj, gnum, gtot, outb, gone,
     vis, vist, hcar, tail, passf, hcar_n, tail_n, loc, sin, tloc, tin, bd_lo, bd_hi, bdm, xsend, xrecv, tsend, trecv,
     ssem, rsem, lsem) = scr[:51]
    rest = scr[51:]

    slot = lax.axis_index("slot")
    dp = lax.axis_index("dp")
    y, c = slot // 2, slot % 2
    row, half = y, c
    tokens = x_v.shape[0]
    chunks = tokens // CHUNK
    partner = (dp, y * 2 + (1 - c))
    y_peer = (dp, (1 - y) * 2 + c)
    if linked:
        ag1, ag2, rs1, rs2, rc1, rc2, ra1, ra2, rb1, rb2, rz1, rz2 = rest
        z, x = dp // 2, dp % 2
        xa = y + c * (x - y)
        xb = x + c * (y - x)
        place = xa * 8 + xb * 4 + z
        dev_a = ((z * 2 + x + c * (1 - 2 * x)), slot + (1 - c) * 2 * (1 - 2 * y))
        dev_b = ((z * 2 + x + (1 - c) * (1 - 2 * x)), slot + c * 2 * (1 - 2 * y))
        peers = [partner, dev_a, dev_b] + [((((z + s) % 4) * 2 + x), slot) for s in (1, 2, 3)]
    else:
        peers = [partner, y_peer]

    barrier = pltpu.get_barrier_semaphore()
    for peer in peers:
        pl.semaphore_signal(barrier, inc=1, device_id=peer, device_id_type=MESH)

    own_rows = pl.ds(pl.multiple_of(half * tokens, tokens), tokens)
    x_copy = pltpu.make_async_copy(inputs_ref.at[row, own_rows], x_v, lsem.at[0])
    cot_copy = pltpu.make_async_copy(cot_ref.at[row, own_rows], cot_v, lsem.at[1])
    x_copy.start()
    cot_copy.start()

    def remote(src, dst, at, device):
        return pltpu.make_async_remote_copy(
            src_ref=src, dst_ref=dst, send_sem=ssem.at[at], recv_sem=rsem.at[at],
            device_id=device, device_id_type=MESH,
        )

    def gather_z(buf, at):
        return [
            remote(buf.at[c, place], buf.at[c, place], at + s - 1, ((((z + s) % 4) * 2 + x), slot))
            for s in (1, 2, 3)
        ]

    def gather_b(buf, at):
        part = buf.at[c, pl.ds(xa * 8 + xb * 4, 4)]
        return [remote(part, part, at + 3, dev_b), remote(part, part, at + 5, partner)]

    def gather_a(buf, at):
        part = buf.at[c, pl.ds(xa * 8, 8)]
        other = buf.at[c, pl.ds(xa * 8 + (1 - xb) * 4, 4)]
        return [remote(part, part, at + 4, dev_a), remote(other, other, at + 6, partner)]

    def gather_last(buf, at):
        part = buf.at[c, pl.ds((1 - xa) * 8, 8)]
        return [remote(part, part, at + 7, partner)]

    def start(copies):
        for copy in copies:
            copy.start()

    def recv(copies):
        for copy in copies:
            copy.wait_recv()

    def sent(copies):
        for copy in copies:
            copy.wait_send()

    def scatter_core(buf, got, at):
        return remote(buf.at[1 - c], got, at, partner)

    def scatter_a(buf, got, at):
        return remote(buf.at[c, pl.ds((1 - xa) * 8, 8)], got, at + 1, dev_a)

    def scatter_b(buf, got, at):
        return remote(buf.at[c, pl.ds(xa * 8 + (1 - xb) * 4, 4)], got, at + 2, dev_b)

    def scatter_z(buf, got, at):
        return [
            remote(
                buf.at[c, xa * 8 + xb * 4 + (z + s) % 4], got.at[s - 1], at + 2 + s,
                ((((z + s) % 4) * 2 + x), slot),
            )
            for s in (1, 2, 3)
        ]

    def add_blocks(buf, got, first, count):
        def step(i, _):
            at = first + i
            buf[c, at] = low(buf[c, at].astype(WIDE) + got[i].astype(WIDE))
            return 0

        lax.fori_loop(0, count, step, 0)

    LOCAL1, LOCAL2 = 0, 8
    STATE, BACK, OUT, GIN, SC2, SC1 = 16, 18, 20, 23, 26, 32

    ins_w = ins[3:]
    if linked:
        wq, wk, wv, wo, ws, wu, wd, ga1, ga2 = ins_w
        for n, shard in enumerate((wq, wk, wv)):
            for t in range(4):
                ag1[c, place, pl.ds(n * 64 + t * 16, 16), :] = shard[:, t * 128 : t * 128 + 128]
        ag1[c, place, pl.ds(192, 64), :] = ws[...]
        rows16 = iota2((16, 16), 0)
        both = jnp.where(
            rows16 == 0,
            jnp.broadcast_to(ga1[...].astype(WIDE), (16, 16)),
            jnp.where(rows16 == 1, jnp.broadcast_to(ga2[...].astype(WIDE), (16, 16)), 0.0),
        )
        lane_at = ((dp * 4 + slot) % 8) * 16
        spread = jnp.where(iota2((16, 128), 1) == iota2((16, 128), 0) + lane_at, 1.0, 0.0)
        ag1[c, place, pl.ds(256, 16), :] = low(dot(low(both), low(spread)))
        for t in range(4):
            ag2[c, place, pl.ds(t * 16, 16), :] = wo[:, t * 128 : t * 128 + 128]
            ag2[c, place, pl.ds(64 + t * 64, 64), :] = wu[:, t * 128 : t * 128 + 128]
        eye = low(jnp.where(iota2((64, 64), 0) == iota2((64, 64), 1), 1.0, 0.0))
        for t in range(4):
            ag2[c, place, pl.ds(320 + t * 64, 64), :] = low(dot_nt(eye, wd[t * 128 : t * 128 + 128, :]))
        pl.semaphore_wait(barrier, len(peers))
        start(gather_z(ag1, LOCAL1))
    else:
        fw_q, fw_k, fw_v, fw_o, fw_s, fw_u, fw_d, fg1, fg2 = ins_w
        pl.semaphore_wait(barrier, len(peers))
        copies = [
            pltpu.make_async_copy(src, dst, lsem.at[4 + i])
            for i, (src, dst) in enumerate((
                (fw_q, w_first.at[0]), (fw_k, w_first.at[1]), (fw_v, w_first.at[2]), (fw_s, w_first.at[3]),
                (fw_o, w_out_v), (fw_u, w_up_v), (fw_d, w_down_v),
            ))
        ]
        start(copies)
        for copy in copies:
            copy.wait()
        gains[0:1, :] = fg1[...].astype(WIDE)
        gains[1:2, :] = fg2[...].astype(WIDE)

    lane = iota2((CHUNK, LANES), 1)
    sub = iota2((CHUNK, LANES), 0)
    bd_lo[...] = low(jnp.where(lane < 64, 1.0, 0.0))
    bd_hi[...] = low(jnp.where(lane < 64, 0.0, 1.0))
    bdm[...] = jnp.where((lane < 64) == (sub < 64), 1.0, 0.0)
    upper = low(jnp.where(sub <= lane, 1.0, 0.0))
    lower = low(jnp.where(sub >= lane, 1.0, 0.0))
    ones = jnp.ones((CHUNK, LANES), NARROW)
    for n in range(chunks):
        begin = starts_ref[:, pl.ds(pl.multiple_of(half * tokens + n * CHUNK, CHUNK), CHUNK)].astype(WIDE)
        begin = jnp.where(row == 0, begin[0:1], begin[1:2])
        begin = low(jnp.broadcast_to(begin, (CHUNK, LANES)))
        by_lane = dot(begin, upper)
        by_row = dot_nt(lower, begin)
        total = dot(begin, ones)
        same = by_row == by_lane
        v = low(jnp.where(same & (sub >= lane), 1.0, 0.0))
        vt = low(jnp.where(same & (sub <= lane), 1.0, 0.0))
        vis[n, :, 0:128] = v
        vis[n, :, 128:256] = v
        vist[n, :, 0:128] = vt
        vist[n, :, 128:256] = vt
        carried = jnp.where(by_row == 0.0, 1.0, 0.0)
        ending = jnp.where(by_row == total, 1.0, 0.0)
        hcar[n] = carried
        tail[n] = ending
        hcar_n[n] = low(carried)
        tail_n[n] = low(ending)
        passf[n] = jnp.where(total == 0.0, 1.0, 0.0)

    def perm_rows(i, _):
        r = iota2((CHUNK, WIDTH), 0) + i * CHUNK
        n = iota2((CHUNK, WIDTH), 1)
        source = ((n >> 4) & 3) * 128 + (n & 15) * 8 + (n >> 6)
        perm[pl.ds(pl.multiple_of(i * CHUNK, CHUNK), CHUNK), :] = low(jnp.where(r == source, 1.0, 0.0))
        return 0

    lax.fori_loop(0, WIDTH // CHUNK, perm_rows, 0)
    x_copy.wait()

    if linked:
        zs = gather_z(ag1, LOCAL1)
        recv(zs)
        bs = gather_b(ag1, LOCAL1)
        start(bs)
        start(gather_z(ag2, LOCAL2))
        recv(bs[:1])
        as_ = gather_a(ag1, LOCAL1)
        start(as_)
        recv(as_[:1])
        ls = gather_last(ag1, LOCAL1)
        start(ls)
        recv(bs[1:])
        recv(as_[1:])
        recv(ls)
        for index, core, at, odp, oslot in owners():
            for n in range(3):
                for t in range(4):
                    w_first[n, index * 16 : index * 16 + 16, t * 128 : t * 128 + 128] = ag1[
                        core, at, n * 64 + t * 16 : n * 64 + t * 16 + 16, :
                    ]
            w_first[3, odp * 64 : odp * 64 + 64, oslot * 128 : oslot * 128 + 128] = ag1[core, at, 192:256, :]
        for window in range(4):
            total = jnp.zeros((16, 128), WIDE)
            for index, core, at, _, _ in owners():
                if index // 8 == window:
                    total = total + ag1[core, at, 256:272, :].astype(WIDE)
            gains[0:8, window * 128 : window * 128 + 128] = total[0:8]
    w_first[3] = low(dot(w_first[3], perm[...]))

    gain_one = gains[0:1, :]
    gain_two = gains[1:2, :]

    def by_chunk(body):
        def step(i, _):
            body(pl.ds(pl.multiple_of(i * CHUNK, CHUNK), CHUNK), i)
            return 0

        lax.fori_loop(0, chunks, step, 0)

    def norm_one(rows, i):
        xhat, _ = norm_parts(x_v[rows, :])
        n1[rows, :] = low(xhat * gain_one)

    by_chunk(norm_one)
    for n in range(3):
        proj[n] = low(dot(n1[...], w_first[n]))
    expo[...] = jnp.exp(dot(n1[...], w_first[3]))
    proj[3] = low(expo[...])
    n1t[...] = n1[...].T

    def two(v):
        return jnp.concatenate([v * bd_lo[...], v * bd_hi[...]], axis=0)

    def local_states(rows, i):
        w_tail = proj[3, rows, :]
        tloc[i] = jnp.broadcast_to(
            dot(jnp.ones((8, CHUNK), NARROW), w_tail * jnp.concatenate([tail_n[i]] * PAIRS, axis=1)),
            (8, WIDTH),
        )
        for p in range(PAIRS):
            cols = slice(p * 128, p * 128 + 128)
            w = proj[3, rows, cols]
            loc[0, i, p] = dot_tn(proj[1, rows, cols] * tail_n[i], w) * bdm[...]
            loc[1, i, p] = dot_tn(w * tail_n[i], proj[2, rows, cols]) * bdm[...]

    by_chunk(local_states)

    def scan_states(order, initial, t_initial, keep):
        def one(kind, p):
            state = initial(kind, p)
            for i in order:
                if keep:
                    sin[kind, i, p] = low(state)
                state = loc[kind, i, p] + passf[i] * state
            if not keep:
                xsend[kind, p] = state

        def step(k, _):
            one(k // PAIRS, k % PAIRS)
            return 0

        lax.fori_loop(0, 2 * PAIRS, step, 0)
        state = t_initial()
        for i in order:
            if keep:
                tin[i] = state
            state = tloc[i] + jnp.concatenate([passf[i, 0:8, :]] * PAIRS, axis=1) * state
        if not keep:
            tsend[...] = state

    def exchange(at):
        return [remote(xsend, xrecv.at[(at - STATE) // 2], at, partner), remote(tsend, trecv.at[(at - STATE) // 2], at + 1, partner)]

    def scan_and_carry(order, at, takes):
        n = (at - STATE) // 2
        scan_states(order, lambda k, p: jnp.zeros((128, 128), WIDE), lambda: jnp.zeros((8, WIDTH), WIDE), False)
        copies = exchange(at)
        start(copies)
        recv(copies)
        scan_states(order, lambda k, p: xrecv[n, k, p] * takes, lambda: trecv[n] * takes, True)

    forward = list(range(chunks))
    takes_forward = half.astype(WIDE)
    scan_and_carry(forward, STATE, takes_forward)

    if linked:
        zs2 = gather_z(ag2, LOCAL2)
        bs2 = gather_b(ag2, LOCAL2)
        as2 = gather_a(ag2, LOCAL2)
        ls2 = gather_last(ag2, LOCAL2)
        recv(zs2)
        start(bs2)

    first_half = iota2((CHUNK, LANES), 1) < 64

    def over_heads(lo_part, hi_part):
        return jnp.where(first_half, lo_part, hi_part)

    def head_max(v):
        return over_heads(
            jnp.max(jnp.where(first_half, v, -jnp.inf), axis=-1, keepdims=True),
            jnp.max(jnp.where(first_half, -jnp.inf, v), axis=-1, keepdims=True),
        )

    def head_sum(v):
        return over_heads(
            jnp.sum(jnp.where(first_half, v, 0.0), axis=-1, keepdims=True),
            jnp.sum(jnp.where(first_half, 0.0, v), axis=-1, keepdims=True),
        )

    def attend(rows, i):
        mask = vis[i]
        carried = hcar[i]
        totals = dot(mask[:, 0:128], proj[3, rows, :]) + jnp.concatenate([carried] * PAIRS, axis=1) * tin[i, 0:1, :]
        rtot[rows, :] = 1.0 / totals
        for p in range(PAIRS):
            cols = slice(p * 128, p * 128 + 128)
            q, k, v, w = (proj[n, rows, cols] for n in range(4))
            w2 = two(w)
            r = rtot[rows, cols]
            cross = low(dot_nt(q, two(k))) * mask
            s = (dot(cross, w2) + carried * dot(q, sin[0, i, p])) * r
            e = jnp.exp(s - head_max(s))
            pr = e / head_sum(e)
            sc = low(pr * r)
            mix = low(dot_nt(sc, w2)) * mask
            score[rows, cols] = s
            prob[rows, cols] = pr
            scaled[rows, cols] = sc
            att[rows, cols] = low(dot(mix, two(v)) + carried * dot(sc, sin[1, i, p]))

    by_chunk(attend)

    if linked:
        recv(bs2[:1])
        start(as2)
        recv(as2[:1])
        start(ls2)
        recv(bs2[1:])
        recv(as2[1:])
        recv(ls2)
        for index, core, at, odp, oslot in owners():
            for t in range(4):
                cols = slice(t * 128, t * 128 + 128)
                w_out_v[index * 16 : index * 16 + 16, cols] = ag2[core, at, t * 16 : t * 16 + 16, :]
                w_up_v[oslot, odp * 64 : odp * 64 + 64, cols] = ag2[core, at, 64 + t * 64 : 128 + t * 64, :]
                w_down_v[oslot, odp * 64 : odp * 64 + 64, cols] = ag2[core, at, 320 + t * 64 : 384 + t * 64, :]

    middle[...] = x_v[...] + dot(att[...], w_out_v[...])
    cot_copy.wait()

    def norm_two(rows, i):
        xhat, _ = norm_parts(middle[rows, :])
        n2[rows, :] = low(xhat * gain_two)
        gf[rows, :] = low(cot_v[rows, :])
        acc[rows, :] = jnp.zeros((CHUNK, WIDTH), WIDE)
        gtwo[rows, :] = jnp.zeros((CHUNK, WIDTH), WIDE)

    by_chunk(norm_two)
    n2t[...] = n2[...].T
    gft[...] = gf[...].T

    def feed(j, _):
        hidden = dot(n2[...], w_up_v[j])
        cdf = 0.5 * (1.0 + lax.erf(hidden * 0.7071067811865476))
        active = low(hidden * cdf)
        slope = cdf + hidden * (jnp.exp(-0.5 * hidden * hidden) * 0.3989422804014327)
        grad_hidden = low(dot(gf[...], w_down_v[j]) * slope)
        acc[...] += dot_nt(active, w_down_v[j])
        gtwo[...] += dot_nt(grad_hidden, w_up_v[j])
        g_up = low(dot(n2t[...], grad_hidden))
        g_down = low(dot(gft[...], active))
        if linked:
            jy, jc = j // 2, j % 2
            for odp in range(8):
                oz, ox = odp // 2, odp % 2
                at = (jy + jc * (ox - jy)) * 8 + (ox + jc * (jy - ox)) * 4 + oz
                for t in range(4):
                    rows, cols = slice(odp * 64, odp * 64 + 64), slice(t * 128, t * 128 + 128)
                    rs2[jc, at, pl.ds(64 + t * 64, 64), :] = g_up[rows, cols]
                    rs2[jc, at, pl.ds(320 + t * 64, 64), :] = g_down[rows, cols]
        else:
            outs[7][j] = g_up
            outs[8][j] = g_down
        return 0

    lax.fori_loop(0, 4, feed, 0)

    def spread_output(target, base):
        mine = target.at[row, own_rows]
        ycopy = remote(outb, mine, base, y_peer)
        ccopy = remote(outb, mine, base + 1, partner)
        lcopy = pltpu.make_async_copy(outb, mine, lsem.at[2 + (base - OUT) // 3])
        theirs = target.at[1 - row, own_rows]
        forward_copy = remote(theirs, theirs, base + 2, partner)
        return ycopy, ccopy, lcopy, forward_copy

    def norm_two_back(rows, i):
        outb[rows, :] = low(middle[rows, :] + acc[rows, :])
        xhat, inv = norm_parts(middle[rows, :])
        up = gtwo[rows, :]
        grad = cot_v[rows, :] + norm_back(xhat, inv, gain_two, up)
        cot_v[rows, :] = grad
        gf[rows, :] = low(grad)
        gains[3:4, :] = gains[3:4, :] + jnp.sum(up * xhat, axis=0, keepdims=True)

    gains[2:8, :] = jnp.zeros((6, WIDTH), WIDE)
    by_chunk(norm_two_back)
    oy, oc, ol, of = spread_output(out_ref, OUT)
    oy.start()
    oc.start()
    ol.start()
    ga[...] = low(dot_nt(gf[...], w_out_v[...]))
    g_out = low(dot_tn(att[...], gf[...]))
    if linked:
        for index, core, at, _, _ in owners():
            for t in range(4):
                rs2[core, at, t * 16 : t * 16 + 16, :] = g_out[index * 16 : index * 16 + 16, t * 128 : t * 128 + 128]
        c2 = scatter_core(rs2, rc2, SC2)
        c2.start()
    else:
        outs[5][...] = g_out

    def back_first(rows, i):
        mask = vis[i]
        carried = hcar[i]
        carried_n = hcar_n[i]
        for p in range(PAIRS):
            cols = slice(p * 128, p * 128 + 128)
            q, k, v, w = (proj[n, rows, cols] for n in range(4))
            w2 = two(w)
            g = ga[rows, cols]
            r, pr, s = rtot[rows, cols], prob[rows, cols], score[rows, cols]
            gmix = low(dot_nt(g, two(v))) * mask
            gs = low(dot(gmix, w2) + carried * dot_nt(g, sin[1, i, p])).astype(WIDE)
            gp = gs * r
            gscore = pr * (gp - head_sum(pr * gp))
            gt = low(-(gs * pr * r + gscore * s) * r)
            gn = low(gscore * r)
            gcross = low(dot_nt(gn, w2)) * mask
            gproj[0, rows, cols] = low(dot(gcross, two(k)) + carried * dot_nt(gn, sin[0, i, p]))
            gnum[rows, cols] = gn
            gtot[rows, cols] = gt
            loc[0, i, p] = dot_tn(q * carried_n, gn) * bdm[...]
            loc[1, i, p] = dot_tn(g * carried_n, scaled[rows, cols]) * bdm[...]
        tloc[i] = jnp.broadcast_to(
            dot(jnp.ones((8, CHUNK), NARROW), gtot[rows, :] * jnp.concatenate([carried_n] * PAIRS, axis=1)),
            (8, WIDTH),
        )

    by_chunk(back_first)
    if linked:
        c2.wait_recv()
        add_blocks(rs2, rc2, 0, 16)
        a2 = scatter_a(rs2, ra2, SC2)
        a2.start()
    oy.wait_recv()
    of.start()
    sent(exchange(STATE))
    scan_and_carry(forward[::-1], BACK, 1.0 - takes_forward)

    def back_second(rows, i):
        mask = vist[i]
        ends = tail[i]
        wc = dot(mask[:, 0:128], gtot[rows, :]) + jnp.concatenate([ends] * PAIRS, axis=1) * tin[i, 0:1, :]
        for p in range(PAIRS):
            cols = slice(p * 128, p * 128 + 128)
            q, k, v, w = (proj[n, rows, cols] for n in range(4))
            g, sc, gn = ga[rows, cols], scaled[rows, cols], gnum[rows, cols]
            g2, sc2, gn2, q2 = two(g), two(sc), two(gn), two(q)
            s_query, s_grad = sin[0, i, p], sin[1, i, p]
            gmix = low(dot_nt(v, g2)) * mask
            mix = low(dot_nt(w, sc2)) * mask
            gcross = low(dot_nt(w, gn2)) * mask
            cross = low(dot_nt(k, q2)) * mask
            gw = dot(gmix, sc2) + dot(cross, gn2) + ends * (dot(v, s_grad) + dot(k, s_query)) + wc[:, cols]
            gproj[3, rows, cols] = low(low(gw).astype(WIDE) * expo[rows, cols])
            gproj[2, rows, cols] = low(dot(mix, g2) + ends * dot_nt(w, s_grad))
            gproj[1, rows, cols] = low(dot(gcross, q2) + ends * dot_nt(w, s_query))

    by_chunk(back_second)

    gone[...] = dot_nt(gproj[0], w_first[0])
    for n in range(1, 4):
        gone[...] += dot_nt(gproj[n], w_first[n])
    ol.wait()
    oy.wait_send()
    oc.wait_send()

    def norm_one_back(rows, i):
        xhat, inv = norm_parts(x_v[rows, :])
        up = gone[rows, :]
        outb[rows, :] = low(cot_v[rows, :] + norm_back(xhat, inv, gain_one, up))
        gains[2:3, :] = gains[2:3, :] + jnp.sum(up * xhat, axis=0, keepdims=True)

    by_chunk(norm_one_back)
    iy, ic, il, if_ = spread_output(gin_ref, GIN)
    iy.start()
    ic.start()
    il.start()

    for n in range(4):
        grad = low(dot(n1t[...], gproj[n]))
        if n == 3:
            grad = low(dot_nt(grad, perm[...]))
        if not linked:
            outs[(2, 3, 4, 6)[n]][...] = grad
            continue
        for index, core, at, odp, oslot in owners():
            if n == 3:
                rs1[core, at, 192:256, :] = grad[odp * 64 : odp * 64 + 64, oslot * 128 : oslot * 128 + 128]
            else:
                for t in range(4):
                    rs1[core, at, n * 64 + t * 16 : n * 64 + t * 16 + 16, :] = grad[
                        index * 16 : index * 16 + 16, t * 128 : t * 128 + 128
                    ]
    if linked:
        for index, core, at, _, _ in owners():
            window = index // 8
            rs1[core, at, 256:272, :] = low(
                jnp.concatenate(
                    [gains[2:4, window * 128 : window * 128 + 128], jnp.zeros((14, 128), WIDE)], axis=0
                )
            )
        c1 = scatter_core(rs1, rc1, SC1)
        c1.start()
        a2.wait_recv()
        add_blocks(rs2, ra2, xa * 8, 8)
        b2 = scatter_b(rs2, rb2, SC2)
        b2.start()
        c1.wait_recv()
        add_blocks(rs1, rc1, 0, 16)
        a1 = scatter_a(rs1, ra1, SC1)
        a1.start()
        b2.wait_recv()
        add_blocks(rs2, rb2, xa * 8 + xb * 4, 4)
        z2 = scatter_z(rs2, rz2, SC2)
        start(z2)
        a1.wait_recv()
        add_blocks(rs1, ra1, xa * 8, 8)
        b1 = scatter_b(rs1, rb1, SC1)
        b1.start()
        b1.wait_recv()
        add_blocks(rs1, rb1, xa * 8 + xb * 4, 4)
        z1 = scatter_z(rs1, rz1, SC1)
        start(z1)
        iy.wait_recv()
        if_.start()
        recv(z2)

        def summed(buf, got, first, count):
            rows = pl.ds(first, count)
            total = buf[c, place, rows, :].astype(WIDE)
            for s in range(3):
                total = total + got[s, rows, :].astype(WIDE)
            return total

        oq, ok, ov, oo, os_, ou, od, og = outs[2:]
        for t in range(4):
            cols = slice(t * 128, t * 128 + 128)
            oo[:, cols] = summed(rs2, rz2, t * 16, 16)
            ou[:, cols] = summed(rs2, rz2, 64 + t * 64, 64)
            od[:, cols] = summed(rs2, rz2, 320 + t * 64, 64)
        recv(z1)
        for n, target in enumerate((oq, ok, ov)):
            for t in range(4):
                target[:, t * 128 : t * 128 + 128] = summed(rs1, rz1, n * 64 + t * 16, 16)
        os_[...] = summed(rs1, rz1, 192, 64)
        og[...] = summed(rs1, rz1, 256, 16)
    else:
        outs[9][...] = gains[2:4, :]
        iy.wait_recv()
        if_.start()

    oc.wait_recv()
    of.wait()
    il.wait()
    iy.wait_send()
    ic.wait()
    if_.wait()
    sent(exchange(BACK))
    if linked:
        for buf, at in ((ag1, LOCAL1), (ag2, LOCAL2)):
            sent(gather_z(buf, at) + gather_b(buf, at) + gather_a(buf, at) + gather_last(buf, at))
        sent([c1, c2, a1, a2, b1, b2] + z1 + z2)


def run_block(linked, inputs, starts, cotangent, weights):
    rows, length, width = inputs.shape
    tokens = length // 2
    chunks = tokens // CHUNK
    vm = pltpu.VMEM
    scratch = [
        vm((tokens, width), WIDE), vm((tokens, width), WIDE),
        vm((4, width, width), NARROW), vm((width, width), NARROW),
        vm((4, width, width), NARROW), vm((4, width, width), NARROW),
        vm((width, width), NARROW), vm((8, width), WIDE),
        vm((tokens, width), NARROW), vm((width, tokens), NARROW),
        vm((4, tokens, width), NARROW), vm((tokens, width), WIDE),
        vm((tokens, width), WIDE), vm((tokens, width), WIDE), vm((tokens, width), WIDE),
        vm((tokens, width), NARROW), vm((tokens, width), NARROW),
        vm((tokens, width), WIDE), vm((tokens, width), NARROW), vm((width, tokens), NARROW),
        vm((tokens, width), NARROW), vm((width, tokens), NARROW),
        vm((tokens, width), WIDE), vm((tokens, width), WIDE),
        vm((tokens, width), NARROW), vm((4, tokens, width), NARROW),
        vm((tokens, width), NARROW), vm((tokens, width), NARROW),
        vm((tokens, width), NARROW), vm((tokens, width), WIDE),
        vm((chunks, CHUNK, 256), NARROW), vm((chunks, CHUNK, 256), NARROW),
        vm((chunks, CHUNK, LANES), WIDE), vm((chunks, CHUNK, LANES), WIDE), vm((chunks, CHUNK, LANES), WIDE),
        vm((chunks, CHUNK, LANES), NARROW), vm((chunks, CHUNK, LANES), NARROW),
        vm((2, chunks, PAIRS, 128, 128), WIDE), vm((2, chunks, PAIRS, 128, 128), NARROW),
        vm((chunks, 8, width), WIDE), vm((chunks, 8, width), WIDE),
        vm((CHUNK, LANES), NARROW), vm((CHUNK, LANES), NARROW), vm((CHUNK, LANES), WIDE),
        vm((2, PAIRS, 128, 128), WIDE), vm((2, 2, PAIRS, 128, 128), WIDE),
        vm((8, width), WIDE), vm((2, 8, width), WIDE),
        pltpu.SemaphoreType.DMA((40,)), pltpu.SemaphoreType.DMA((40,)), pltpu.SemaphoreType.DMA((12,)),
    ]
    if linked:
        scratch += [
            vm((2, 16, EARLY, LANES), NARROW), vm((2, 16, LATE, LANES), NARROW),
            vm((2, 16, EARLY, LANES), NARROW), vm((2, 16, LATE, LANES), NARROW),
            vm((16, EARLY, LANES), NARROW), vm((16, LATE, LANES), NARROW),
            vm((8, EARLY, LANES), NARROW), vm((8, LATE, LANES), NARROW),
            vm((4, EARLY, LANES), NARROW), vm((4, LATE, LANES), NARROW),
            vm((3, EARLY, LANES), NARROW), vm((3, LATE, LANES), NARROW),
        ]
    anywhere = pl.BlockSpec(memory_space=pl.ANY)
    here = pl.BlockSpec(memory_space=pltpu.VMEM)
    shape = jax.ShapeDtypeStruct
    big = [shape((rows, length, width), NARROW)] * 2
    square = (width, width)
    if linked:
        small = [shape((16, width), WIDE)] * 4 + [
            shape((64, 128), WIDE), shape((64, width), WIDE), shape((64, width), WIDE), shape((16, 128), WIDE)
        ]
        weight_specs = [here] * 9
    else:
        small = [shape(square, NARROW)] * 5 + [shape((4, *square), NARROW)] * 2 + [shape((2, width), WIDE)]
        weight_specs = [anywhere] * 7 + [here] * 2
    return pl.pallas_call(
        functools.partial(block_kernel, linked, 12, 2 + len(small)),
        out_shape=big + small,
        in_specs=[anywhere, here, anywhere] + weight_specs,
        out_specs=[anywhere] * 2 + [here] * len(small),
        scratch_shapes=scratch,
        compiler_params=pltpu.CompilerParams(
            collective_id=0, has_side_effects=True, vmem_limit_bytes=62 * 1024 * 1024
        ),
    )(inputs, starts, cotangent, *weights)


def on_device(
    inputs, starts, w_query, w_key, w_value, w_out, w_slot, w_up, w_down, gain_attn, gain_ffn, cotangent
):
    n_dp, n_slot = lax.axis_size("dp"), lax.axis_size("slot")
    if n_dp == 8 and n_slot == 4:
        weights = (
            w_query, w_key, w_value, w_out, w_slot, w_up, w_down,
            gain_attn.reshape(1, -1), gain_ffn.reshape(1, -1),
        )
        out, gin, gq, gk, gv, go, gs, gu, gd, gg = run_block(True, inputs, starts, cotangent, weights)
        at = ((lax.axis_index("dp") * n_slot + lax.axis_index("slot")) % 8) * 16
        gains = lax.dynamic_slice(gg, (0, at), (2, 16))
        return (
            out.astype(WIDE), gin.astype(WIDE), gq, gk, gv, go, gs, gu, gd.T, gains[0], gains[1],
        )

    def whole(v, names, axis):
        return lax.all_gather(v, names, axis=axis, tiled=True)

    both = ("dp", "slot")
    width = inputs.shape[-1]
    up = whole(whole(w_up, "dp", 0), "slot", 1).reshape(width, n_slot, -1).transpose(1, 0, 2)
    down = whole(whole(w_down, "dp", 1), "slot", 0).reshape(n_slot, -1, width).transpose(0, 2, 1)
    weights = (
        whole(w_query, both, 0), whole(w_key, both, 0), whole(w_value, both, 0), whole(w_out, both, 0),
        whole(whole(w_slot, "dp", 0), "slot", 1), up, down,
        whole(gain_attn, both, 0).reshape(1, -1), whole(gain_ffn, both, 0).reshape(1, -1),
    )
    out, gin, gq, gk, gv, go, gs, gu, gd, gg = run_block(False, inputs, starts, cotangent, weights)

    def shared(v, names, axis):
        return lax.psum_scatter(v.astype(WIDE), names, scatter_dimension=axis, tiled=True)

    gu = gu.transpose(1, 0, 2).reshape(width, -1)
    gd = gd.transpose(0, 2, 1).reshape(-1, width)
    return (
        out.astype(WIDE), gin.astype(WIDE),
        shared(gq, both, 0), shared(gk, both, 0), shared(gv, both, 0), shared(go, both, 0),
        shared(shared(gs, "slot", 1), "dp", 0), shared(shared(gu, "slot", 1), "dp", 0),
        shared(shared(gd, "slot", 0), "dp", 1), shared(gg[0], both, 0), shared(gg[1], both, 0),
    )


def solution(mesh):
    every = ("dp", "slot")
    rows = P("dp", None, None)
    return jax.shard_map(
        on_device,
        mesh=mesh,
        in_specs=(
            rows, P("dp", None), P(every, None), P(every, None), P(every, None), P(every, None),
            P("dp", "slot"), P("dp", "slot"), P("slot", "dp"), P(every), P(every), rows,
        ),
        out_specs=(
            rows, rows, P(every, None), P(every, None), P(every, None), P(every, None),
            P("dp", "slot"), P("dp", "slot"), P("slot", "dp"), P(every), P(every),
        ),
        check_vma=False,
    )
```

```python
import functools

import jax
import jax.numpy as jnp
from jax import lax
from jax.experimental import pallas as pl
from jax.experimental.pallas import tpu as pltpu
from jax.sharding import PartitionSpec as P

HEADS = 8
EPSILON = 1e-05
NARROW = jnp.bfloat16
WIDE = jnp.float32
MESH = pl.DeviceIdType.MESH

WIDTH = 512
CHUNK = 128
PAIRS = 4
LANES = 128
PIECE_ROWS = (80, 64, 64, 64, 64, 128, 128, 128, 128)
SLOT, KEY, VALUE, QUERY, OUT_W, TILE = range(6)
SMALL_ROWS = sum(PIECE_ROWS)
GATHER_SEMS, SCATTER_SEMS = 8, 6


def dot(a, b):
    return lax.dot_general(a, b, (((1,), (0,)), ((), ())), preferred_element_type=WIDE)


def dot_nt(a, b):
    return lax.dot_general(a, b, (((1,), (1,)), ((), ())), preferred_element_type=WIDE)


def dot_tn(a, b):
    return lax.dot_general(a, b, (((0,), (0,)), ((), ())), preferred_element_type=WIDE)


def low(v):
    return v.astype(NARROW)


def iota2(shape, dim):
    return lax.broadcasted_iota(jnp.int32, shape, dim)


def row_mean(v):
    return jnp.sum(v, axis=-1, keepdims=True) * (1.0 / v.shape[-1])


def norm_parts(v):
    center = v - row_mean(v)
    inv = lax.rsqrt(row_mean(center * center) + EPSILON)
    return center * inv, inv


def norm_back(xhat, inv, gain, up):
    u = up * gain
    return (u - row_mean(u) - xhat * row_mean(u * xhat)) * inv


def owners(mixed):
    out = []
    for dp in range(8):
        for slot in range(4):
            z, x, y, c = dp // 2, dp % 2, slot // 2, slot % 2
            a, b = (y, x) if c == 0 and mixed else (x, y)
            out.append((dp * 4 + slot, c, a * 8 + b * 4 + z, dp, slot))
    return out


def square_of(buf):
    return jnp.concatenate(
        [
            jnp.concatenate([buf[core, at, t * 16 : t * 16 + 16, :] for t in range(4)], axis=1)
            for _, core, at, _, _ in owners(True)
        ],
        axis=0,
    )


def tile_of(buf, n, first):
    place = {(dp, slot): (core, at) for _, core, at, dp, slot in owners(True)}
    return jnp.concatenate(
        [
            jnp.concatenate(
                [buf[(n, *place[dp, slot], slice(first, first + 64), slice(None))] for dp in range(8)], axis=0
            )
            for slot in range(4)
        ],
        axis=1,
    )


def block_kernel(linked, n_in, n_out, *refs):
    ins, outs, scr = refs[:n_in], refs[n_in : n_in + n_out], refs[n_in + n_out :]
    inputs_ref, starts_ref, cot_ref = ins[:3]
    out_ref, gin_ref = outs[:2]
    (x_v, cot_v, w_slot, perm, gains, n1, n1t, proj, expo, score, prob,
     rtot, scaled, att, mid, acc, n2, n2t, gf, gft, gtwo, ga, gproj, gnum, gtot, outb, ginb,
     vis, vist, hcar, tail, passf, hcar_n, tail_n, loc, sin, tloc, tin, bd_lo, bd_hi, bdm, xsend, xrecv, tsend, trecv,
     ssem, rsem, lsem) = scr[:48]
    rest = scr[48:]

    slot = lax.axis_index("slot")
    dp = lax.axis_index("dp")
    y, c = slot // 2, slot % 2
    row, half = y, c
    tokens = x_v.shape[0]
    chunks = tokens // CHUNK
    partner = (dp, y * 2 + (1 - c))
    y_peer = (dp, (1 - y) * 2 + c)
    if linked:
        ags, rss, rcs, ras, rbs, rzs = (rest[6 * n : 6 * n + 6] for n in range(6))
        z, x = dp // 2, dp % 2
        xa = y + c * (x - y)
        xb = x + c * (y - x)
        place = xa * 8 + xb * 4 + z
        own = x * 8 + y * 4 + z
        x_peer = (z * 2 + 1 - x, slot)
        dev_a = ((z * 2 + x + c * (1 - 2 * x)), slot + (1 - c) * 2 * (1 - 2 * y))
        dev_b = ((z * 2 + x + (1 - c) * (1 - 2 * x)), slot + c * 2 * (1 - 2 * y))
        z_peers = [((((z + s) % 4) * 2 + x), slot) for s in (1, 2, 3)]
        peers = [partner, x_peer, y_peer] + z_peers
    else:
        peers = [partner, y_peer]

    barrier = pltpu.get_barrier_semaphore()
    for peer in peers:
        pl.semaphore_signal(barrier, inc=1, device_id=peer, device_id_type=MESH)

    own_rows = pl.ds(pl.multiple_of(half * tokens, tokens), tokens)
    x_copy = pltpu.make_async_copy(inputs_ref.at[row, own_rows], x_v, lsem.at[0])
    cot_copy = pltpu.make_async_copy(cot_ref.at[row, own_rows], cot_v, lsem.at[1])
    x_copy.start()
    cot_copy.start()

    def remote(src, dst, at, device):
        return pltpu.make_async_remote_copy(
            src_ref=src, dst_ref=dst, send_sem=ssem.at[at], recv_sem=rsem.at[at],
            device_id=device, device_id_type=MESH,
        )

    def start(copies):
        for copy in copies:
            copy.start()

    def recv(copies):
        for copy in copies:
            copy.wait_recv()

    def sent(copies):
        for copy in copies:
            copy.wait_send()

    def view(bufs, n):
        return bufs[n] if isinstance(n, int) and n < TILE else bufs[TILE].at[n - TILE]

    def gather_z(n):
        mine, at = view(ags, n).at[c, place], n * GATHER_SEMS
        return [remote(mine, mine, at + s, z_peers[s]) for s in range(3)]

    def gather_b(n):
        part, at = view(ags, n).at[c, pl.ds(xa * 8 + xb * 4, 4)], n * GATHER_SEMS
        return [remote(part, part, at + 3, dev_b), remote(part, part, at + 5, partner)]

    def gather_a(n):
        buf, at = view(ags, n), n * GATHER_SEMS
        part = buf.at[c, pl.ds(xa * 8, 8)]
        other = buf.at[c, pl.ds(xa * 8 + (1 - xb) * 4, 4)]
        return [remote(part, part, at + 4, dev_a), remote(other, other, at + 6, partner)]

    def gather_last(n):
        part = view(ags, n).at[c, pl.ds((1 - xa) * 8, 8)]
        return [remote(part, part, n * GATHER_SEMS + 7, partner)]

    def gather_step(n, stage):
        if stage == 0:
            start(gather_z(n))
        elif stage == 1:
            recv(gather_z(n))
            start(gather_b(n))
        elif stage == 2:
            recv(gather_b(n)[:1])
            start(gather_a(n))
        elif stage == 3:
            recv(gather_a(n)[:1])
            start(gather_last(n))
        else:
            recv(gather_b(n)[1:] + gather_a(n)[1:] + gather_last(n))

    def scatter_copies(n, stage):
        buf, at = view(rss, n), SCATTER + n * SCATTER_SEMS
        if stage == 0:
            return [remote(buf.at[1 - c], view(rcs, n), at, partner)]
        if stage == 1:
            return [remote(buf.at[c, pl.ds((1 - x) * 8, 8)], view(ras, n), at + 1, x_peer)]
        if stage == 2:
            return [remote(buf.at[c, pl.ds(x * 8 + (1 - y) * 4, 4)], view(rbs, n), at + 2, y_peer)]
        got = view(rzs, n)
        return [
            remote(buf.at[c, x * 8 + y * 4 + (z + s + 1) % 4], got.at[s], at + 3 + s, z_peers[s])
            for s in range(3)
        ]

    def scatter_step(n, stage, rows):
        if stage:
            recv(scatter_copies(n, stage - 1))
            buf = view(rss, n)
            if stage < 4:
                got = view((rcs, ras, rbs)[stage - 1], n)
                first, count = ((0, 16), (x * 8, 8), (x * 8 + y * 4, 4))[stage - 1]

                def step(i, _):
                    at = first + i
                    buf[c, at] = low(buf[c, at].astype(WIDE) + got[i].astype(WIDE))
                    return 0

                lax.fori_loop(0, count, step, 0)
            else:
                got = view(rzs, n)
                total = buf[c, own].astype(WIDE)
                for s in range(3):
                    total = total + got[s].astype(WIDE)
                base = sum(PIECE_ROWS[:n]) if isinstance(n, int) else sum(PIECE_ROWS[:TILE]) + (n - TILE) * 128
                small_ref[pl.ds(base, rows), :] = total
        if stage < 4:
            start(scatter_copies(n, stage))

    SCATTER = 9 * GATHER_SEMS
    STATE = SCATTER + 9 * SCATTER_SEMS
    BACK, OUT, GIN = STATE + 2, STATE + 4, STATE + 7

    ins_w = ins[3:]
    if linked:
        small_ref = outs[2]
        wq, wk, wv, wo, ws, wu, wd, ga1, ga2 = ins_w
        for n, shard in ((QUERY, wq), (KEY, wk), (VALUE, wv), (OUT_W, wo)):
            for t in range(4):
                ags[n][c, place, pl.ds(t * 16, 16), :] = shard[:, t * 128 : t * 128 + 128]
        ags[SLOT][c, place, pl.ds(0, 64), :] = ws[...]
        rows16 = iota2((16, 16), 0)
        both = jnp.where(
            rows16 == 0,
            jnp.broadcast_to(ga1[...].astype(WIDE), (16, 16)),
            jnp.where(rows16 == 1, jnp.broadcast_to(ga2[...].astype(WIDE), (16, 16)), 0.0),
        )
        lane_at = ((dp * 4 + slot) % 8) * 16
        spread = jnp.where(iota2((16, 128), 1) == iota2((16, 128), 0) + lane_at, 1.0, 0.0)
        ags[SLOT][c, place, pl.ds(64, 16), :] = low(dot(low(both), low(spread)))
        for t in range(4):
            ags[TILE][t, c, place, pl.ds(0, 64), :] = wu[:, t * 128 : t * 128 + 128]
            ags[TILE][t, c, place, pl.ds(64, 64), :] = wd[:, t * 128 : t * 128 + 128]
        query_w, key_w, value_w, out_w = (
            functools.partial(square_of, ags[n]) for n in (QUERY, KEY, VALUE, OUT_W)
        )

        def up_w(t):
            return tile_of(ags[TILE], t, 0)

        def down_w(t):
            return tile_of(ags[TILE], t, 64)
    else:
        square_v, up_v, down_v = rest
        fw_q, fw_k, fw_v, fw_o, fw_s, fw_u, fw_d, fg1, fg2 = ins_w
        copies = [
            pltpu.make_async_copy(src, dst, lsem.at[4 + i])
            for i, (src, dst) in enumerate((
                (fw_q, square_v.at[0]), (fw_k, square_v.at[1]), (fw_v, square_v.at[2]), (fw_o, square_v.at[3]),
                (fw_s, w_slot), (fw_u, up_v), (fw_d, down_v),
            ))
        ]
        start(copies)
        for copy in copies:
            copy.wait()
        gains[0:1, :] = fg1[...].astype(WIDE)
        gains[1:2, :] = fg2[...].astype(WIDE)
        query_w, key_w, value_w, out_w = (lambda n=n: square_v[n] for n in range(4))

        def up_w(t):
            return up_v[t]

        def down_w(t):
            return down_v[t]

    lane = iota2((CHUNK, LANES), 1)
    sub = iota2((CHUNK, LANES), 0)
    bd_lo[...] = low(jnp.where(lane < 64, 1.0, 0.0))
    bd_hi[...] = low(jnp.where(lane < 64, 0.0, 1.0))
    bdm[...] = jnp.where((lane < 64) == (sub < 64), 1.0, 0.0)
    upper = low(jnp.where(sub <= lane, 1.0, 0.0))
    lower = low(jnp.where(sub >= lane, 1.0, 0.0))
    ones = jnp.ones((CHUNK, LANES), NARROW)
    for n in range(chunks):
        begin = starts_ref[:, pl.ds(pl.multiple_of(half * tokens + n * CHUNK, CHUNK), CHUNK)].astype(WIDE)
        begin = jnp.where(row == 0, begin[0:1], begin[1:2])
        begin = low(jnp.broadcast_to(begin, (CHUNK, LANES)))
        by_lane = dot(begin, upper)
        by_row = dot_nt(lower, begin)
        total = dot(begin, ones)
        same = by_row == by_lane
        v = low(jnp.where(same & (sub >= lane), 1.0, 0.0))
        vt = low(jnp.where(same & (sub <= lane), 1.0, 0.0))
        vis[n, :, 0:128] = v
        vis[n, :, 128:256] = v
        vist[n, :, 0:128] = vt
        vist[n, :, 128:256] = vt
        carried = jnp.where(by_row == 0.0, 1.0, 0.0)
        ending = jnp.where(by_row == total, 1.0, 0.0)
        hcar[n] = carried
        tail[n] = ending
        hcar_n[n] = low(carried)
        tail_n[n] = low(ending)
        passf[n] = jnp.where(total == 0.0, 1.0, 0.0)

    def perm_rows(i, _):
        r = iota2((CHUNK, WIDTH), 0) + i * CHUNK
        n = iota2((CHUNK, WIDTH), 1)
        source = ((n >> 4) & 3) * 128 + (n & 15) * 8 + (n >> 6)
        perm[pl.ds(pl.multiple_of(i * CHUNK, CHUNK), CHUNK), :] = low(jnp.where(r == source, 1.0, 0.0))
        return 0

    lax.fori_loop(0, WIDTH // CHUNK, perm_rows, 0)
    pl.semaphore_wait(barrier, len(peers))

    def gather_steps(*steps):
        if linked:
            for n, stage in steps:
                gather_step(n, stage)

    T0, T1, T2, T3 = range(TILE, TILE + 4)
    gather_steps(*((n, 0) for n in range(9)))
    x_copy.wait()

    def by_chunk(body):
        def step(i, _):
            body(pl.ds(pl.multiple_of(i * CHUNK, CHUNK), CHUNK), i)
            return 0

        lax.fori_loop(0, chunks, step, 0)

    def norm_one(rows, i):
        gtwo[rows, :], _ = norm_parts(x_v[rows, :])

    by_chunk(norm_one)

    if linked:
        gather_steps(
            (SLOT, 1), (KEY, 1), (SLOT, 2), (VALUE, 1), (KEY, 2), (QUERY, 1), (VALUE, 2), (OUT_W, 1), (SLOT, 3),
            (QUERY, 2), (KEY, 3), (T0, 1), (SLOT, 4),
        )
        for index, core, at, odp, oslot in owners(True):
            w_slot[odp * 64 : odp * 64 + 64, oslot * 128 : oslot * 128 + 128] = ags[SLOT][core, at, 0:64, :]
        for window in range(4):
            total = jnp.zeros((16, 128), WIDE)
            for index, core, at, _, _ in owners(True):
                if index // 8 == window:
                    total = total + ags[SLOT][core, at, 64:80, :].astype(WIDE)
            gains[0:8, window * 128 : window * 128 + 128] = total[0:8]
    w_slot[...] = low(dot(w_slot[...], perm[...]))

    gain_one = gains[0:1, :]
    gain_two = gains[1:2, :]

    n1[...] = low(gtwo[...] * gain_one)
    expo[...] = jnp.exp(dot(n1[...], w_slot[...]))
    proj[3] = low(expo[...])
    gather_steps((OUT_W, 2), (VALUE, 3), (KEY, 4))
    proj[1] = low(dot(n1[...], key_w()))
    gather_steps((T1, 1), (QUERY, 3), (VALUE, 4), (T0, 2))
    proj[2] = low(dot(n1[...], value_w()))
    def two(v):
        return jnp.concatenate([v * bd_lo[...], v * bd_hi[...]], axis=0)

    every = range(PAIRS)
    pair_cols = [slice(p * 128, p * 128 + 128) for p in every]

    def local_states(rows, i):
        w_tail = proj[3, rows, :]
        tloc[i] = jnp.broadcast_to(
            dot(jnp.ones((8, CHUNK), NARROW), w_tail * jnp.concatenate([tail_n[i]] * PAIRS, axis=1)),
            (8, WIDTH),
        )
        w = [proj[3, rows, cols] for cols in pair_cols]
        k_tail = [proj[1, rows, cols] * tail_n[i] for cols in pair_cols]
        v = [proj[2, rows, cols] for cols in pair_cols]
        kw = [dot_tn(k_tail[p], w[p]) for p in every]
        wv = [dot_tn(w[p] * tail_n[i], v[p]) for p in every]
        for p in every:
            loc[0, i, p] = kw[p] * bdm[...]
            loc[1, i, p] = wv[p] * bdm[...]

    by_chunk(local_states)

    def scan_states(order, initial, t_initial, keep):
        def one(kind, p):
            state = initial(kind, p)
            for i in order:
                if keep:
                    sin[kind, i, p] = low(state)
                state = loc[kind, i, p] + passf[i] * state
            if not keep:
                xsend[kind, p] = state

        def step(k, _):
            one(k // PAIRS, k % PAIRS)
            return 0

        lax.fori_loop(0, 2 * PAIRS, step, 0)
        state = t_initial()
        for i in order:
            if keep:
                tin[i] = state
            state = tloc[i] + jnp.concatenate([passf[i, 0:8, :]] * PAIRS, axis=1) * state
        if not keep:
            tsend[...] = state

    def exchange(at):
        return [remote(xsend, xrecv.at[(at - STATE) // 2], at, partner), remote(tsend, trecv.at[(at - STATE) // 2], at + 1, partner)]

    def send_states(order, at):
        scan_states(order, lambda k, p: jnp.zeros((128, 128), WIDE), lambda: jnp.zeros((8, WIDTH), WIDE), False)
        start(exchange(at))

    def carry_states(order, at, takes):
        n = (at - STATE) // 2
        recv(exchange(at))
        scan_states(order, lambda k, p: xrecv[n, k, p] * takes, lambda: trecv[n] * takes, True)

    forward = list(range(chunks))
    takes_forward = half.astype(WIDE)
    send_states(forward, STATE)
    gather_steps((OUT_W, 3), (T2, 1), (QUERY, 4))
    proj[0] = low(dot(n1[...], query_w()))
    n1t[...] = n1[...].T
    carry_states(forward, STATE, takes_forward)
    gather_steps((OUT_W, 4), (T1, 2))
    first_half = iota2((CHUNK, LANES), 1) < 64

    def over_heads(lo_part, hi_part):
        return jnp.where(first_half, lo_part, hi_part)

    def head_max(v):
        return over_heads(
            jnp.max(jnp.where(first_half, v, -jnp.inf), axis=-1, keepdims=True),
            jnp.max(jnp.where(first_half, -jnp.inf, v), axis=-1, keepdims=True),
        )

    def head_sum(v):
        return over_heads(
            jnp.sum(jnp.where(first_half, v, 0.0), axis=-1, keepdims=True),
            jnp.sum(jnp.where(first_half, 0.0, v), axis=-1, keepdims=True),
        )

    def attend(rows, i):
        mask = vis[i]
        carried = hcar[i]
        totals = dot(mask[:, 0:128], proj[3, rows, :]) + jnp.concatenate([carried] * PAIRS, axis=1) * tin[i, 0:1, :]
        rtot[rows, :] = 1.0 / totals
        q, k, v, w = ([proj[n, rows, cols] for cols in pair_cols] for n in range(4))
        w2 = [two(w[p]) for p in every]
        cross = [low(dot_nt(q[p], two(k[p]))) * mask for p in every]
        from_state = [dot(q[p], sin[0, i, p]) for p in every]
        numer = [dot(cross[p], w2[p]) for p in every]
        r = [rtot[rows, cols] for cols in pair_cols]
        s = [(numer[p] + carried * from_state[p]) * r[p] for p in every]
        e = [jnp.exp(s[p] - head_max(s[p])) for p in every]
        pr = [e[p] / head_sum(e[p]) for p in every]
        sc = [low(pr[p] * r[p]) for p in every]
        for p in every:
            score[rows, pair_cols[p]] = s[p]
            prob[rows, pair_cols[p]] = pr[p]
            scaled[rows, pair_cols[p]] = sc[p]
        mix = [low(dot_nt(sc[p], w2[p])) * mask for p in every]
        from_state = [dot(sc[p], sin[1, i, p]) for p in every]
        near = [dot(mix[p], two(v[p])) for p in every]
        for p in every:
            att[rows, pair_cols[p]] = low(near[p] + carried * from_state[p])
        if linked:
            for at, steps in ((0, ((T0, 3),)), (1, ((T3, 1),)), (3, ((T2, 2),))):
                pl.when(i == at)(functools.partial(gather_steps, *steps))

    by_chunk(attend)

    mid[...] = x_v[...] + dot(att[...], out_w())
    acc[...] = mid[...]
    cot_copy.wait()

    def norm_two(rows, i):
        xhat, _ = norm_parts(mid[rows, :])
        n2[rows, :] = low(xhat * gain_two)
        gf[rows, :] = low(cot_v[rows, :])
        gtwo[rows, :] = jnp.zeros((CHUNK, WIDTH), WIDE)

    by_chunk(norm_two)
    n2t[...] = n2[...].T
    gft[...] = gf[...].T

    def scatter_steps(*steps):
        if linked:
            for n, stage in steps:
                scatter_step(n, stage, PIECE_ROWS[n])

    def feed(t, _):
        if linked:
            for at, gathered, scattered in (
                (0, ((T1, 3), (T0, 4)), ()),
                (1, ((T3, 2), (T2, 3), (T1, 4)), ((T0, 1),)),
                (2, ((T3, 3), (T2, 4)), ((T1, 1),)),
                (3, ((T3, 4),), ((T0, 2), (T2, 1))),
            ):
                @pl.when(t == at)
                def _(gathered=gathered, scattered=scattered):
                    gather_steps(*gathered)
                    scatter_steps(*scattered)

        hidden = dot(n2[...], up_w(t))
        cdf = 0.5 * (1.0 + lax.erf(hidden * 0.7071067811865476))
        active = low(hidden * cdf)
        slope = cdf + hidden * (jnp.exp(-0.5 * hidden * hidden) * 0.3989422804014327)
        grad_hidden = low(dot(gf[...], down_w(t)) * slope)
        acc[...] += dot_nt(active, down_w(t))
        gtwo[...] += dot_nt(grad_hidden, up_w(t))
        g_up = low(dot(n2t[...], grad_hidden))
        g_down = low(dot(gft[...], active))
        if linked:
            for _, core, at, odp, oslot in owners(False):
                rows, cols = slice(odp * 64, odp * 64 + 64), slice(oslot * 128, oslot * 128 + 128)
                rss[TILE][t, core, at, 0:64, :] = g_up[rows, cols]
                rss[TILE][t, core, at, 64:128, :] = g_down[rows, cols]
            scatter_step(TILE + t, 0, 128)
        else:
            outs[7][t] = g_up
            outs[8][t] = g_down
        return 0

    lax.fori_loop(0, 4, feed, 0)

    mine, theirs = out_ref.at[row, own_rows], out_ref.at[1 - row, own_rows]
    oy, oc, of = remote(outb, mine, OUT, y_peer), remote(outb, mine, OUT + 1, partner), remote(theirs, theirs, OUT + 2, partner)
    ol = pltpu.make_async_copy(outb, mine, lsem.at[2])

    def norm_two_back(rows, i):
        outb[rows, :] = low(acc[rows, :])
        xhat, inv = norm_parts(mid[rows, :])
        up = gtwo[rows, :]
        grad = cot_v[rows, :] + norm_back(xhat, inv, gain_two, up)
        cot_v[rows, :] = grad
        gf[rows, :] = low(grad)
        gains[3:4, :] = gains[3:4, :] + jnp.sum(up * xhat, axis=0, keepdims=True)

    scatter_steps((T3, 1))
    gains[2:8, :] = jnp.zeros((6, WIDTH), WIDE)
    by_chunk(norm_two_back)
    oy.start()
    oc.start()
    ol.start()
    scatter_steps((T0, 3))
    ga[...] = low(dot_nt(gf[...], out_w()))
    g_out = low(dot_tn(att[...], gf[...]))

    def pack_square(n, grad):
        for index, core, at, _, _ in owners(False):
            for t in range(4):
                rss[n][core, at, t * 16 : t * 16 + 16, :] = grad[
                    index * 16 : index * 16 + 16, t * 128 : t * 128 + 128
                ]

    if linked:
        pack_square(OUT_W, g_out)
        scatter_steps((OUT_W, 0))
    else:
        outs[5][...] = g_out

    def back_first(rows, i):
        mask = vis[i]
        carried = hcar[i]
        carried_n = hcar_n[i]
        q, k, v, w = ([proj[n, rows, cols] for cols in pair_cols] for n in range(4))
        g = [ga[rows, cols] for cols in pair_cols]
        w2 = [two(w[p]) for p in every]
        gmix = [low(dot_nt(g[p], two(v[p]))) * mask for p in every]
        from_state = [dot_nt(g[p], sin[1, i, p]) for p in every]
        near = [dot(gmix[p], w2[p]) for p in every]
        r, pr, s = ([ref[rows, cols] for cols in pair_cols] for ref in (rtot, prob, score))
        gs = [low(near[p] + carried * from_state[p]).astype(WIDE) for p in every]
        gp = [gs[p] * r[p] for p in every]
        gscore = [pr[p] * (gp[p] - head_sum(pr[p] * gp[p])) for p in every]
        gn = [low(gscore[p] * r[p]) for p in every]
        gt = [low(-(gp[p] * pr[p] + gscore[p] * s[p]) * r[p]) for p in every]
        for p in every:
            gnum[rows, pair_cols[p]] = gn[p]
            gtot[rows, pair_cols[p]] = gt[p]
        gcross = [low(dot_nt(gn[p], w2[p])) * mask for p in every]
        from_state = [dot_nt(gn[p], sin[0, i, p]) for p in every]
        near = [dot(gcross[p], two(k[p])) for p in every]
        qn = [dot_tn(q[p] * carried_n, gn[p]) for p in every]
        gsc = [dot_tn(g[p] * carried_n, scaled[rows, pair_cols[p]]) for p in every]
        for p in every:
            gproj[0, rows, pair_cols[p]] = low(near[p] + carried * from_state[p])
            loc[0, i, p] = qn[p] * bdm[...]
            loc[1, i, p] = gsc[p] * bdm[...]
        tloc[i] = jnp.broadcast_to(
            dot(
                jnp.ones((8, CHUNK), NARROW),
                jnp.concatenate(gt, axis=1) * jnp.concatenate([carried_n] * PAIRS, axis=1),
            ),
            (8, WIDTH),
        )
        if linked:
            for at, steps in ((0, ((OUT_W, 1),)), (1, ((T1, 2),)), (3, ((T0, 4),))):
                pl.when(i == at)(functools.partial(scatter_steps, *steps))
    by_chunk(back_first)
    sent(exchange(STATE))
    send_states(forward[::-1], BACK)
    grad = low(dot(n1t[...], gproj[0]))
    if linked:
        pack_square(QUERY, grad)
        scatter_steps((QUERY, 0))
    else:
        outs[2][...] = grad
    carry_states(forward[::-1], BACK, 1.0 - takes_forward)
    def spread_gin(i):
        part = pl.ds(pl.multiple_of(half * tokens + i * CHUNK, CHUNK), CHUNK)
        mine, theirs, at = gin_ref.at[row, part], gin_ref.at[1 - row, part], GIN + 3 * i
        source = ginb.at[pl.ds(pl.multiple_of(i * CHUNK, CHUNK), CHUNK)]
        return remote(source, mine, at, y_peer), remote(source, mine, at + 1, partner), remote(theirs, theirs, at + 2, partner)

    def back_second(rows, i):
        mask = vist[i]
        ends = tail[i]
        wc = dot(mask[:, 0:128], gtot[rows, :]) + jnp.concatenate([ends] * PAIRS, axis=1) * tin[i, 0:1, :]
        q, k, v, w = ([proj[n, rows, cols] for cols in pair_cols] for n in range(4))
        g, sc, gn = ([ref[rows, cols] for cols in pair_cols] for ref in (ga, scaled, gnum))
        g2, sc2, gn2, q2 = ([two(m[p]) for p in every] for m in (g, sc, gn, q))
        s_query, s_grad = ([sin[n, i, p] for p in every] for n in range(2))
        mix = [low(dot_nt(w[p], sc2[p])) * mask for p in every]
        gmix = [low(dot_nt(v[p], g2[p])) * mask for p in every]
        cross = [low(dot_nt(k[p], q2[p])) * mask for p in every]
        gcross = [low(dot_nt(w[p], gn2[p])) * mask for p in every]
        from_state = [dot_nt(w[p], s_grad[p]) for p in every]
        near = [dot(mix[p], g2[p]) for p in every]
        for p in every:
            gproj[2, rows, pair_cols[p]] = low(near[p] + ends * from_state[p])
        from_state = [dot_nt(w[p], s_query[p]) for p in every]
        near = [dot(gcross[p], q2[p]) for p in every]
        for p in every:
            gproj[1, rows, pair_cols[p]] = low(near[p] + ends * from_state[p])
        from_state = [dot(v[p], s_grad[p]) + dot(k[p], s_query[p]) for p in every]
        near = [dot(gmix[p], sc2[p]) + dot(cross[p], gn2[p]) for p in every]
        for p in every:
            gw = low(near[p] + ends * from_state[p] + wc[:, pair_cols[p]]).astype(WIDE)
            gproj[3, rows, pair_cols[p]] = low(gw * expo[rows, pair_cols[p]])
        up = dot_nt(gproj[0, rows, :], query_w()) + dot_nt(gproj[1, rows, :], key_w())
        up = up + dot_nt(gproj[2, rows, :], value_w()) + dot_nt(gproj[3, rows, :], w_slot[...])
        xhat, inv = norm_parts(x_v[rows, :])
        ginb[rows, :] = low(cot_v[rows, :] + norm_back(xhat, inv, gain_one, up))
        gains[2:3, :] = gains[2:3, :] + jnp.sum(up * xhat, axis=0, keepdims=True)
        if linked:
            for at, steps in (
                (0, ((QUERY, 1), (T2, 2), (T1, 3))), (2, ((T3, 2),)), (3, ((OUT_W, 2), (T2, 3)))
            ):
                pl.when(i == at)(functools.partial(scatter_steps, *steps))
        iy, ic = spread_gin(i)[:2]
        iy.start()
        ic.start()

        @pl.when(i == 1)
        def _():
            oy.wait_recv()
            of.start()


    by_chunk(back_second)

    il = pltpu.make_async_copy(ginb, gin_ref.at[row, own_rows], lsem.at[3])
    il.start()
    for n, piece in ((2, VALUE), (1, KEY), (3, SLOT)):
        grad = low(dot(n1t[...], gproj[n]))
        if n == 3:
            grad = low(dot_nt(grad, perm[...]))
        if not linked:
            outs[2 + n if n < 3 else 6][...] = grad
        elif n < 3:
            pack_square(piece, grad)
        else:
            for index, core, at, odp, oslot in owners(False):
                rss[SLOT][core, at, 0:64, :] = grad[odp * 64 : odp * 64 + 64, oslot * 128 : oslot * 128 + 128]
                window = index // 8
                rss[SLOT][core, at, 64:80, :] = low(
                    jnp.concatenate(
                        [gains[2:4, window * 128 : window * 128 + 128], jnp.zeros((14, 128), WIDE)], axis=0
                    )
                )
        scatter_steps((piece, 0))
    def forward_gin(i):
        _, _, if_ = spread_gin(i)
        spread_gin(i)[0].wait_recv()
        if_.start()

    scatter_steps((T1, 4), (QUERY, 2), (VALUE, 1))
    forward_gin(0)
    scatter_steps((KEY, 1), (T2, 4))
    forward_gin(1)
    scatter_steps((SLOT, 1), (T3, 3), (OUT_W, 3))
    forward_gin(2)
    scatter_steps((VALUE, 2), (KEY, 2))
    forward_gin(3)
    scatter_steps((SLOT, 2), (T3, 4), (OUT_W, 4), (QUERY, 3), (VALUE, 3), (KEY, 3))
    scatter_steps((QUERY, 4), (SLOT, 3), (VALUE, 4), (KEY, 4))
    scatter_steps((SLOT, 4))
    if not linked:
        outs[9][...] = gains[2:4, :]

    oc.wait()
    oy.wait_send()
    ol.wait()
    of.wait()
    il.wait()
    for i in range(chunks):
        iy, ic, if_ = spread_gin(i)
        iy.wait_send()
        ic.wait()
        if_.wait()
    sent(exchange(BACK))
    if linked:
        for n in range(9):
            sent(gather_z(n) + gather_b(n) + gather_a(n) + gather_last(n))
            for stage in range(4):
                sent(scatter_copies(n, stage))


def finish_kernel(out_ref, gin_ref, small_ref, o, g, gq, gk, gv, go, gs, gu, gd, g1, g2):
    o[...] = out_ref[...].astype(WIDE)
    g[...] = gin_ref[...].astype(WIDE)

    @pl.when(pl.program_id(0) == 0)
    def _():
        base = 0
        bases = []
        for rows in PIECE_ROWS:
            bases.append(base)
            base += rows
        gs[...] = small_ref[0:64, :]
        mine = lax.axis_index("dp") * lax.axis_size("slot") + lax.axis_index("slot")
        window = small_ref[64:72, :]
        lanes = iota2((8, 128), 1)
        first = (mine % 8) * 16
        moved = jnp.concatenate(
            [
                jnp.sum(jnp.where(lanes == first + k, window, 0.0), axis=1, keepdims=True)
                for k in range(16)
            ],
            axis=1,
        )
        g1[...] = moved[0:1]
        g2[...] = moved[1:2]
        for t in range(4):
            cols = slice(t * 128, t * 128 + 128)
            for n, target in ((QUERY, gq), (KEY, gk), (VALUE, gv), (OUT_W, go)):
                target[:, cols] = small_ref[bases[n] + t * 16 : bases[n] + t * 16 + 16, :]
            gu[:, cols] = small_ref[bases[TILE + t] : bases[TILE + t] + 64, :]
            gd[:, cols] = small_ref[bases[TILE + t] + 64 : bases[TILE + t] + 128, :]


def finish(out, gin, small):
    rows, length, width = out.shape
    block = pl.BlockSpec((1, 512, width), lambda i: (i // (length // 512), i % (length // 512), 0))
    whole = lambda shape: pl.BlockSpec(shape, lambda i: (0,) * len(shape))
    shapes = [(16, width)] * 4 + [(64, 128), (64, width), (64, width), (1, 16), (1, 16)]
    shape = jax.ShapeDtypeStruct
    return pl.pallas_call(
        finish_kernel,
        grid=(rows * length // 512,),
        out_shape=[shape(out.shape, WIDE)] * 2 + [shape(s, WIDE) for s in shapes],
        in_specs=[block, block, whole(small.shape)],
        out_specs=[block, block] + [whole(s) for s in shapes],
        compiler_params=pltpu.CompilerParams(vmem_limit_bytes=60 * 1024 * 1024),
    )(out, gin, small)


def run_block(linked, inputs, starts, cotangent, weights):
    rows, length, width = inputs.shape
    tokens = length // 2
    chunks = tokens // CHUNK
    vm = pltpu.VMEM
    scratch = [
        vm((tokens, width), WIDE), vm((tokens, width), WIDE),
        vm((width, width), NARROW), vm((width, width), NARROW), vm((8, width), WIDE),
        vm((tokens, width), NARROW), vm((width, tokens), NARROW),
        vm((4, tokens, width), NARROW), vm((tokens, width), WIDE),
        vm((tokens, width), WIDE), vm((tokens, width), WIDE), vm((tokens, width), WIDE),
        vm((tokens, width), NARROW), vm((tokens, width), NARROW),
        vm((tokens, width), WIDE), vm((tokens, width), WIDE),
        vm((tokens, width), NARROW), vm((width, tokens), NARROW),
        vm((tokens, width), NARROW), vm((width, tokens), NARROW), vm((tokens, width), WIDE),
        vm((tokens, width), NARROW), vm((4, tokens, width), NARROW),
        vm((tokens, width), NARROW), vm((tokens, width), NARROW),
        vm((tokens, width), NARROW), vm((tokens, width), NARROW),
        vm((chunks, CHUNK, 256), NARROW), vm((chunks, CHUNK, 256), NARROW),
        vm((chunks, CHUNK, LANES), WIDE), vm((chunks, CHUNK, LANES), WIDE), vm((chunks, CHUNK, LANES), WIDE),
        vm((chunks, CHUNK, LANES), NARROW), vm((chunks, CHUNK, LANES), NARROW),
        vm((2, chunks, PAIRS, 128, 128), WIDE), vm((2, chunks, PAIRS, 128, 128), NARROW),
        vm((chunks, 8, width), WIDE), vm((chunks, 8, width), WIDE),
        vm((CHUNK, LANES), NARROW), vm((CHUNK, LANES), NARROW), vm((CHUNK, LANES), WIDE),
        vm((2, PAIRS, 128, 128), WIDE), vm((2, 2, PAIRS, 128, 128), WIDE),
        vm((8, width), WIDE), vm((2, 8, width), WIDE),
        pltpu.SemaphoreType.DMA((152,)), pltpu.SemaphoreType.DMA((152,)), pltpu.SemaphoreType.DMA((12,)),
    ]
    if linked:
        for lead in ((2, 16), (2, 16), (16,), (8,), (4,), (3,)):
            scratch += [vm((*lead, r, LANES), NARROW) for r in PIECE_ROWS[:TILE]]
            scratch += [vm((4, *lead, 128, LANES), NARROW)]
    else:
        scratch += [vm((4, width, width), NARROW)] * 3
    anywhere = pl.BlockSpec(memory_space=pl.ANY)
    here = pl.BlockSpec(memory_space=pltpu.VMEM)
    shape = jax.ShapeDtypeStruct
    big = [shape((rows, length, width), NARROW)] * 2
    square = (width, width)
    if linked:
        small = [shape((SMALL_ROWS, LANES), WIDE)]
        weight_specs = [here] * 9
    else:
        small = [shape(square, NARROW)] * 5 + [shape((4, *square), NARROW)] * 2 + [shape((2, width), WIDE)]
        weight_specs = [anywhere] * 7 + [here] * 2
    return pl.pallas_call(
        functools.partial(block_kernel, linked, 12, 2 + len(small)),
        out_shape=big + small,
        in_specs=[anywhere, here, anywhere] + weight_specs,
        out_specs=[anywhere] * 2 + [here] * len(small),
        scratch_shapes=scratch,
        compiler_params=pltpu.CompilerParams(
            collective_id=0, has_side_effects=True, vmem_limit_bytes=62 * 1024 * 1024
        ),
    )(inputs, starts, cotangent, *weights)


def on_device(
    inputs, starts, w_query, w_key, w_value, w_out, w_slot, w_up, w_down, gain_attn, gain_ffn, cotangent
):
    n_dp, n_slot = lax.axis_size("dp"), lax.axis_size("slot")
    if n_dp == 8 and n_slot == 4:
        weights = (
            w_query, w_key, w_value, w_out, w_slot, w_up, w_down.T,
            gain_attn.reshape(1, -1), gain_ffn.reshape(1, -1),
        )
        out, gin, small = run_block(True, inputs, starts, cotangent, weights)
        out, gin, gq, gk, gv, go, gs, gu, gd, g1, g2 = finish(out, gin, small)
        return out, gin, gq, gk, gv, go, gs, gu, gd.T, g1.reshape(-1), g2.reshape(-1)

    def whole(v, names, axis):
        return lax.all_gather(v, names, axis=axis, tiled=True)

    both = ("dp", "slot")
    width = inputs.shape[-1]
    up = whole(whole(w_up, "dp", 0), "slot", 1).reshape(width, 4, 4, 128).transpose(2, 0, 1, 3)
    down = whole(whole(w_down, "dp", 1), "slot", 0).reshape(4, 4, 128, width).transpose(1, 3, 0, 2)
    up, down = up.reshape(4, width, width), down.reshape(4, width, width)
    weights = (
        whole(w_query, both, 0), whole(w_key, both, 0), whole(w_value, both, 0), whole(w_out, both, 0),
        whole(whole(w_slot, "dp", 0), "slot", 1), up, down,
        whole(gain_attn, both, 0).reshape(1, -1), whole(gain_ffn, both, 0).reshape(1, -1),
    )
    out, gin, gq, gk, gv, go, gs, gu, gd, gg = run_block(False, inputs, starts, cotangent, weights)

    def shared(v, names, axis):
        return lax.psum_scatter(v.astype(WIDE), names, scatter_dimension=axis, tiled=True)

    gu = gu.reshape(4, width, 4, 128).transpose(1, 2, 0, 3).reshape(width, -1)
    gd = gd.reshape(4, width, 4, 128).transpose(2, 0, 3, 1).reshape(-1, width)
    return (
        out.astype(WIDE), gin.astype(WIDE),
        shared(gq, both, 0), shared(gk, both, 0), shared(gv, both, 0), shared(go, both, 0),
        shared(shared(gs, "slot", 1), "dp", 0), shared(shared(gu, "slot", 1), "dp", 0),
        shared(shared(gd, "slot", 0), "dp", 1), shared(gg[0], both, 0), shared(gg[1], both, 0),
    )


def solution(mesh):
    every = ("dp", "slot")
    rows = P("dp", None, None)
    return jax.shard_map(
        on_device,
        mesh=mesh,
        in_specs=(
            rows, P("dp", None), P(every, None), P(every, None), P(every, None), P(every, None),
            P("dp", "slot"), P("dp", "slot"), P("slot", "dp"), P(every), P(every), rows,
        ),
        out_specs=(
            rows, rows, P(every, None), P(every, None), P(every, None), P(every, None),
            P("dp", "slot"), P("dp", "slot"), P("slot", "dp"), P(every), P(every),
        ),
        check_vma=False,
    )
```

```python
import functools

import jax
import jax.numpy as jnp
from jax import lax
from jax.experimental import pallas as pl
from jax.experimental.pallas import tpu as pltpu
from jax.sharding import PartitionSpec as P

HEADS = 8
EPSILON = 1e-05
NARROW = jnp.bfloat16
WIDE = jnp.float32
MESH = pl.DeviceIdType.MESH

WIDTH = 512
CHUNK = 128
PAIRS = 4
LANES = 128
PIECE_ROWS = (80, 64, 64, 64, 64, 128, 128, 128, 128)
SLOT, KEY, VALUE, QUERY, OUT_W, TILE = range(6)
SMALL_ROWS = sum(PIECE_ROWS)
GATHER_MODES = (
    ("ABZ", "m"), ("ABZ", "m"), ("ABZ", "m"), ("ABZ", "m"), ("ABZ", "m"),
    ("ABZ", "m"), ("ABZ", "m"), ("ABZ", "m"), ("ABZ", "m"),
)
SCATTER_MODES = (
    ("ABZ", "x"), ("ABZ", "m"), ("ABZ", "x"), ("AZB", "x"), ("ABZ", "m"),
    ("ABZ", "m"), ("AZB", "m"), ("AZB", "x"), ("ABZ", "x"),
)
PLAN = {
    "slot": ("S1", "K1", "V1", "S2", "K2", "Q1", "V2", "O1", "S3", "K3", "T01", "Q2", "S4",),
    "key": ("V3", "K4", "O2",),
    "val": ("V4",),
    "loc": ("T11", "Q3", "T02",),
    "qry": ("Q4", "O3",),
    "scan": ("O4", "T21",),
    "att0": ("T12",),
    "att3": ("T31",),
    "outp": ("T03", "T22",),
    "ffn0a": ("T13", "T04",),
    "ffn0b": ("T32",),
    "ffn1a": ("T14",),
    "ffn1b": ("T23",),
    "ffn2a": ("T0.1", "T24",),
    "ffn2b": ("T33",),
    "ffn3a": ("T1.1", "T34",),
    "n2b": ("T0.2",),
    "ga": ("T2.1",),
    "gout": ("T1.2",),
    "B1_2": ("O.0",),
    "scan2": ("T0.3", "T3.1", "Q.0", "T2.2", "O.1",),
    "B2_1": ("y0",),
    "B2_2": ("V.0", "y1", "Q.1",),
    "B2_3": ("V.1", "O.2", "T3.2",),
    "wS": ("K.0", "Q.2",),
    "end": (
        "S.0", "K.1", "V.2", "O.3", "y2", "S.1", "K.2", "T3.3", "Q.3", "V.3", "S.2", "f0", "T2.3", "T0.4",
        "T1.3", "K.3", "y3", "f", "T3.4", "f2", "V.4", "S.3", "T1.4", "T2.4", "Q.4", "K.4", "O.4", "f1",
        "S.4", "f3",
    ),
}
SEMS = 4


def dot(a, b):
    return lax.dot_general(a, b, (((1,), (0,)), ((), ())), preferred_element_type=WIDE)


def dot_nt(a, b):
    return lax.dot_general(a, b, (((1,), (1,)), ((), ())), preferred_element_type=WIDE)


def dot_tn(a, b):
    return lax.dot_general(a, b, (((0,), (0,)), ((), ())), preferred_element_type=WIDE)


def low(v):
    return v.astype(NARROW)


def iota2(shape, dim):
    return lax.broadcasted_iota(jnp.int32, shape, dim)


def row_mean(v):
    return jnp.sum(v, axis=-1, keepdims=True) * (1.0 / v.shape[-1])


def norm_parts(v):
    center = v - row_mean(v)
    inv = lax.rsqrt(row_mean(center * center) + EPSILON)
    return center * inv, inv


def norm_back(xhat, inv, gain, up):
    u = up * gain
    return (u - row_mean(u) - xhat * row_mean(u * xhat)) * inv


def strides(mode):
    sizes = tuple(4 if axis == "Z" else 2 for axis in mode[0])
    return sizes, (sizes[1] * sizes[2], sizes[2], 1)


def owners(mode):
    out = []
    _, steps = strides(mode)
    for dp in range(8):
        for slot in range(4):
            z, x, y, c = dp // 2, dp % 2, slot // 2, slot % 2
            first_y = mode[1] == "y" or (mode[1] == "m" and c == 0)
            at = {"A": y if first_y else x, "B": x if first_y else y, "Z": z}
            place = sum(at[axis] * step for axis, step in zip(mode[0], steps))
            out.append((dp * 4 + slot, c, place, dp, slot))
    return out


def square_of(buf, n):
    return jnp.concatenate(
        [
            jnp.concatenate([buf[core, at, t * 16 : t * 16 + 16, :] for t in range(4)], axis=1)
            for _, core, at, _, _ in owners(GATHER_MODES[n])
        ],
        axis=0,
    )


def tile_of(buf, n, first):
    place = {(dp, slot): (core, at) for _, core, at, dp, slot in owners(GATHER_MODES[TILE])}
    return jnp.concatenate(
        [
            jnp.concatenate(
                [buf[(n, *place[dp, slot], slice(first, first + 64), slice(None))] for dp in range(8)], axis=0
            )
            for slot in range(4)
        ],
        axis=1,
    )


def block_kernel(linked, n_in, n_out, *refs):
    ins, outs, scr = refs[:n_in], refs[n_in : n_in + n_out], refs[n_in + n_out :]
    inputs_ref, starts_ref, cot_ref = ins[:3]
    out_ref, gin_ref = outs[:2]
    (x_v, cot_v, w_slot, perm, gains, n1, n1t, proj, expo, score, prob,
     rtot, scaled, att, mid, acc, n2, n2t, gf, gft, gtwo, ga, gproj, gnum, gtot, outb, ginb,
     vis, vist, hcar, tail, passf, hcar_n, tail_n, loc, sin, tloc, tin, bd_lo, bd_hi, bdm, xsend, xrecv, tsend, trecv,
     ssem, rsem, lsem) = scr[:48]
    rest = scr[48:]

    slot = lax.axis_index("slot")
    dp = lax.axis_index("dp")
    y, c = slot // 2, slot % 2
    row, half = y, c
    tokens = x_v.shape[0]
    chunks = tokens // CHUNK
    partner = (dp, y * 2 + (1 - c))
    y_peer = (dp, (1 - y) * 2 + c)
    if linked:
        ags, rss, rcs = (rest[6 * n : 6 * n + 6] for n in range(3))
        got_refs = [rest[18 + 9 * n : 27 + 9 * n] for n in range(3)]
        z, x = dp // 2, dp % 2
        x_peer = (z * 2 + 1 - x, slot)
        near = {
            "x": (x, y, x_peer, y_peer),
            "y": (y, x, y_peer, x_peer),
            "m": (
                y + c * (x - y),
                x + c * (y - x),
                (z * 2 + x + c * (1 - 2 * x), slot + (1 - c) * 2 * (1 - 2 * y)),
                (z * 2 + x + (1 - c) * (1 - 2 * x), slot + c * 2 * (1 - 2 * y)),
            ),
        }
        z_peers = [((((z + s) % 4) * 2 + x), slot) for s in (1, 2, 3)]
        peers = [partner, x_peer, y_peer] + z_peers
    else:
        peers = [partner, y_peer]

    barrier = pltpu.get_barrier_semaphore()
    for peer in peers:
        pl.semaphore_signal(barrier, inc=1, device_id=peer, device_id_type=MESH)

    own_rows = pl.ds(pl.multiple_of(half * tokens, tokens), tokens)
    x_copy = pltpu.make_async_copy(inputs_ref.at[row, own_rows], x_v, lsem.at[0])
    cot_copy = pltpu.make_async_copy(cot_ref.at[row, own_rows], cot_v, lsem.at[1])
    x_copy.start()
    cot_copy.start()

    def remote(src, dst, at, device, send_at=None):
        return pltpu.make_async_remote_copy(
            src_ref=src, dst_ref=dst, send_sem=ssem.at[at if send_at is None else send_at], recv_sem=rsem.at[at],
            device_id=device, device_id_type=MESH,
        )

    def start(copies):
        for copy in copies:
            copy.start()

    def recv(copies):
        for copy in copies:
            copy.wait_recv()

    def sent(copies):
        for copy in copies:
            copy.wait_send()

    def view(bufs, n):
        return bufs[n] if isinstance(n, int) and n < TILE else bufs[TILE].at[n - TILE]

    def mode_of(modes, n):
        return modes[n if isinstance(n, int) else TILE]

    def axes(mode):
        pa, pb, dev_a, dev_b = near[mode[1]]
        known = {
            "A": (pa, [(1 - pa, dev_a)]),
            "B": (pb, [(1 - pb, dev_b)]),
            "Z": (z, [((z + s + 1) % 4, z_peers[s]) for s in range(3)]),
        }
        return [(known[axis][0], step, known[axis][1]) for axis, step in zip(mode[0], strides(mode)[1])]

    def place_in(mode, upto=3):
        return sum(at * step for at, step, _ in axes(mode)[:upto])

    def gather_along(n, k):
        mode = mode_of(GATHER_MODES, n)
        _, step, others = axes(mode)[k]
        part = view(ags, n).at[c, pl.ds(place_in(mode, k + 1), step)]
        return [remote(part, part, n * SEMS + k, device) for _, device in others]

    def gather_along_all(n, k):
        _, step, others = axes(mode_of(GATHER_MODES, n))[k]
        part = view(ags, n).at[c, pl.ds(0, step * len(others))]
        return remote(part, part, n * SEMS + k, partner)

    def gather_across(n, k):
        mode = mode_of(GATHER_MODES, n)
        _, step, others = axes(mode)[k]
        base = place_in(mode, k)
        if k == 2:
            parts = [pl.ds(base, strides(mode)[0][2])]
        else:
            parts = [pl.ds(base + place * step, step) for place, _ in others]
        refs = [view(ags, n).at[c, part] for part in parts]
        return [remote(ref, ref, n * SEMS + 3, partner) for ref in refs]

    def gather_across_all(n):
        every_block = view(ags, n).at[c]
        return remote(every_block, every_block, n * SEMS + 3, partner)

    def gather_step(n, stage):
        if stage == 4:
            gather_across_all(n).wait_recv()
            return
        if stage:
            gather_along_all(n, 3 - stage).wait_recv()
        if stage < 3:
            start(gather_along(n, 2 - stage))
        if stage:
            start(gather_across(n, 3 - stage))

    def gather_sent(n):
        sent([gather_along_all(n, k) for k in range(3)] + [gather_across_all(n)])

    def scatter_copies(n, stage):
        buf, at, send = view(rss, n), SCATTER + n * SEMS + stage, n * SEMS + stage
        if stage == 0:
            return [remote(buf.at[1 - c], view(rcs, n), at, partner, send)]
        mode = SCATTER_MODES[n]
        _, step, others = axes(mode)[stage - 1]
        base, got = place_in(mode, stage - 1), got_refs[stage - 1][n]
        return [
            remote(buf.at[c, pl.ds(base + place * step, step)], got.at[pl.ds(i * step, step)], at, device, send)
            for i, (place, device) in enumerate(others)
        ]

    def scatter_all(n, stage):
        if stage == 0:
            return scatter_copies(n, stage)[0]
        got = got_refs[stage - 1][n]
        part = view(rss, n).at[c, pl.ds(0, got.shape[0])]
        return remote(part, got, SCATTER + n * SEMS + stage, partner, n * SEMS + stage)

    def scatter_step(n, stage, rows):
        if stage:
            scatter_all(n, stage - 1).wait_recv()
            buf, mode = view(rss, n), SCATTER_MODES[n]
            got = view(rcs, n) if stage == 1 else got_refs[stage - 2][n]
            count = 16 if stage == 1 else axes(mode)[stage - 2][1]
            first, terms = place_in(mode, stage - 1), got.shape[0] // count

            def summed(i):
                total = buf[c, first + i].astype(WIDE)
                for k in range(terms):
                    total = total + got[k * count + i].astype(WIDE)
                return total

            if stage < 4:
                def step(i, _):
                    buf[c, first + i] = low(summed(i))
                    return 0

                lax.fori_loop(0, count, step, 0)
            else:
                small_ref[pl.ds(sum(PIECE_ROWS[:n]), rows), :] = summed(0)
        else:
            gather_sent(n)
        if stage < 4:
            start(scatter_copies(n, stage))

    SCATTER = 9 * SEMS
    STATE = SCATTER + 9 * SEMS
    BACK, OUT, GIN = STATE + 2, STATE + 4, STATE + 7

    ins_w = ins[3:]
    if linked:
        small_ref = outs[2]
        wq, wk, wv, wo, ws, wu, wd, ga1, ga2 = ins_w
        place = [place_in(mode) for mode in GATHER_MODES]
        for n, shard in ((QUERY, wq), (KEY, wk), (VALUE, wv), (OUT_W, wo)):
            for t in range(4):
                ags[n][c, place[n], pl.ds(t * 16, 16), :] = shard[:, t * 128 : t * 128 + 128]
        ags[SLOT][c, place[SLOT], pl.ds(0, 64), :] = ws[...]
        rows16 = iota2((16, 16), 0)
        both = jnp.where(
            rows16 == 0,
            jnp.broadcast_to(ga1[...].astype(WIDE), (16, 16)),
            jnp.where(rows16 == 1, jnp.broadcast_to(ga2[...].astype(WIDE), (16, 16)), 0.0),
        )
        lane_at = ((dp * 4 + slot) % 8) * 16
        spread = jnp.where(iota2((16, 128), 1) == iota2((16, 128), 0) + lane_at, 1.0, 0.0)
        ags[SLOT][c, place[SLOT], pl.ds(64, 16), :] = low(dot(low(both), low(spread)))
        for t in range(4):
            ags[TILE][t, c, place[TILE], pl.ds(0, 64), :] = wu[:, t * 128 : t * 128 + 128]
            ags[TILE][t, c, place[TILE], pl.ds(64, 64), :] = wd[:, t * 128 : t * 128 + 128]
        query_w, key_w, value_w, out_w = (
            functools.partial(square_of, ags[n], n) for n in (QUERY, KEY, VALUE, OUT_W)
        )

        def up_w(t):
            return tile_of(ags[TILE], t, 0)

        def down_w(t):
            return tile_of(ags[TILE], t, 64)
    else:
        square_v, up_v, down_v = rest
        fw_q, fw_k, fw_v, fw_o, fw_s, fw_u, fw_d, fg1, fg2 = ins_w
        copies = [
            pltpu.make_async_copy(src, dst, lsem.at[4 + i])
            for i, (src, dst) in enumerate((
                (fw_q, square_v.at[0]), (fw_k, square_v.at[1]), (fw_v, square_v.at[2]), (fw_o, square_v.at[3]),
                (fw_s, w_slot), (fw_u, up_v), (fw_d, down_v),
            ))
        ]
        start(copies)
        for copy in copies:
            copy.wait()
        gains[0:1, :] = fg1[...].astype(WIDE)
        gains[1:2, :] = fg2[...].astype(WIDE)
        query_w, key_w, value_w, out_w = (lambda n=n: square_v[n] for n in range(4))

        def up_w(t):
            return up_v[t]

        def down_w(t):
            return down_v[t]

    pl.semaphore_wait(barrier, len(peers))

    mine, theirs = out_ref.at[row, own_rows], out_ref.at[1 - row, own_rows]
    oy, oc, of = remote(outb, mine, OUT, y_peer), remote(outb, mine, OUT + 1, partner), remote(theirs, theirs, OUT + 2, partner)
    ol = pltpu.make_async_copy(outb, mine, lsem.at[2])

    def spread_gin(i):
        part = pl.ds(pl.multiple_of(half * tokens + i * CHUNK, CHUNK), CHUNK)
        mine, theirs = gin_ref.at[row, part], gin_ref.at[1 - row, part]
        source = ginb.at[pl.ds(pl.multiple_of(i * CHUNK, CHUNK), CHUNK)]
        return (
            remote(source, mine, GIN + i, y_peer),
            remote(source, mine, GIN + chunks, partner),
            remote(theirs, theirs, GIN + chunks + 1, partner),
        )

    def spread_gin_all(k):
        mine = gin_ref.at[row, own_rows]
        return remote(mine, mine, GIN + chunks + k, partner)

    def spread_steps(word):
        if word == "f":
            oy.wait_recv()
            of.start()
            return
        sends = spread_gin(int(word[1]))
        if word[0] == "y":
            sends[0].start()
            sends[1].start()
        else:
            sends[0].wait_recv()
            sends[2].start()

    names = {"S": SLOT, "K": KEY, "V": VALUE, "Q": QUERY, "O": OUT_W}
    names.update({"T%d" % t: TILE + t for t in range(4)})

    def planned(block):
        for word in PLAN.get(block, ()):
            if word[0] in "yf":
                spread_steps(word)
            elif linked:
                if "." in word:
                    piece, stage = word.split(".")
                    scatter_step(names[piece], int(stage), PIECE_ROWS[names[piece]])
                else:
                    gather_step(names[word[:-1]], int(word[-1]))

    def planned_at(block, i):
        for k in range(4):
            if PLAN.get(block % k):
                pl.when(i == k)(functools.partial(planned, block % k))

    if linked:
        for n in range(9):
            gather_step(n, 0)
    lane = iota2((CHUNK, LANES), 1)
    sub = iota2((CHUNK, LANES), 0)
    bd_lo[...] = low(jnp.where(lane < 64, 1.0, 0.0))
    bd_hi[...] = low(jnp.where(lane < 64, 0.0, 1.0))
    bdm[...] = jnp.where((lane < 64) == (sub < 64), 1.0, 0.0)
    upper = low(jnp.where(sub <= lane, 1.0, 0.0))
    lower = low(jnp.where(sub >= lane, 1.0, 0.0))
    ones = jnp.ones((CHUNK, LANES), NARROW)
    for n in range(chunks):
        begin = starts_ref[:, pl.ds(pl.multiple_of(half * tokens + n * CHUNK, CHUNK), CHUNK)].astype(WIDE)
        begin = jnp.where(row == 0, begin[0:1], begin[1:2])
        begin = low(jnp.broadcast_to(begin, (CHUNK, LANES)))
        by_lane = dot(begin, upper)
        by_row = dot_nt(lower, begin)
        total = dot(begin, ones)
        same = by_row == by_lane
        v = low(jnp.where(same & (sub >= lane), 1.0, 0.0))
        vt = low(jnp.where(same & (sub <= lane), 1.0, 0.0))
        vis[n, :, 0:128] = v
        vis[n, :, 128:256] = v
        vist[n, :, 0:128] = vt
        vist[n, :, 128:256] = vt
        carried = jnp.where(by_row == 0.0, 1.0, 0.0)
        ending = jnp.where(by_row == total, 1.0, 0.0)
        hcar[n] = carried
        tail[n] = ending
        hcar_n[n] = low(carried)
        tail_n[n] = low(ending)
        passf[n] = jnp.where(total == 0.0, 1.0, 0.0)

    def perm_rows(i, _):
        r = iota2((CHUNK, WIDTH), 0) + i * CHUNK
        n = iota2((CHUNK, WIDTH), 1)
        source = ((n >> 4) & 3) * 128 + (n & 15) * 8 + (n >> 6)
        perm[pl.ds(pl.multiple_of(i * CHUNK, CHUNK), CHUNK), :] = low(jnp.where(r == source, 1.0, 0.0))
        return 0

    lax.fori_loop(0, WIDTH // CHUNK, perm_rows, 0)
    x_copy.wait()

    def by_chunk(body):
        def step(i, _):
            body(pl.ds(pl.multiple_of(i * CHUNK, CHUNK), CHUNK), i)
            return 0

        lax.fori_loop(0, chunks, step, 0)

    def norm_one(rows, i):
        gtwo[rows, :], _ = norm_parts(x_v[rows, :])

    by_chunk(norm_one)

    if linked:
        planned("slot")
        for index, core, at, odp, oslot in owners(GATHER_MODES[SLOT]):
            w_slot[odp * 64 : odp * 64 + 64, oslot * 128 : oslot * 128 + 128] = ags[SLOT][core, at, 0:64, :]
        for window in range(4):
            total = jnp.zeros((16, 128), WIDE)
            for index, core, at, _, _ in owners(GATHER_MODES[SLOT]):
                if index // 8 == window:
                    total = total + ags[SLOT][core, at, 64:80, :].astype(WIDE)
            gains[0:8, window * 128 : window * 128 + 128] = total[0:8]
    w_slot[...] = low(dot(w_slot[...], perm[...]))

    gain_one = gains[0:1, :]
    gain_two = gains[1:2, :]

    n1[...] = low(gtwo[...] * gain_one)
    expo[...] = jnp.exp(dot(n1[...], w_slot[...]))
    proj[3] = low(expo[...])
    planned("key")
    proj[1] = low(dot(n1[...], key_w()))
    planned("val")
    proj[2] = low(dot(n1[...], value_w()))
    def two(v):
        return jnp.concatenate([v * bd_lo[...], v * bd_hi[...]], axis=0)

    every = range(PAIRS)
    pair_cols = [slice(p * 128, p * 128 + 128) for p in every]

    def local_states(rows, i):
        w_tail = proj[3, rows, :]
        tloc[i] = jnp.broadcast_to(
            dot(jnp.ones((8, CHUNK), NARROW), w_tail * jnp.concatenate([tail_n[i]] * PAIRS, axis=1)),
            (8, WIDTH),
        )
        w = [proj[3, rows, cols] for cols in pair_cols]
        k_tail = [proj[1, rows, cols] * tail_n[i] for cols in pair_cols]
        v = [proj[2, rows, cols] for cols in pair_cols]
        kw = [dot_tn(k_tail[p], w[p]) for p in every]
        wv = [dot_tn(w[p] * tail_n[i], v[p]) for p in every]
        for p in every:
            loc[0, i, p] = kw[p] * bdm[...]
            loc[1, i, p] = wv[p] * bdm[...]

    planned("loc")
    by_chunk(local_states)

    def scan_states(order, initial, t_initial, keep):
        def one(kind, p):
            state = initial(kind, p)
            for i in order:
                if keep:
                    sin[kind, i, p] = low(state)
                state = loc[kind, i, p] + passf[i] * state
            if not keep:
                xsend[kind, p] = state

        def step(k, _):
            one(k // PAIRS, k % PAIRS)
            return 0

        lax.fori_loop(0, 2 * PAIRS, step, 0)
        state = t_initial()
        for i in order:
            if keep:
                tin[i] = state
            state = tloc[i] + jnp.concatenate([passf[i, 0:8, :]] * PAIRS, axis=1) * state
        if not keep:
            tsend[...] = state

    def exchange(at):
        return [remote(xsend, xrecv.at[(at - STATE) // 2], at, partner), remote(tsend, trecv.at[(at - STATE) // 2], at + 1, partner)]

    def send_states(order, at):
        scan_states(order, lambda k, p: jnp.zeros((128, 128), WIDE), lambda: jnp.zeros((8, WIDTH), WIDE), False)
        start(exchange(at))

    def carry_states(order, at, takes):
        n = (at - STATE) // 2
        recv(exchange(at))
        scan_states(order, lambda k, p: xrecv[n, k, p] * takes, lambda: trecv[n] * takes, True)

    forward = list(range(chunks))
    takes_forward = half.astype(WIDE)
    send_states(forward, STATE)
    planned("qry")
    proj[0] = low(dot(n1[...], query_w()))
    n1t[...] = n1[...].T
    planned("scan")
    carry_states(forward, STATE, takes_forward)
    first_half = iota2((CHUNK, LANES), 1) < 64

    def over_heads(lo_part, hi_part):
        return jnp.where(first_half, lo_part, hi_part)

    def head_max(v):
        return over_heads(
            jnp.max(jnp.where(first_half, v, -jnp.inf), axis=-1, keepdims=True),
            jnp.max(jnp.where(first_half, -jnp.inf, v), axis=-1, keepdims=True),
        )

    def head_sum(v):
        return over_heads(
            jnp.sum(jnp.where(first_half, v, 0.0), axis=-1, keepdims=True),
            jnp.sum(jnp.where(first_half, 0.0, v), axis=-1, keepdims=True),
        )

    def attend(rows, i):
        planned_at("att%d", i)
        mask = vis[i]
        carried = hcar[i]
        totals = dot(mask[:, 0:128], proj[3, rows, :]) + jnp.concatenate([carried] * PAIRS, axis=1) * tin[i, 0:1, :]
        rtot[rows, :] = 1.0 / totals
        q, k, v, w = ([proj[n, rows, cols] for cols in pair_cols] for n in range(4))
        w2 = [two(w[p]) for p in every]
        cross = [low(dot_nt(q[p], two(k[p]))) * mask for p in every]
        from_state = [dot(q[p], sin[0, i, p]) for p in every]
        numer = [dot(cross[p], w2[p]) for p in every]
        r = [rtot[rows, cols] for cols in pair_cols]
        s = [(numer[p] + carried * from_state[p]) * r[p] for p in every]
        e = [jnp.exp(s[p] - head_max(s[p])) for p in every]
        pr = [e[p] / head_sum(e[p]) for p in every]
        sc = [low(pr[p] * r[p]) for p in every]
        for p in every:
            score[rows, pair_cols[p]] = s[p]
            prob[rows, pair_cols[p]] = pr[p]
            scaled[rows, pair_cols[p]] = sc[p]
        mix = [low(dot_nt(sc[p], w2[p])) * mask for p in every]
        from_state = [dot(sc[p], sin[1, i, p]) for p in every]
        near = [dot(mix[p], two(v[p])) for p in every]
        for p in every:
            att[rows, pair_cols[p]] = low(near[p] + carried * from_state[p])

    by_chunk(attend)

    planned("outp")
    mid[...] = x_v[...] + dot(att[...], out_w())
    acc[...] = mid[...]
    cot_copy.wait()

    def norm_two(rows, i):
        xhat, _ = norm_parts(mid[rows, :])
        n2[rows, :] = low(xhat * gain_two)
        gf[rows, :] = low(cot_v[rows, :])
        gtwo[rows, :] = jnp.zeros((CHUNK, WIDTH), WIDE)

    by_chunk(norm_two)
    n2t[...] = n2[...].T
    gft[...] = gf[...].T

    def tile_place(t, places):
        at = places[0]
        for k in range(1, 4):
            if places[k] != places[0]:
                at = jnp.where(t == k, places[k], at)
        return at

    def feed(t, _):
        planned_at("ffn%da", t)
        hidden = dot(n2[...], up_w(t))
        cdf = 0.5 * (1.0 + lax.erf(hidden * 0.7071067811865476))
        active = low(hidden * cdf)
        slope = cdf + hidden * (jnp.exp(-0.5 * hidden * hidden) * 0.3989422804014327)
        grad_hidden = low(dot(gf[...], down_w(t)) * slope)
        planned_at("ffn%db", t)
        acc[...] += dot_nt(active, down_w(t))
        gtwo[...] += dot_nt(grad_hidden, up_w(t))
        g_up = low(dot(n2t[...], grad_hidden))
        g_down = low(dot(gft[...], active))
        if linked:
            for (_, core, at, odp, oslot), *later in zip(*(owners(mode) for mode in SCATTER_MODES[TILE:])):
                at = tile_place(t, [at] + [other[2] for other in later])
                rows, cols = slice(odp * 64, odp * 64 + 64), slice(oslot * 128, oslot * 128 + 128)
                rss[TILE][t, core, at, 0:64, :] = g_up[rows, cols]
                rss[TILE][t, core, at, 64:128, :] = g_down[rows, cols]
            scatter_step(TILE + t, 0, 128)
        else:
            outs[7][t] = g_up
            outs[8][t] = g_down
        return 0

    lax.fori_loop(0, 4, feed, 0)

    def norm_two_back(rows, i):
        outb[rows, :] = low(acc[rows, :])
        xhat, inv = norm_parts(mid[rows, :])
        up = gtwo[rows, :]
        grad = cot_v[rows, :] + norm_back(xhat, inv, gain_two, up)
        cot_v[rows, :] = grad
        gf[rows, :] = low(grad)
        gains[3:4, :] = gains[3:4, :] + jnp.sum(up * xhat, axis=0, keepdims=True)

    planned("n2b")
    gains[2:8, :] = jnp.zeros((6, WIDTH), WIDE)
    by_chunk(norm_two_back)
    oy.start()
    oc.start()
    ol.start()
    planned("ga")
    ga[...] = low(dot_nt(gf[...], out_w()))
    planned("gout")
    g_out = low(dot_tn(att[...], gf[...]))

    def pack_square(n, grad):
        for index, core, at, _, _ in owners(SCATTER_MODES[n]):
            for t in range(4):
                rss[n][core, at, t * 16 : t * 16 + 16, :] = grad[
                    index * 16 : index * 16 + 16, t * 128 : t * 128 + 128
                ]

    if linked:
        pack_square(OUT_W, g_out)
    else:
        outs[5][...] = g_out

    def back_first(rows, i):
        planned_at("B1_%d", i)
        mask = vis[i]
        carried = hcar[i]
        carried_n = hcar_n[i]
        q, k, v, w = ([proj[n, rows, cols] for cols in pair_cols] for n in range(4))
        g = [ga[rows, cols] for cols in pair_cols]
        w2 = [two(w[p]) for p in every]
        gmix = [low(dot_nt(g[p], two(v[p]))) * mask for p in every]
        from_state = [dot_nt(g[p], sin[1, i, p]) for p in every]
        near = [dot(gmix[p], w2[p]) for p in every]
        r, pr, s = ([ref[rows, cols] for cols in pair_cols] for ref in (rtot, prob, score))
        gs = [low(near[p] + carried * from_state[p]).astype(WIDE) for p in every]
        gp = [gs[p] * r[p] for p in every]
        gscore = [pr[p] * (gp[p] - head_sum(pr[p] * gp[p])) for p in every]
        gn = [low(gscore[p] * r[p]) for p in every]
        gt = [low(-(gp[p] * pr[p] + gscore[p] * s[p]) * r[p]) for p in every]
        for p in every:
            gnum[rows, pair_cols[p]] = gn[p]
            gtot[rows, pair_cols[p]] = gt[p]
        gcross = [low(dot_nt(gn[p], w2[p])) * mask for p in every]
        from_state = [dot_nt(gn[p], sin[0, i, p]) for p in every]
        near = [dot(gcross[p], two(k[p])) for p in every]
        qn = [dot_tn(q[p] * carried_n, gn[p]) for p in every]
        gsc = [dot_tn(g[p] * carried_n, scaled[rows, pair_cols[p]]) for p in every]
        for p in every:
            gproj[0, rows, pair_cols[p]] = low(near[p] + carried * from_state[p])
            loc[0, i, p] = qn[p] * bdm[...]
            loc[1, i, p] = gsc[p] * bdm[...]
        tloc[i] = jnp.broadcast_to(
            dot(
                jnp.ones((8, CHUNK), NARROW),
                jnp.concatenate(gt, axis=1) * jnp.concatenate([carried_n] * PAIRS, axis=1),
            ),
            (8, WIDTH),
        )

    by_chunk(back_first)
    planned("send2")
    sent(exchange(STATE))
    send_states(forward[::-1], BACK)
    planned("qg")
    grad = low(dot(n1t[...], gproj[0]))
    if linked:
        pack_square(QUERY, grad)
    else:
        outs[2][...] = grad
    planned("scan2")
    carry_states(forward[::-1], BACK, 1.0 - takes_forward)
    def back_value(rows, i):
        planned_at("bv%d", i)
        mask = vist[i]
        ends = tail[i]
        w, g, sc = ([m[rows, cols] for cols in pair_cols] for m in (proj.at[3], ga, scaled))
        g2, sc2 = ([two(m[p]) for p in every] for m in (g, sc))
        mix = [low(dot_nt(w[p], sc2[p])) * mask for p in every]
        from_state = [dot_nt(w[p], sin[1, i, p]) for p in every]
        near = [dot(mix[p], g2[p]) for p in every]
        for p in every:
            gproj[2, rows, pair_cols[p]] = low(near[p] + ends * from_state[p])

    by_chunk(back_value)
    planned("wV")
    grad = low(dot(n1t[...], gproj[2]))
    if linked:
        pack_square(VALUE, grad)
    else:
        outs[4][...] = grad

    def back_second(rows, i):
        planned_at("B2_%d", i)
        mask = vist[i]
        ends = tail[i]
        wc = dot(mask[:, 0:128], gtot[rows, :]) + jnp.concatenate([ends] * PAIRS, axis=1) * tin[i, 0:1, :]
        q, k, v, w = ([proj[n, rows, cols] for cols in pair_cols] for n in range(4))
        g, sc, gn = ([ref[rows, cols] for cols in pair_cols] for ref in (ga, scaled, gnum))
        g2, sc2, gn2, q2 = ([two(m[p]) for p in every] for m in (g, sc, gn, q))
        s_query, s_grad = ([sin[n, i, p] for p in every] for n in range(2))
        gmix = [low(dot_nt(v[p], g2[p])) * mask for p in every]
        cross = [low(dot_nt(k[p], q2[p])) * mask for p in every]
        gcross = [low(dot_nt(w[p], gn2[p])) * mask for p in every]
        from_state = [dot_nt(w[p], s_query[p]) for p in every]
        near = [dot(gcross[p], q2[p]) for p in every]
        for p in every:
            gproj[1, rows, pair_cols[p]] = low(near[p] + ends * from_state[p])
        from_state = [dot(v[p], s_grad[p]) + dot(k[p], s_query[p]) for p in every]
        near = [dot(gmix[p], sc2[p]) + dot(cross[p], gn2[p]) for p in every]
        for p in every:
            gw = low(near[p] + ends * from_state[p] + wc[:, pair_cols[p]]).astype(WIDE)
            gproj[3, rows, pair_cols[p]] = low(gw * expo[rows, pair_cols[p]])
        up = dot_nt(gproj[0, rows, :], query_w()) + dot_nt(gproj[1, rows, :], key_w())
        up = up + dot_nt(gproj[2, rows, :], value_w()) + dot_nt(gproj[3, rows, :], w_slot[...])
        xhat, inv = norm_parts(x_v[rows, :])
        ginb[rows, :] = low(cot_v[rows, :] + norm_back(xhat, inv, gain_one, up))
        gains[2:3, :] = gains[2:3, :] + jnp.sum(up * xhat, axis=0, keepdims=True)

    by_chunk(back_second)

    il = pltpu.make_async_copy(ginb, gin_ref.at[row, own_rows], lsem.at[3])
    il.start()
    planned("wK")
    for n, piece in ((1, KEY), (3, SLOT)):
        grad = low(dot(n1t[...], gproj[n]))
        if n == 3:
            grad = low(dot_nt(grad, perm[...]))
        if not linked:
            outs[2 + n if n < 3 else 6][...] = grad
        elif n < 3:
            pack_square(piece, grad)
        else:
            for index, core, at, odp, oslot in owners(SCATTER_MODES[SLOT]):
                rss[SLOT][core, at, 0:64, :] = grad[odp * 64 : odp * 64 + 64, oslot * 128 : oslot * 128 + 128]
                window = index // 8
                rss[SLOT][core, at, 64:80, :] = low(
                    jnp.concatenate(
                        [gains[2:4, window * 128 : window * 128 + 128], jnp.zeros((14, 128), WIDE)], axis=0
                    )
                )
        planned("wS" if n == 1 else "end")
    if not linked:
        outs[9][...] = gains[2:4, :]

    oc.wait()
    oy.wait_send()
    ol.wait()
    of.wait()
    il.wait()
    for i in range(chunks):
        spread_gin(i)[0].wait_send()
    spread_gin_all(0).wait()
    spread_gin_all(1).wait()
    sent(exchange(BACK))
    if linked:
        for n in range(9):
            sent([scatter_all(n, stage) for stage in range(4)])


def finish_kernel(out_ref, gin_ref, small_ref, o, g, gq, gk, gv, go, gs, gu, gd, g1, g2):
    o[...] = out_ref[...].astype(WIDE)
    g[...] = gin_ref[...].astype(WIDE)

    @pl.when(pl.program_id(0) == 0)
    def _():
        base = 0
        bases = []
        for rows in PIECE_ROWS:
            bases.append(base)
            base += rows
        gs[...] = small_ref[0:64, :]
        mine = lax.axis_index("dp") * lax.axis_size("slot") + lax.axis_index("slot")
        window = small_ref[64:72, :]
        lanes = iota2((8, 128), 1)
        first = (mine % 8) * 16
        moved = jnp.concatenate(
            [
                jnp.sum(jnp.where(lanes == first + k, window, 0.0), axis=1, keepdims=True)
                for k in range(16)
            ],
            axis=1,
        )
        g1[...] = moved[0:1]
        g2[...] = moved[1:2]
        for t in range(4):
            cols = slice(t * 128, t * 128 + 128)
            for n, target in ((QUERY, gq), (KEY, gk), (VALUE, gv), (OUT_W, go)):
                target[:, cols] = small_ref[bases[n] + t * 16 : bases[n] + t * 16 + 16, :]
            gu[:, cols] = small_ref[bases[TILE + t] : bases[TILE + t] + 64, :]
            gd[:, cols] = small_ref[bases[TILE + t] + 64 : bases[TILE + t] + 128, :]


def finish(out, gin, small):
    rows, length, width = out.shape
    block = pl.BlockSpec((1, 512, width), lambda i: (i // (length // 512), i % (length // 512), 0))
    whole = lambda shape: pl.BlockSpec(shape, lambda i: (0,) * len(shape))
    shapes = [(16, width)] * 4 + [(64, 128), (64, width), (64, width), (1, 16), (1, 16)]
    shape = jax.ShapeDtypeStruct
    return pl.pallas_call(
        finish_kernel,
        grid=(rows * length // 512,),
        out_shape=[shape(out.shape, WIDE)] * 2 + [shape(s, WIDE) for s in shapes],
        in_specs=[block, block, whole(small.shape)],
        out_specs=[block, block] + [whole(s) for s in shapes],
        compiler_params=pltpu.CompilerParams(vmem_limit_bytes=60 * 1024 * 1024),
    )(out, gin, small)


def run_block(linked, inputs, starts, cotangent, weights):
    rows, length, width = inputs.shape
    tokens = length // 2
    chunks = tokens // CHUNK
    vm = pltpu.VMEM
    scratch = [
        vm((tokens, width), WIDE), vm((tokens, width), WIDE),
        vm((width, width), NARROW), vm((width, width), NARROW), vm((8, width), WIDE),
        vm((tokens, width), NARROW), vm((width, tokens), NARROW),
        vm((4, tokens, width), NARROW), vm((tokens, width), WIDE),
        vm((tokens, width), WIDE), vm((tokens, width), WIDE), vm((tokens, width), WIDE),
        vm((tokens, width), NARROW), vm((tokens, width), NARROW),
        vm((tokens, width), WIDE), vm((tokens, width), WIDE),
        vm((tokens, width), NARROW), vm((width, tokens), NARROW),
        vm((tokens, width), NARROW), vm((width, tokens), NARROW), vm((tokens, width), WIDE),
        vm((tokens, width), NARROW), vm((4, tokens, width), NARROW),
        vm((tokens, width), NARROW), vm((tokens, width), NARROW),
        vm((tokens, width), NARROW), vm((tokens, width), NARROW),
        vm((chunks, CHUNK, 256), NARROW), vm((chunks, CHUNK, 256), NARROW),
        vm((chunks, CHUNK, LANES), WIDE), vm((chunks, CHUNK, LANES), WIDE), vm((chunks, CHUNK, LANES), WIDE),
        vm((chunks, CHUNK, LANES), NARROW), vm((chunks, CHUNK, LANES), NARROW),
        vm((2, chunks, PAIRS, 128, 128), WIDE), vm((2, chunks, PAIRS, 128, 128), NARROW),
        vm((chunks, 8, width), WIDE), vm((chunks, 8, width), WIDE),
        vm((CHUNK, LANES), NARROW), vm((CHUNK, LANES), NARROW), vm((CHUNK, LANES), WIDE),
        vm((2, PAIRS, 128, 128), WIDE), vm((2, 2, PAIRS, 128, 128), WIDE),
        vm((8, width), WIDE), vm((2, 8, width), WIDE),
        pltpu.SemaphoreType.DMA((88,)), pltpu.SemaphoreType.DMA((88,)), pltpu.SemaphoreType.DMA((12,)),
    ]
    if linked:
        for lead in ((2, 16), (2, 16), (16,)):
            scratch += [vm((*lead, r, LANES), NARROW) for r in PIECE_ROWS[:TILE]]
            scratch += [vm((4, *lead, 128, LANES), NARROW)]
        for k in range(3):
            for r, mode in zip(PIECE_ROWS, SCATTER_MODES):
                sizes, steps = strides(mode)
                scratch += [vm(((sizes[k] - 1) * steps[k], r, LANES), NARROW)]
    else:
        scratch += [vm((4, width, width), NARROW)] * 3
    anywhere = pl.BlockSpec(memory_space=pl.ANY)
    here = pl.BlockSpec(memory_space=pltpu.VMEM)
    shape = jax.ShapeDtypeStruct
    big = [shape((rows, length, width), NARROW)] * 2
    square = (width, width)
    if linked:
        small = [shape((SMALL_ROWS, LANES), WIDE)]
        weight_specs = [here] * 9
    else:
        small = [shape(square, NARROW)] * 5 + [shape((4, *square), NARROW)] * 2 + [shape((2, width), WIDE)]
        weight_specs = [anywhere] * 7 + [here] * 2
    return pl.pallas_call(
        functools.partial(block_kernel, linked, 12, 2 + len(small)),
        out_shape=big + small,
        in_specs=[anywhere, here, anywhere] + weight_specs,
        out_specs=[anywhere] * 2 + [here] * len(small),
        scratch_shapes=scratch,
        compiler_params=pltpu.CompilerParams(
            collective_id=0, has_side_effects=True, vmem_limit_bytes=62 * 1024 * 1024
        ),
    )(inputs, starts, cotangent, *weights)


def on_device(
    inputs, starts, w_query, w_key, w_value, w_out, w_slot, w_up, w_down, gain_attn, gain_ffn, cotangent
):
    n_dp, n_slot = lax.axis_size("dp"), lax.axis_size("slot")
    if n_dp == 8 and n_slot == 4:
        weights = (
            w_query, w_key, w_value, w_out, w_slot, w_up, w_down.T,
            gain_attn.reshape(1, -1), gain_ffn.reshape(1, -1),
        )
        out, gin, small = run_block(True, inputs, starts, cotangent, weights)
        out, gin, gq, gk, gv, go, gs, gu, gd, g1, g2 = finish(out, gin, small)
        return out, gin, gq, gk, gv, go, gs, gu, gd.T, g1.reshape(-1), g2.reshape(-1)

    def whole(v, names, axis):
        return lax.all_gather(v, names, axis=axis, tiled=True)

    both = ("dp", "slot")
    width = inputs.shape[-1]
    up = whole(whole(w_up, "dp", 0), "slot", 1).reshape(width, 4, 4, 128).transpose(2, 0, 1, 3)
    down = whole(whole(w_down, "dp", 1), "slot", 0).reshape(4, 4, 128, width).transpose(1, 3, 0, 2)
    up, down = up.reshape(4, width, width), down.reshape(4, width, width)
    weights = (
        whole(w_query, both, 0), whole(w_key, both, 0), whole(w_value, both, 0), whole(w_out, both, 0),
        whole(whole(w_slot, "dp", 0), "slot", 1), up, down,
        whole(gain_attn, both, 0).reshape(1, -1), whole(gain_ffn, both, 0).reshape(1, -1),
    )
    out, gin, gq, gk, gv, go, gs, gu, gd, gg = run_block(False, inputs, starts, cotangent, weights)

    def shared(v, names, axis):
        return lax.psum_scatter(v.astype(WIDE), names, scatter_dimension=axis, tiled=True)

    gu = gu.reshape(4, width, 4, 128).transpose(1, 2, 0, 3).reshape(width, -1)
    gd = gd.reshape(4, width, 4, 128).transpose(2, 0, 3, 1).reshape(-1, width)
    return (
        out.astype(WIDE), gin.astype(WIDE),
        shared(gq, both, 0), shared(gk, both, 0), shared(gv, both, 0), shared(go, both, 0),
        shared(shared(gs, "slot", 1), "dp", 0), shared(shared(gu, "slot", 1), "dp", 0),
        shared(shared(gd, "slot", 0), "dp", 1), shared(gg[0], both, 0), shared(gg[1], both, 0),
    )


def solution(mesh):
    every = ("dp", "slot")
    rows = P("dp", None, None)
    return jax.shard_map(
        on_device,
        mesh=mesh,
        in_specs=(
            rows, P("dp", None), P(every, None), P(every, None), P(every, None), P(every, None),
            P("dp", "slot"), P("dp", "slot"), P("slot", "dp"), P(every), P(every), rows,
        ),
        out_specs=(
            rows, rows, P(every, None), P(every, None), P(every, None), P(every, None),
            P("dp", "slot"), P("dp", "slot"), P("slot", "dp"), P(every), P(every),
        ),
        check_vma=False,
    )
```

```python
import functools

import jax
import jax.numpy as jnp
from jax import lax
from jax.experimental import pallas as pl
from jax.experimental.pallas import tpu as pltpu
from jax.sharding import PartitionSpec as P

HEADS = 8
EPSILON = 1e-05
NARROW = jnp.bfloat16
WIDE = jnp.float32
MESH = pl.DeviceIdType.MESH

WIDTH = 512
CHUNK = 128
PAIRS = 4
LANES = 128
PIECE_ROWS = (80, 64, 64, 64, 64, 128, 128, 128, 128)
SLOT, KEY, VALUE, QUERY, OUT_W, TILE = range(6)
SMALL_ROWS = sum(PIECE_ROWS)
GATHER_MODES = (
    ("PZ", "y"), ("PZ", "x"), ("PZ", "y"), ("PZ", "y"), ("ZAB", "y"),
    ("ABZ", "m"), ("ABZ", "m"), ("ABZ", "m"), ("ABZ", "m"),
)
SCATTER_MODES = (
    ("PZ", "x"), ("AZB", "x"), ("PZ", "x"), ("AZB", "x"), ("AZB", "x"),
    ("PZ", "y"), ("ZAB", "x"), ("AZB", "x"), ("ABZ", "x"),
)
PLAN = {
    "slot": ("O1", "S1", "K1", "V1", "Q1", "S2", "K2", "T11", "S3", "V2",),
    "key": ("T01", "V3", "K3", "O2",),
    "val": ("T21",),
    "loc": ("Q2", "T12",),
    "qry": ("Q3", "T02",),
    "scan": ("T31",),
    "att1": ("T13",),
    "att2": ("T22",),
    "att3": ("T14", "O3",),
    "outp": ("T03", "O4", "T32",),
    "ffn0a": ("T04",),
    "ffn1a": ("T23",),
    "ffn2a": ("T24",),
    "ffn2b": ("T33", "T0.1",),
    "ffn3a": ("T1.1", "T34",),
    "ga": ("o2", "o1", "T2.1",),
    "qg": ("o3", "o0", "T3.1", "O.0",),
    "scan2": ("T0.2", "Q.0",),
    "B2_0": ("T2.2",),
    "B2_1": ("y0", "Q.1",),
    "B2_2": ("y1",),
    "B2_3": ("O.1", "V.0", "T3.2",),
    "G3": ("T1.2",),
    "wK": ("Q.2",),
    "wS": ("K.0", "y3",),
    "end": (
        "p0", "O.2", "K.1", "S.0", "T3.3", "p1", "V.1", "K.2", "S.1", "O.3", "V.2", "y2", "f3", "p2",
        "f1", "S.2", "Q.3", "T2.3", "T3.4", "T0.3", "T1.3", "K.3", "O.4", "f2", "p3", "f0", "Q.4", "T2.4",
        "T1.4", "V.3", "K.4", "S.3",
    ),
}
SEMS = 4


def dot(a, b):
    return lax.dot_general(a, b, (((1,), (0,)), ((), ())), preferred_element_type=WIDE)


def dot_nt(a, b):
    return lax.dot_general(a, b, (((1,), (1,)), ((), ())), preferred_element_type=WIDE)


def dot_tn(a, b):
    return lax.dot_general(a, b, (((0,), (0,)), ((), ())), preferred_element_type=WIDE)


def low(v):
    return v.astype(NARROW)


def iota2(shape, dim):
    return lax.broadcasted_iota(jnp.int32, shape, dim)


def row_mean(v):
    return jnp.sum(v, axis=-1, keepdims=True) * (1.0 / v.shape[-1])


def norm_parts(v):
    center = v - row_mean(v)
    inv = lax.rsqrt(row_mean(center * center) + EPSILON)
    return center * inv, inv


def norm_back(xhat, inv, gain, up):
    u = up * gain
    return (u - row_mean(u) - xhat * row_mean(u * xhat)) * inv


def strides(mode):
    sizes = [2 if axis in "AB" else 4 for axis in mode[0]]
    steps = [1]
    for size in sizes[:0:-1]:
        steps.insert(0, steps[0] * size)
    return sizes, steps


def owners(mode):
    out = []
    _, steps = strides(mode)
    for dp in range(8):
        for slot in range(4):
            z, x, y, c = dp // 2, dp % 2, slot // 2, slot % 2
            first_y = mode[1] == "y" or (mode[1] == "m" and c == 0)
            at = {"A": y if first_y else x, "B": x if first_y else y, "Z": z, "P": x * 2 + y}
            place = sum(at[axis] * step for axis, step in zip(mode[0], steps))
            out.append((dp * 4 + slot, c, place, dp, slot))
    return out


def square_of(buf, n):
    return jnp.concatenate(
        [
            jnp.concatenate([buf[core, at, t * 16 : t * 16 + 16, :] for t in range(4)], axis=1)
            for _, core, at, _, _ in owners(GATHER_MODES[n])
        ],
        axis=0,
    )


def tile_of(buf, n, first):
    place = {(dp, slot): (core, at) for _, core, at, dp, slot in owners(GATHER_MODES[TILE])}
    return jnp.concatenate(
        [
            jnp.concatenate(
                [buf[(n, *place[dp, slot], slice(first, first + 64), slice(None))] for dp in range(8)], axis=0
            )
            for slot in range(4)
        ],
        axis=1,
    )


def block_kernel(linked, n_in, n_out, *refs):
    ins, outs, scr = refs[:n_in], refs[n_in : n_in + n_out], refs[n_in + n_out :]
    inputs_ref, starts_ref, cot_ref = ins[:3]
    out_ref, gin_ref = outs[:2]
    (x_v, cot_v, w_slot, perm, gains, n1, n1t, proj, expo, score, prob,
     rtot, scaled, att, mid, acc, n2, n2t, gf, gft, gtwo, ga, gproj, gnum, gtot, outb, ginb,
     vis, vist, hcar, tail, passf, hcar_n, tail_n, loc, sin, tloc, tin, bd_lo, bd_hi, bdm, xsend, xrecv, tsend, trecv,
     ssem, rsem, lsem) = scr[:48]
    rest = scr[48:]

    slot = lax.axis_index("slot")
    dp = lax.axis_index("dp")
    y, c = slot // 2, slot % 2
    row, half = y, c
    tokens = x_v.shape[0]
    chunks = tokens // CHUNK
    partner = (dp, y * 2 + (1 - c))
    y_peer = (dp, (1 - y) * 2 + c)
    if linked:
        ags, rss, rcs = (rest[6 * n : 6 * n + 6] for n in range(3))
        got_refs = [rest[18 + 9 * n : 27 + 9 * n] for n in range(3)]
        z, x = dp // 2, dp % 2
        x_peer = (z * 2 + 1 - x, slot)
        near = {
            "x": (x, y, x_peer, y_peer),
            "y": (y, x, y_peer, x_peer),
            "m": (
                y + c * (x - y),
                x + c * (y - x),
                (z * 2 + x + c * (1 - 2 * x), slot + (1 - c) * 2 * (1 - 2 * y)),
                (z * 2 + x + (1 - c) * (1 - 2 * x), slot + c * 2 * (1 - 2 * y)),
            ),
        }
        z_peers = [((((z + s) % 4) * 2 + x), slot) for s in (1, 2, 3)]
        diagonal = (z * 2 + 1 - x, (1 - y) * 2 + c)
        peers = [partner, x_peer, y_peer, diagonal] + z_peers
    else:
        peers = [partner, y_peer]

    barrier = pltpu.get_barrier_semaphore()
    for peer in peers:
        pl.semaphore_signal(barrier, inc=1, device_id=peer, device_id_type=MESH)

    own_rows = pl.ds(pl.multiple_of(half * tokens, tokens), tokens)
    x_copy = pltpu.make_async_copy(inputs_ref.at[row, own_rows], x_v, lsem.at[0])
    cot_copy = pltpu.make_async_copy(cot_ref.at[row, own_rows], cot_v, lsem.at[1])
    x_copy.start()
    cot_copy.start()

    def remote(src, dst, at, device, send_at=None):
        return pltpu.make_async_remote_copy(
            src_ref=src, dst_ref=dst, send_sem=ssem.at[at if send_at is None else send_at], recv_sem=rsem.at[at],
            device_id=device, device_id_type=MESH,
        )

    def start(copies):
        for copy in copies:
            copy.start()

    def recv(copies):
        for copy in copies:
            copy.wait_recv()

    def sent(copies):
        for copy in copies:
            copy.wait_send()

    def view(bufs, n):
        return bufs[n] if isinstance(n, int) and n < TILE else bufs[TILE].at[n - TILE]

    def mode_of(modes, n):
        return modes[n if isinstance(n, int) else TILE]

    def axes(mode):
        pa, pb, dev_a, dev_b = near[mode[1]]
        known = {
            "A": (pa, [(1 - pa, dev_a)]),
            "B": (pb, [(1 - pb, dev_b)]),
            "Z": (z, [((z + s + 1) % 4, z_peers[s]) for s in range(3)]),
            "P": (x * 2 + y, [((1 - x) * 2 + y, x_peer), (x * 2 + 1 - y, y_peer), ((1 - x) * 2 + 1 - y, diagonal)]),
        }
        return [(known[axis][0], step, known[axis][1]) for axis, step in zip(mode[0], strides(mode)[1])]

    def place_in(mode, upto=None):
        return sum(at * step for at, step, _ in axes(mode)[:upto])

    def gather_along(n, k):
        mode = mode_of(GATHER_MODES, n)
        _, step, others = axes(mode)[k]
        part = view(ags, n).at[c, pl.ds(place_in(mode, k + 1), step)]
        return [remote(part, part, n * SEMS + k, device) for _, device in others]

    def gather_along_all(n, k):
        _, step, others = axes(mode_of(GATHER_MODES, n))[k]
        part = view(ags, n).at[c, pl.ds(0, step * len(others))]
        return remote(part, part, n * SEMS + k, partner)

    def gather_across(n, k):
        mode = mode_of(GATHER_MODES, n)
        _, step, others = axes(mode)[k]
        base = place_in(mode, k)
        if k == len(mode[0]) - 1:
            parts = [pl.ds(base, strides(mode)[0][k])]
        else:
            parts = [pl.ds(base + place * step, step) for place, _ in others]
        refs = [view(ags, n).at[c, part] for part in parts]
        return [remote(ref, ref, n * SEMS + 3, partner) for ref in refs]

    def gather_across_all(n):
        every_block = view(ags, n).at[c]
        return remote(every_block, every_block, n * SEMS + 3, partner)

    def gather_step(n, stage):
        count = len(mode_of(GATHER_MODES, n)[0])
        if stage > count:
            gather_across_all(n).wait_recv()
            return
        if stage:
            gather_along_all(n, count - stage).wait_recv()
        if stage < count:
            start(gather_along(n, count - 1 - stage))
        if stage:
            start(gather_across(n, count - stage))

    def gather_sent(n):
        sent([gather_along_all(n, k) for k in range(len(mode_of(GATHER_MODES, n)[0]))] + [gather_across_all(n)])

    def scatter_copies(n, stage):
        buf, at, send = view(rss, n), SCATTER + n * SEMS + stage, n * SEMS + stage
        if stage == 0:
            return [remote(buf.at[1 - c], view(rcs, n), at, partner, send)]
        mode = SCATTER_MODES[n]
        _, step, others = axes(mode)[stage - 1]
        base, got = place_in(mode, stage - 1), got_refs[stage - 1][n]
        return [
            remote(buf.at[c, pl.ds(base + place * step, step)], got.at[pl.ds(i * step, step)], at, device, send)
            for i, (place, device) in enumerate(others)
        ]

    def scatter_all(n, stage):
        if stage == 0:
            return scatter_copies(n, stage)[0]
        got = got_refs[stage - 1][n]
        part = view(rss, n).at[c, pl.ds(0, got.shape[0])]
        return remote(part, got, SCATTER + n * SEMS + stage, partner, n * SEMS + stage)

    def scatter_step(n, stage, rows):
        if stage:
            scatter_all(n, stage - 1).wait_recv()
            buf, mode = view(rss, n), SCATTER_MODES[n]
            got = view(rcs, n) if stage == 1 else got_refs[stage - 2][n]
            count = 16 if stage == 1 else axes(mode)[stage - 2][1]
            first, terms = place_in(mode, stage - 1), got.shape[0] // count

            def summed(i):
                total = buf[c, first + i].astype(WIDE)
                for k in range(terms):
                    total = total + got[k * count + i].astype(WIDE)
                return total

            if stage <= len(mode[0]):
                def step(i, _):
                    buf[c, first + i] = low(summed(i))
                    return 0

                lax.fori_loop(0, count, step, 0)
            else:
                small_ref[pl.ds(sum(PIECE_ROWS[:n]), rows), :] = summed(0)
        else:
            gather_sent(n)
        if stage <= (len(SCATTER_MODES[n][0]) if stage else 1):
            start(scatter_copies(n, stage))

    SCATTER = 9 * SEMS
    STATE = SCATTER + 9 * SEMS
    BACK, OUT, GIN = STATE + 2, STATE + 4, STATE + 10

    ins_w = ins[3:]
    if linked:
        small_ref = outs[2]
        wq, wk, wv, wo, ws, wu, wd, ga1, ga2 = ins_w
        place = [place_in(mode) for mode in GATHER_MODES]
        for n, shard in ((QUERY, wq), (KEY, wk), (VALUE, wv), (OUT_W, wo)):
            for t in range(4):
                ags[n][c, place[n], pl.ds(t * 16, 16), :] = shard[:, t * 128 : t * 128 + 128]
        ags[SLOT][c, place[SLOT], pl.ds(0, 64), :] = ws[...]
        rows16 = iota2((16, 16), 0)
        both = jnp.where(
            rows16 == 0,
            jnp.broadcast_to(ga1[...].astype(WIDE), (16, 16)),
            jnp.where(rows16 == 1, jnp.broadcast_to(ga2[...].astype(WIDE), (16, 16)), 0.0),
        )
        lane_at = ((dp * 4 + slot) % 8) * 16
        spread = jnp.where(iota2((16, 128), 1) == iota2((16, 128), 0) + lane_at, 1.0, 0.0)
        ags[SLOT][c, place[SLOT], pl.ds(64, 16), :] = low(dot(low(both), low(spread)))
        for t in range(4):
            ags[TILE][t, c, place[TILE], pl.ds(0, 64), :] = wu[:, t * 128 : t * 128 + 128]
            ags[TILE][t, c, place[TILE], pl.ds(64, 64), :] = wd[:, t * 128 : t * 128 + 128]
        query_w, key_w, value_w, out_w = (
            functools.partial(square_of, ags[n], n) for n in (QUERY, KEY, VALUE, OUT_W)
        )

        def up_w(t):
            return tile_of(ags[TILE], t, 0)

        def down_w(t):
            return tile_of(ags[TILE], t, 64)
    else:
        square_v, up_v, down_v = rest
        fw_q, fw_k, fw_v, fw_o, fw_s, fw_u, fw_d, fg1, fg2 = ins_w
        copies = [
            pltpu.make_async_copy(src, dst, lsem.at[4 + i])
            for i, (src, dst) in enumerate((
                (fw_q, square_v.at[0]), (fw_k, square_v.at[1]), (fw_v, square_v.at[2]), (fw_o, square_v.at[3]),
                (fw_s, w_slot), (fw_u, up_v), (fw_d, down_v),
            ))
        ]
        start(copies)
        for copy in copies:
            copy.wait()
        gains[0:1, :] = fg1[...].astype(WIDE)
        gains[1:2, :] = fg2[...].astype(WIDE)
        query_w, key_w, value_w, out_w = (lambda n=n: square_v[n] for n in range(4))

        def up_w(t):
            return up_v[t]

        def down_w(t):
            return down_v[t]

    pl.semaphore_wait(barrier, len(peers))

    ol = pltpu.make_async_copy(outb, out_ref.at[row, own_rows], lsem.at[2])
    results = {OUT: (outb, out_ref), GIN: (ginb, gin_ref)}

    def spread(base, i):
        source, target = results[base]
        part = pl.ds(pl.multiple_of(half * tokens + i * CHUNK, CHUNK), CHUNK)
        mine, theirs = target.at[row, part], target.at[1 - row, part]
        chunk = source.at[pl.ds(i * CHUNK, CHUNK)]
        return (
            remote(chunk, mine, base + i, y_peer),
            remote(chunk, mine, base + chunks, partner),
            remote(theirs, theirs, base + chunks + 1, partner),
        )

    def spread_all(base, k):
        mine = results[base][1].at[row, own_rows]
        return remote(mine, mine, base + chunks + k, partner)

    def spread_steps(word):
        copies = spread(OUT if word[0] in "op" else GIN, int(word[1]))
        if word[0] in "oy":
            copies[0].start()
            copies[1].start()
        else:
            copies[0].wait_recv()
            copies[2].start()

    names = {"S": SLOT, "K": KEY, "V": VALUE, "Q": QUERY, "O": OUT_W}
    names.update({"T%d" % t: TILE + t for t in range(4)})

    def planned(block):
        for word in PLAN.get(block, ()):
            if word[0] in "opyf":
                spread_steps(word)
            elif linked:
                if "." in word:
                    piece, stage = word.split(".")
                    scatter_step(names[piece], int(stage), PIECE_ROWS[names[piece]])
                else:
                    gather_step(names[word[:-1]], int(word[-1]))

    def planned_at(block, i):
        for k in range(4):
            if PLAN.get(block % k):
                pl.when(i == k)(functools.partial(planned, block % k))

    if linked:
        for n in range(9):
            gather_step(n, 0)
    lane = iota2((CHUNK, LANES), 1)
    sub = iota2((CHUNK, LANES), 0)
    bd_lo[...] = low(jnp.where(lane < 64, 1.0, 0.0))
    bd_hi[...] = low(jnp.where(lane < 64, 0.0, 1.0))
    bdm[...] = jnp.where((lane < 64) == (sub < 64), 1.0, 0.0)
    upper = low(jnp.where(sub <= lane, 1.0, 0.0))
    lower = low(jnp.where(sub >= lane, 1.0, 0.0))
    ones = jnp.ones((CHUNK, LANES), NARROW)
    for n in range(chunks):
        begin = starts_ref[:, pl.ds(pl.multiple_of(half * tokens + n * CHUNK, CHUNK), CHUNK)].astype(WIDE)
        begin = jnp.where(row == 0, begin[0:1], begin[1:2])
        begin = low(jnp.broadcast_to(begin, (CHUNK, LANES)))
        by_lane = dot(begin, upper)
        by_row = dot_nt(lower, begin)
        total = dot(begin, ones)
        same = by_row == by_lane
        v = low(jnp.where(same & (sub >= lane), 1.0, 0.0))
        vt = low(jnp.where(same & (sub <= lane), 1.0, 0.0))
        vis[n, :, 0:128] = v
        vis[n, :, 128:256] = v
        vist[n, :, 0:128] = vt
        vist[n, :, 128:256] = vt
        carried = jnp.where(by_row == 0.0, 1.0, 0.0)
        ending = jnp.where(by_row == total, 1.0, 0.0)
        hcar[n] = carried
        tail[n] = ending
        hcar_n[n] = low(carried)
        tail_n[n] = low(ending)
        passf[n] = jnp.where(total == 0.0, 1.0, 0.0)

    def perm_rows(i, _):
        r = iota2((CHUNK, WIDTH), 0) + i * CHUNK
        n = iota2((CHUNK, WIDTH), 1)
        source = ((n >> 4) & 3) * 128 + (n & 15) * 8 + (n >> 6)
        perm[pl.ds(pl.multiple_of(i * CHUNK, CHUNK), CHUNK), :] = low(jnp.where(r == source, 1.0, 0.0))
        return 0

    lax.fori_loop(0, WIDTH // CHUNK, perm_rows, 0)
    x_copy.wait()

    def by_chunk(body):
        def step(i, _):
            body(pl.ds(pl.multiple_of(i * CHUNK, CHUNK), CHUNK), i)
            return 0

        lax.fori_loop(0, chunks, step, 0)

    def norm_one(rows, i):
        gtwo[rows, :], _ = norm_parts(x_v[rows, :])

    by_chunk(norm_one)

    if linked:
        planned("slot")
        for index, core, at, odp, oslot in owners(GATHER_MODES[SLOT]):
            w_slot[odp * 64 : odp * 64 + 64, oslot * 128 : oslot * 128 + 128] = ags[SLOT][core, at, 0:64, :]
        for window in range(4):
            total = jnp.zeros((16, 128), WIDE)
            for index, core, at, _, _ in owners(GATHER_MODES[SLOT]):
                if index // 8 == window:
                    total = total + ags[SLOT][core, at, 64:80, :].astype(WIDE)
            gains[0:8, window * 128 : window * 128 + 128] = total[0:8]
    w_slot[...] = low(dot(w_slot[...], perm[...]))

    gain_one = gains[0:1, :]
    gain_two = gains[1:2, :]

    n1[...] = low(gtwo[...] * gain_one)
    expo[...] = jnp.exp(dot(n1[...], w_slot[...]))
    proj[3] = low(expo[...])
    planned("key")
    proj[1] = low(dot(n1[...], key_w()))
    planned("val")
    proj[2] = low(dot(n1[...], value_w()))
    def two(v):
        return jnp.concatenate([v * bd_lo[...], v * bd_hi[...]], axis=0)

    every = range(PAIRS)
    pair_cols = [slice(p * 128, p * 128 + 128) for p in every]

    def local_states(rows, i):
        w_tail = proj[3, rows, :]
        tloc[i] = jnp.broadcast_to(
            dot(jnp.ones((8, CHUNK), NARROW), w_tail * jnp.concatenate([tail_n[i]] * PAIRS, axis=1)),
            (8, WIDTH),
        )
        w = [proj[3, rows, cols] for cols in pair_cols]
        k_tail = [proj[1, rows, cols] * tail_n[i] for cols in pair_cols]
        v = [proj[2, rows, cols] for cols in pair_cols]
        kw = [dot_tn(k_tail[p], w[p]) for p in every]
        wv = [dot_tn(w[p] * tail_n[i], v[p]) for p in every]
        for p in every:
            loc[0, i, p] = kw[p] * bdm[...]
            loc[1, i, p] = wv[p] * bdm[...]

    planned("loc")
    by_chunk(local_states)

    def scan_states(order, initial, t_initial, keep):
        def one(kind, p):
            state = initial(kind, p)
            for i in order:
                if keep:
                    sin[kind, i, p] = low(state)
                state = loc[kind, i, p] + passf[i] * state
            if not keep:
                xsend[kind, p] = state

        def step(k, _):
            one(k // PAIRS, k % PAIRS)
            return 0

        lax.fori_loop(0, 2 * PAIRS, step, 0)
        state = t_initial()
        for i in order:
            if keep:
                tin[i] = state
            state = tloc[i] + jnp.concatenate([passf[i, 0:8, :]] * PAIRS, axis=1) * state
        if not keep:
            tsend[...] = state

    def exchange(at):
        return [remote(xsend, xrecv.at[(at - STATE) // 2], at, partner), remote(tsend, trecv.at[(at - STATE) // 2], at + 1, partner)]

    def send_states(order, at):
        scan_states(order, lambda k, p: jnp.zeros((128, 128), WIDE), lambda: jnp.zeros((8, WIDTH), WIDE), False)
        start(exchange(at))

    def carry_states(order, at, takes):
        n = (at - STATE) // 2
        recv(exchange(at))
        scan_states(order, lambda k, p: xrecv[n, k, p] * takes, lambda: trecv[n] * takes, True)

    forward = list(range(chunks))
    takes_forward = half.astype(WIDE)
    send_states(forward, STATE)
    planned("qry")
    proj[0] = low(dot(n1[...], query_w()))
    n1t[...] = n1[...].T
    planned("scan")
    carry_states(forward, STATE, takes_forward)
    first_half = iota2((CHUNK, LANES), 1) < 64

    def over_heads(lo_part, hi_part):
        return jnp.where(first_half, lo_part, hi_part)

    def head_max(v):
        return over_heads(
            jnp.max(jnp.where(first_half, v, -jnp.inf), axis=-1, keepdims=True),
            jnp.max(jnp.where(first_half, -jnp.inf, v), axis=-1, keepdims=True),
        )

    def head_sum(v):
        return over_heads(
            jnp.sum(jnp.where(first_half, v, 0.0), axis=-1, keepdims=True),
            jnp.sum(jnp.where(first_half, 0.0, v), axis=-1, keepdims=True),
        )

    def attend(rows, i):
        planned_at("att%d", i)
        mask = vis[i]
        carried = hcar[i]
        totals = dot(mask[:, 0:128], proj[3, rows, :]) + jnp.concatenate([carried] * PAIRS, axis=1) * tin[i, 0:1, :]
        rtot[rows, :] = 1.0 / totals
        q, k, v, w = ([proj[n, rows, cols] for cols in pair_cols] for n in range(4))
        w2 = [two(w[p]) for p in every]
        cross = [low(dot_nt(q[p], two(k[p]))) * mask for p in every]
        from_state = [dot(q[p], sin[0, i, p]) for p in every]
        numer = [dot(cross[p], w2[p]) for p in every]
        r = [rtot[rows, cols] for cols in pair_cols]
        s = [(numer[p] + carried * from_state[p]) * r[p] for p in every]
        e = [jnp.exp(s[p] - head_max(s[p])) for p in every]
        pr = [e[p] / head_sum(e[p]) for p in every]
        sc = [low(pr[p] * r[p]) for p in every]
        for p in every:
            score[rows, pair_cols[p]] = s[p]
            prob[rows, pair_cols[p]] = pr[p]
            scaled[rows, pair_cols[p]] = sc[p]
        mix = [low(dot_nt(sc[p], w2[p])) * mask for p in every]
        from_state = [dot(sc[p], sin[1, i, p]) for p in every]
        near = [dot(mix[p], two(v[p])) for p in every]
        for p in every:
            att[rows, pair_cols[p]] = low(near[p] + carried * from_state[p])

    by_chunk(attend)

    planned("outp")
    mid[...] = x_v[...] + dot(att[...], out_w())
    acc[...] = mid[...]
    cot_copy.wait()

    def norm_two(rows, i):
        xhat, _ = norm_parts(mid[rows, :])
        n2[rows, :] = low(xhat * gain_two)
        gf[rows, :] = low(cot_v[rows, :])
        gtwo[rows, :] = jnp.zeros((CHUNK, WIDTH), WIDE)

    by_chunk(norm_two)
    n2t[...] = n2[...].T
    gft[...] = gf[...].T

    def tile_place(t, places):
        at = places[0]
        for k in range(1, 4):
            if places[k] != places[0]:
                at = jnp.where(t == k, places[k], at)
        return at

    def feed(t, _):
        planned_at("ffn%da", t)
        hidden = dot(n2[...], up_w(t))
        cdf = 0.5 * (1.0 + lax.erf(hidden * 0.7071067811865476))
        active = low(hidden * cdf)
        slope = cdf + hidden * (jnp.exp(-0.5 * hidden * hidden) * 0.3989422804014327)
        grad_hidden = low(dot(gf[...], down_w(t)) * slope)
        planned_at("ffn%db", t)
        acc[...] += dot_nt(active, down_w(t))
        gtwo[...] += dot_nt(grad_hidden, up_w(t))
        g_up = low(dot(n2t[...], grad_hidden))
        g_down = low(dot(gft[...], active))
        if linked:
            for (_, core, at, odp, oslot), *later in zip(*(owners(mode) for mode in SCATTER_MODES[TILE:])):
                at = tile_place(t, [at] + [other[2] for other in later])
                rows, cols = slice(odp * 64, odp * 64 + 64), slice(oslot * 128, oslot * 128 + 128)
                rss[TILE][t, core, at, 0:64, :] = g_up[rows, cols]
                rss[TILE][t, core, at, 64:128, :] = g_down[rows, cols]
            scatter_step(TILE + t, 0, 128)
        else:
            outs[7][t] = g_up
            outs[8][t] = g_down
        return 0

    lax.fori_loop(0, 4, feed, 0)

    def norm_two_back(rows, i):
        outb[rows, :] = low(acc[rows, :])
        xhat, inv = norm_parts(mid[rows, :])
        up = gtwo[rows, :]
        grad = cot_v[rows, :] + norm_back(xhat, inv, gain_two, up)
        cot_v[rows, :] = grad
        gf[rows, :] = low(grad)
        gains[3:4, :] = gains[3:4, :] + jnp.sum(up * xhat, axis=0, keepdims=True)

    planned("n2b")
    gains[2:8, :] = jnp.zeros((6, WIDTH), WIDE)
    by_chunk(norm_two_back)
    ol.start()
    planned("ga")
    ga[...] = low(dot_nt(gf[...], out_w()))
    planned("gout")
    g_out = low(dot_tn(att[...], gf[...]))

    def pack_square(n, grad):
        for index, core, at, _, _ in owners(SCATTER_MODES[n]):
            for t in range(4):
                rss[n][core, at, t * 16 : t * 16 + 16, :] = grad[
                    index * 16 : index * 16 + 16, t * 128 : t * 128 + 128
                ]

    if linked:
        pack_square(OUT_W, g_out)
    else:
        outs[5][...] = g_out

    def back_first(rows, i):
        planned_at("B1_%d", i)
        mask = vis[i]
        carried = hcar[i]
        carried_n = hcar_n[i]
        q, k, v, w = ([proj[n, rows, cols] for cols in pair_cols] for n in range(4))
        g = [ga[rows, cols] for cols in pair_cols]
        w2 = [two(w[p]) for p in every]
        gmix = [low(dot_nt(g[p], two(v[p]))) * mask for p in every]
        from_state = [dot_nt(g[p], sin[1, i, p]) for p in every]
        near = [dot(gmix[p], w2[p]) for p in every]
        r, pr, s = ([ref[rows, cols] for cols in pair_cols] for ref in (rtot, prob, score))
        gs = [low(near[p] + carried * from_state[p]).astype(WIDE) for p in every]
        gp = [gs[p] * r[p] for p in every]
        gscore = [pr[p] * (gp[p] - head_sum(pr[p] * gp[p])) for p in every]
        gn = [low(gscore[p] * r[p]) for p in every]
        gt = [low(-(gp[p] * pr[p] + gscore[p] * s[p]) * r[p]) for p in every]
        for p in every:
            gnum[rows, pair_cols[p]] = gn[p]
            gtot[rows, pair_cols[p]] = gt[p]
        gcross = [low(dot_nt(gn[p], w2[p])) * mask for p in every]
        from_state = [dot_nt(gn[p], sin[0, i, p]) for p in every]
        near = [dot(gcross[p], two(k[p])) for p in every]
        qn = [dot_tn(q[p] * carried_n, gn[p]) for p in every]
        gsc = [dot_tn(g[p] * carried_n, scaled[rows, pair_cols[p]]) for p in every]
        for p in every:
            gproj[0, rows, pair_cols[p]] = low(near[p] + carried * from_state[p])
            loc[0, i, p] = qn[p] * bdm[...]
            loc[1, i, p] = gsc[p] * bdm[...]
        tloc[i] = jnp.broadcast_to(
            dot(
                jnp.ones((8, CHUNK), NARROW),
                jnp.concatenate(gt, axis=1) * jnp.concatenate([carried_n] * PAIRS, axis=1),
            ),
            (8, WIDTH),
        )

    by_chunk(back_first)
    planned("send2")
    sent(exchange(STATE))
    send_states(forward[::-1], BACK)
    planned("qg")
    grad = low(dot(n1t[...], gproj[0]))
    if linked:
        pack_square(QUERY, grad)
    else:
        outs[2][...] = grad
    planned("scan2")
    carry_states(forward[::-1], BACK, 1.0 - takes_forward)
    def back_value(rows, i):
        planned_at("bv%d", i)
        mask = vist[i]
        ends = tail[i]
        w, g, sc = ([m[rows, cols] for cols in pair_cols] for m in (proj.at[3], ga, scaled))
        g2, sc2 = ([two(m[p]) for p in every] for m in (g, sc))
        mix = [low(dot_nt(w[p], sc2[p])) * mask for p in every]
        from_state = [dot_nt(w[p], sin[1, i, p]) for p in every]
        near = [dot(mix[p], g2[p]) for p in every]
        for p in every:
            gproj[2, rows, pair_cols[p]] = low(near[p] + ends * from_state[p])

    by_chunk(back_value)
    planned("wV")
    grad = low(dot(n1t[...], gproj[2]))
    if linked:
        pack_square(VALUE, grad)
    else:
        outs[4][...] = grad

    def back_second(rows, i):
        planned_at("B2_%d", i)
        mask = vist[i]
        ends = tail[i]
        wc = dot(mask[:, 0:128], gtot[rows, :]) + jnp.concatenate([ends] * PAIRS, axis=1) * tin[i, 0:1, :]
        q, k, v, w = ([proj[n, rows, cols] for cols in pair_cols] for n in range(4))
        g, sc, gn = ([ref[rows, cols] for cols in pair_cols] for ref in (ga, scaled, gnum))
        g2, sc2, gn2, q2 = ([two(m[p]) for p in every] for m in (g, sc, gn, q))
        s_query, s_grad = ([sin[n, i, p] for p in every] for n in range(2))
        gmix = [low(dot_nt(v[p], g2[p])) * mask for p in every]
        cross = [low(dot_nt(k[p], q2[p])) * mask for p in every]
        gcross = [low(dot_nt(w[p], gn2[p])) * mask for p in every]
        from_state = [dot_nt(w[p], s_query[p]) for p in every]
        near = [dot(gcross[p], q2[p]) for p in every]
        for p in every:
            gproj[1, rows, pair_cols[p]] = low(near[p] + ends * from_state[p])
        from_state = [dot(v[p], s_grad[p]) + dot(k[p], s_query[p]) for p in every]
        near = [dot(gmix[p], sc2[p]) + dot(cross[p], gn2[p]) for p in every]
        for p in every:
            gw = low(near[p] + ends * from_state[p] + wc[:, pair_cols[p]]).astype(WIDE)
            gproj[3, rows, pair_cols[p]] = low(gw * expo[rows, pair_cols[p]])
        planned_at("G%d", i)
        up = dot_nt(gproj[0, rows, :], query_w()) + dot_nt(gproj[1, rows, :], key_w())
        up = up + dot_nt(gproj[2, rows, :], value_w()) + dot_nt(gproj[3, rows, :], w_slot[...])
        xhat, inv = norm_parts(x_v[rows, :])
        ginb[rows, :] = low(cot_v[rows, :] + norm_back(xhat, inv, gain_one, up))
        gains[2:3, :] = gains[2:3, :] + jnp.sum(up * xhat, axis=0, keepdims=True)

    by_chunk(back_second)

    il = pltpu.make_async_copy(ginb, gin_ref.at[row, own_rows], lsem.at[3])
    il.start()
    planned("wK")
    for n, piece in ((1, KEY), (3, SLOT)):
        grad = low(dot(n1t[...], gproj[n]))
        if n == 3:
            grad = low(dot_nt(grad, perm[...]))
        if not linked:
            outs[2 + n if n < 3 else 6][...] = grad
        elif n < 3:
            pack_square(piece, grad)
        else:
            for index, core, at, odp, oslot in owners(SCATTER_MODES[SLOT]):
                rss[SLOT][core, at, 0:64, :] = grad[odp * 64 : odp * 64 + 64, oslot * 128 : oslot * 128 + 128]
                window = index // 8
                rss[SLOT][core, at, 64:80, :] = low(
                    jnp.concatenate(
                        [gains[2:4, window * 128 : window * 128 + 128], jnp.zeros((14, 128), WIDE)], axis=0
                    )
                )
        planned("wS" if n == 1 else "end")
    if not linked:
        outs[9][...] = gains[2:4, :]

    ol.wait()
    il.wait()
    for base in (OUT, GIN):
        for i in range(chunks):
            spread(base, i)[0].wait_send()
        spread_all(base, 0).wait()
        spread_all(base, 1).wait()
    sent(exchange(BACK))
    if linked:
        for n in range(9):
            sent([scatter_all(n, stage) for stage in range(len(SCATTER_MODES[n][0]) + 1)])


def finish_kernel(out_ref, gin_ref, small_ref, o, g, gq, gk, gv, go, gs, gu, gd, g1, g2):
    step = pl.program_id(0)
    per_row = out_ref.shape[1] // o.shape[1]
    rows = pl.ds(pl.multiple_of((step % per_row) * o.shape[1], o.shape[1]), o.shape[1])
    o[0] = out_ref[step // per_row, rows, :].astype(WIDE)
    g[0] = gin_ref[step // per_row, rows, :].astype(WIDE)

    @pl.when(pl.program_id(0) == 0)
    def _():
        base = 0
        bases = []
        for rows in PIECE_ROWS:
            bases.append(base)
            base += rows
        gs[...] = small_ref[0:64, :]
        mine = lax.axis_index("dp") * lax.axis_size("slot") + lax.axis_index("slot")
        window = small_ref[64:72, :]
        lanes = iota2((8, 128), 1)
        first = (mine % 8) * 16
        moved = jnp.concatenate(
            [
                jnp.sum(jnp.where(lanes == first + k, window, 0.0), axis=1, keepdims=True)
                for k in range(16)
            ],
            axis=1,
        )
        g1[...] = moved[0:1]
        g2[...] = moved[1:2]
        for t in range(4):
            cols = slice(t * 128, t * 128 + 128)
            for n, target in ((QUERY, gq), (KEY, gk), (VALUE, gv), (OUT_W, go)):
                target[:, cols] = small_ref[bases[n] + t * 16 : bases[n] + t * 16 + 16, :]
            gu[:, cols] = small_ref[bases[TILE + t] : bases[TILE + t] + 64, :]
            gd[:, cols] = small_ref[bases[TILE + t] + 64 : bases[TILE + t] + 128, :]


def finish(out, gin, small):
    rows, length, width = out.shape
    count = 512
    block = pl.BlockSpec((1, count, width), lambda i: (i // (length // count), i % (length // count), 0))
    here = pl.BlockSpec(memory_space=pltpu.VMEM)
    whole = lambda shape: pl.BlockSpec(shape, lambda i: (0,) * len(shape))
    shapes = [(16, width)] * 4 + [(64, 128), (64, width), (64, width), (1, 16), (1, 16)]
    shape = jax.ShapeDtypeStruct
    return pl.pallas_call(
        finish_kernel,
        grid=(rows * length // count,),
        out_shape=[shape(out.shape, WIDE)] * 2 + [shape(s, WIDE) for s in shapes],
        in_specs=[here] * 3,
        out_specs=[block, block] + [whole(s) for s in shapes],
        compiler_params=pltpu.CompilerParams(vmem_limit_bytes=32 * 1024 * 1024),
    )(*(pltpu.with_memory_space_constraint(v, pltpu.VMEM) for v in (out, gin, small)))


def run_block(linked, inputs, starts, cotangent, weights):
    rows, length, width = inputs.shape
    tokens = length // 2
    chunks = tokens // CHUNK
    vm = pltpu.VMEM
    scratch = [
        vm((tokens, width), WIDE), vm((tokens, width), WIDE),
        vm((width, width), NARROW), vm((width, width), NARROW), vm((8, width), WIDE),
        vm((tokens, width), NARROW), vm((width, tokens), NARROW),
        vm((4, tokens, width), NARROW), vm((tokens, width), WIDE),
        vm((tokens, width), WIDE), vm((tokens, width), WIDE), vm((tokens, width), WIDE),
        vm((tokens, width), NARROW), vm((tokens, width), NARROW),
        vm((tokens, width), WIDE), vm((tokens, width), WIDE),
        vm((tokens, width), NARROW), vm((width, tokens), NARROW),
        vm((tokens, width), NARROW), vm((width, tokens), NARROW), vm((tokens, width), WIDE),
        vm((tokens, width), NARROW), vm((4, tokens, width), NARROW),
        vm((tokens, width), NARROW), vm((tokens, width), NARROW),
        vm((tokens, width), NARROW), vm((tokens, width), NARROW),
        vm((chunks, CHUNK, 256), NARROW), vm((chunks, CHUNK, 256), NARROW),
        vm((chunks, CHUNK, LANES), WIDE), vm((chunks, CHUNK, LANES), WIDE), vm((chunks, CHUNK, LANES), WIDE),
        vm((chunks, CHUNK, LANES), NARROW), vm((chunks, CHUNK, LANES), NARROW),
        vm((2, chunks, PAIRS, 128, 128), WIDE), vm((2, chunks, PAIRS, 128, 128), NARROW),
        vm((chunks, 8, width), WIDE), vm((chunks, 8, width), WIDE),
        vm((CHUNK, LANES), NARROW), vm((CHUNK, LANES), NARROW), vm((CHUNK, LANES), WIDE),
        vm((2, PAIRS, 128, 128), WIDE), vm((2, 2, PAIRS, 128, 128), WIDE),
        vm((8, width), WIDE), vm((2, 8, width), WIDE),
        pltpu.SemaphoreType.DMA((88,)), pltpu.SemaphoreType.DMA((88,)), pltpu.SemaphoreType.DMA((12,)),
    ]
    if linked:
        for lead in ((2, 16), (2, 16), (16,)):
            scratch += [vm((*lead, r, LANES), NARROW) for r in PIECE_ROWS[:TILE]]
            scratch += [vm((4, *lead, 128, LANES), NARROW)]
        for k in range(3):
            for r, mode in zip(PIECE_ROWS, SCATTER_MODES):
                sizes, steps = strides(mode)
                blocks = (sizes[k] - 1) * steps[k] if k < len(sizes) else 0
                scratch += [vm((blocks, r, LANES) if blocks else (1, 16, LANES), NARROW)]
    else:
        scratch += [vm((4, width, width), NARROW)] * 3
    anywhere = pl.BlockSpec(memory_space=pl.ANY)
    here = pl.BlockSpec(memory_space=pltpu.VMEM)
    shape = jax.ShapeDtypeStruct
    big = [pltpu.VMEM((rows, length, width), NARROW)] * 2
    square = (width, width)
    if linked:
        small = [pltpu.VMEM((SMALL_ROWS, LANES), WIDE)]
        weight_specs = [here] * 9
    else:
        small = [shape(square, NARROW)] * 5 + [shape((4, *square), NARROW)] * 2 + [shape((2, width), WIDE)]
        weight_specs = [anywhere] * 7 + [here] * 2
    return pl.pallas_call(
        functools.partial(block_kernel, linked, 12, 2 + len(small)),
        out_shape=big + small,
        in_specs=[anywhere, here, anywhere] + weight_specs,
        out_specs=[here] * (2 + len(small)),
        scratch_shapes=scratch,
        compiler_params=pltpu.CompilerParams(
            collective_id=0, has_side_effects=True, vmem_limit_bytes=57 * 1024 * 1024
        ),
    )(inputs, starts, cotangent, *weights)


def on_device(
    inputs, starts, w_query, w_key, w_value, w_out, w_slot, w_up, w_down, gain_attn, gain_ffn, cotangent
):
    n_dp, n_slot = lax.axis_size("dp"), lax.axis_size("slot")
    if n_dp == 8 and n_slot == 4:
        weights = (
            w_query, w_key, w_value, w_out, w_slot, w_up, w_down.T,
            gain_attn.reshape(1, -1), gain_ffn.reshape(1, -1),
        )
        out, gin, small = run_block(True, inputs, starts, cotangent, weights)
        out, gin, gq, gk, gv, go, gs, gu, gd, g1, g2 = finish(out, gin, small)
        return out, gin, gq, gk, gv, go, gs, gu, gd.T, g1.reshape(-1), g2.reshape(-1)

    def whole(v, names, axis):
        return lax.all_gather(v, names, axis=axis, tiled=True)

    both = ("dp", "slot")
    width = inputs.shape[-1]
    up = whole(whole(w_up, "dp", 0), "slot", 1).reshape(width, 4, 4, 128).transpose(2, 0, 1, 3)
    down = whole(whole(w_down, "dp", 1), "slot", 0).reshape(4, 4, 128, width).transpose(1, 3, 0, 2)
    up, down = up.reshape(4, width, width), down.reshape(4, width, width)
    weights = (
        whole(w_query, both, 0), whole(w_key, both, 0), whole(w_value, both, 0), whole(w_out, both, 0),
        whole(whole(w_slot, "dp", 0), "slot", 1), up, down,
        whole(gain_attn, both, 0).reshape(1, -1), whole(gain_ffn, both, 0).reshape(1, -1),
    )
    out, gin, gq, gk, gv, go, gs, gu, gd, gg = run_block(False, inputs, starts, cotangent, weights)

    def shared(v, names, axis):
        return lax.psum_scatter(v.astype(WIDE), names, scatter_dimension=axis, tiled=True)

    gu = gu.reshape(4, width, 4, 128).transpose(1, 2, 0, 3).reshape(width, -1)
    gd = gd.reshape(4, width, 4, 128).transpose(2, 0, 3, 1).reshape(-1, width)
    return (
        out.astype(WIDE), gin.astype(WIDE),
        shared(gq, both, 0), shared(gk, both, 0), shared(gv, both, 0), shared(go, both, 0),
        shared(shared(gs, "slot", 1), "dp", 0), shared(shared(gu, "slot", 1), "dp", 0),
        shared(shared(gd, "slot", 0), "dp", 1), shared(gg[0], both, 0), shared(gg[1], both, 0),
    )


def solution(mesh):
    every = ("dp", "slot")
    rows = P("dp", None, None)
    return jax.shard_map(
        on_device,
        mesh=mesh,
        in_specs=(
            rows, P("dp", None), P(every, None), P(every, None), P(every, None), P(every, None),
            P("dp", "slot"), P("dp", "slot"), P("slot", "dp"), P(every), P(every), rows,
        ),
        out_specs=(
            rows, rows, P(every, None), P(every, None), P(every, None), P(every, None),
            P("dp", "slot"), P("dp", "slot"), P("slot", "dp"), P(every), P(every),
        ),
        check_vma=False,
    )
```

```python
import functools

import jax
import jax.numpy as jnp
from jax import lax
from jax.experimental import pallas as pl
from jax.experimental.pallas import tpu as pltpu
from jax.sharding import PartitionSpec as P

HEADS = 8
EPSILON = 1e-05
NARROW = jnp.bfloat16
WIDE = jnp.float32
MESH = pl.DeviceIdType.MESH

WIDTH = 512
CHUNK = 128
PAIRS = 4
LANES = 128
PIECE_ROWS = (80, 64, 64, 64, 64, 128, 128, 128, 128)
SLOT, KEY, VALUE, QUERY, OUT_W, TILE = range(6)
SMALL_ROWS = sum(PIECE_ROWS)
GATHER_MODES = (
    ("ABZ", "m"), ("ABZ", "m"), ("ABZ", "m"), ("ABZ", "m"), ("ABZ", "m"),
    ("ABZ", "m"), ("AZB", "m"), ("ABZ", "m"), ("AZB", "m"),
)
SCATTER_MODES = (
    ("ABZ", "m"), ("AZB", "x"), ("ABZ", "x"), ("ABZ", "m"), ("ABZ", "m"),
    ("ABZ", "y"), ("ZAB", "x"), ("AZB", "x"), ("AZB", "x"),
)
PLAN = {
    "slot": (
        "S1", "K1", "T11", "V1", "S2", "Q1", "K2", "V2", "S3", "O1", "T01", "K3", "S4", "Q2",
        "V3", "K4", "T31", "T21",
    ),
    "val": ("O2", "V4", "T02",),
    "qry": ("Q3", "Q4", "T12",),
    "att0": ("O3",),
    "att1": ("T22",),
    "att3": ("T03",),
    "outp": ("O4",),
    "ffn0a": ("T04", "T32", "T13",),
    "ffn1a": ("T23", "T14",),
    "ffn2a": ("T24",),
    "ffn2b": ("T33", "T0.1",),
    "ffn3a": ("T1.1", "T34",),
    "ga": ("o1", "T2.1", "o0",),
    "B1_1": ("O.0", "T3.1",),
    "send2": ("o2",),
    "qg": ("o3", "p1",),
    "scan2": ("Q.0", "T2.2", "O.1",),
    "B2_0": ("V.0",),
    "B2_1": ("Q.1", "T0.2",),
    "B2_2": ("T3.2", "y1",),
    "B2_3": ("y2", "V.1",),
    "wS": ("O.2", "K.0",),
    "end": (
        "S.0", "p3", "Q.2", "T2.3", "T0.3", "K.1", "S.1", "V.2", "O.3", "Q.3", "T1.2", "y0", "K.2", "T3.3",
        "S.2", "T2.4", "V.3", "p0", "y3", "O.4", "f0", "p2", "S.3", "T1.3", "T3.4", "T0.4", "f2", "f1",
        "K.3", "f3", "V.4", "Q.4", "T1.4", "K.4", "S.4",
    ),
}
SEMS = 4


def dot(a, b):
    return lax.dot_general(a, b, (((1,), (0,)), ((), ())), preferred_element_type=WIDE)


def dot_nt(a, b):
    return lax.dot_general(a, b, (((1,), (1,)), ((), ())), preferred_element_type=WIDE)


def dot_tn(a, b):
    return lax.dot_general(a, b, (((0,), (0,)), ((), ())), preferred_element_type=WIDE)


def low(v):
    return v.astype(NARROW)


def iota2(shape, dim):
    return lax.broadcasted_iota(jnp.int32, shape, dim)


def row_mean(v):
    return jnp.sum(v, axis=-1, keepdims=True) * (1.0 / v.shape[-1])


def norm_parts(v):
    center = v - row_mean(v)
    inv = lax.rsqrt(row_mean(center * center) + EPSILON)
    return center * inv, inv


def norm_back(xhat, inv, gain, up):
    u = up * gain
    return (u - row_mean(u) - xhat * row_mean(u * xhat)) * inv


def strides(mode):
    sizes = [2 if axis in "AB" else 4 for axis in mode[0]]
    steps = [1]
    for size in sizes[:0:-1]:
        steps.insert(0, steps[0] * size)
    return sizes, steps


def owners(mode):
    out = []
    _, steps = strides(mode)
    for dp in range(8):
        for slot in range(4):
            z, x, y, c = dp // 2, dp % 2, slot // 2, slot % 2
            first_y = mode[1] == "y" or (mode[1] == "m" and c == 0)
            at = {"A": y if first_y else x, "B": x if first_y else y, "Z": z, "P": x * 2 + y}
            place = sum(at[axis] * step for axis, step in zip(mode[0], steps))
            out.append((dp * 4 + slot, c, place, dp, slot))
    return out


def square_of(buf, n):
    return jnp.concatenate(
        [
            jnp.concatenate([buf[core, at, t * 16 : t * 16 + 16, :] for t in range(4)], axis=1)
            for _, core, at, _, _ in owners(GATHER_MODES[n])
        ],
        axis=0,
    )


def tile_place(t, places):
    at = places[0]
    for k in range(1, 4):
        if places[k] != places[0]:
            at = jnp.where(t == k, places[k], at)
    return at


def tile_of(buf, n, first):
    spots = {}
    for each in zip(*(owners(mode) for mode in GATHER_MODES[TILE:])):
        _, core, _, dp, slot = each[0]
        spots[dp, slot] = core, tile_place(n, [at for _, _, at, _, _ in each])
    return jnp.concatenate(
        [
            jnp.concatenate(
                [buf[(n, *spots[dp, slot], slice(first, first + 64), slice(None))] for dp in range(8)], axis=0
            )
            for slot in range(4)
        ],
        axis=1,
    )


def block_kernel(linked, n_in, n_out, *refs):
    ins, outs, scr = refs[:n_in], refs[n_in : n_in + n_out], refs[n_in + n_out :]
    inputs_ref, starts_ref, cot_ref = ins[:3]
    out_ref, gin_ref = outs[:2]
    (x_v, cot_v, w_slot, perm, gains, n1, n1t, proj, expo, score, prob,
     rtot, scaled, att, mid, acc, n2, n2t, gf, gft, gtwo, ga, gproj, gnum, gtot, outb, ginb,
     vis, vist, hcar, tail, passf, hcar_n, tail_n, loc, sin, tloc, tin, bd_lo, bd_hi, bdm, xsend, xrecv, tsend, trecv,
     ssem, rsem, lsem) = scr[:48]
    rest = scr[48:]

    slot = lax.axis_index("slot")
    dp = lax.axis_index("dp")
    y, c = slot // 2, slot % 2
    row, half = y, c
    tokens = x_v.shape[0]
    chunks = tokens // CHUNK
    partner = (dp, y * 2 + (1 - c))
    y_peer = (dp, (1 - y) * 2 + c)
    if linked:
        ags, rss, rcs = (rest[6 * n : 6 * n + 6] for n in range(3))
        got_refs = [rest[18 + 9 * n : 27 + 9 * n] for n in range(3)]
        z, x = dp // 2, dp % 2
        x_peer = (z * 2 + 1 - x, slot)
        near = {
            "x": (x, y, x_peer, y_peer),
            "y": (y, x, y_peer, x_peer),
            "m": (
                y + c * (x - y),
                x + c * (y - x),
                (z * 2 + x + c * (1 - 2 * x), slot + (1 - c) * 2 * (1 - 2 * y)),
                (z * 2 + x + (1 - c) * (1 - 2 * x), slot + c * 2 * (1 - 2 * y)),
            ),
        }
        z_peers = [((((z + s) % 4) * 2 + x), slot) for s in (1, 2, 3)]
        diagonal = (z * 2 + 1 - x, (1 - y) * 2 + c)
        peers = [partner, x_peer, y_peer] + z_peers
    else:
        peers = [partner, y_peer]

    barrier = pltpu.get_barrier_semaphore()
    for peer in peers:
        pl.semaphore_signal(barrier, inc=1, device_id=peer, device_id_type=MESH)

    own_rows = pl.ds(pl.multiple_of(half * tokens, tokens), tokens)
    x_copy = pltpu.make_async_copy(inputs_ref.at[row, own_rows], x_v, lsem.at[0])
    cot_copy = pltpu.make_async_copy(cot_ref.at[row, own_rows], cot_v, lsem.at[1])
    x_copy.start()
    cot_copy.start()

    def remote(src, dst, at, device, send_at=None):
        return pltpu.make_async_remote_copy(
            src_ref=src, dst_ref=dst, recv_sem=rsem.at[at],
            send_sem=ssem.at[send_at if send_at is not None else at if at < SCATTER else at - SCATTER],
            device_id=device, device_id_type=MESH,
        )

    def start(copies):
        for copy in copies:
            copy.start()

    def recv(copies):
        for copy in copies:
            copy.wait_recv()

    def sent(copies):
        for copy in copies:
            copy.wait_send()

    def view(bufs, n):
        return bufs[n] if n < TILE else bufs[TILE].at[n - TILE]

    def axes(mode):
        pa, pb, dev_a, dev_b = near[mode[1]]
        known = {
            "A": (pa, [(1 - pa, dev_a)]),
            "B": (pb, [(1 - pb, dev_b)]),
            "Z": (z, [((z + s + 1) % 4, z_peers[s]) for s in range(3)]),
            "P": (x * 2 + y, [((1 - x) * 2 + y, x_peer), (x * 2 + 1 - y, y_peer), ((1 - x) * 2 + 1 - y, diagonal)]),
        }
        return [(known[axis][0], step, known[axis][1]) for axis, step in zip(mode[0], strides(mode)[1])]

    def place_in(mode, upto=None):
        return sum(at * step for at, step, _ in axes(mode)[:upto])

    def gather_along(n, k):
        mode = GATHER_MODES[n]
        _, step, others = axes(mode)[k]
        part = view(ags, n).at[c, pl.ds(place_in(mode, k + 1), step)]
        return [remote(part, part, n * SEMS + k, device) for _, device in others]

    def gather_along_all(n, k):
        _, step, others = axes(GATHER_MODES[n])[k]
        part = view(ags, n).at[c, pl.ds(0, step * len(others))]
        return remote(part, part, n * SEMS + k, partner)

    def gather_across(n, k):
        mode = GATHER_MODES[n]
        _, step, others = axes(mode)[k]
        base = place_in(mode, k)
        if k == len(mode[0]) - 1:
            parts = [pl.ds(base, strides(mode)[0][k])]
        else:
            parts = [pl.ds(base + place * step, step) for place, _ in others]
        refs = [view(ags, n).at[c, part] for part in parts]
        return [remote(ref, ref, n * SEMS + 3, partner) for ref in refs]

    def gather_across_all(n):
        every_block = view(ags, n).at[c]
        return remote(every_block, every_block, n * SEMS + 3, partner)

    def gather_step(n, stage):
        count = len(GATHER_MODES[n][0])
        if stage > count:
            gather_across_all(n).wait_recv()
            return
        if stage:
            gather_along_all(n, count - stage).wait_recv()
        if stage < count:
            start(gather_along(n, count - 1 - stage))
        if stage:
            start(gather_across(n, count - stage))

    def gather_sent(n):
        sent([gather_along_all(n, k) for k in range(len(GATHER_MODES[n][0]))] + [gather_across_all(n)])

    def scatter_copies(n, stage):
        buf, at, send = view(rss, n), SCATTER + n * SEMS + stage, n * SEMS + stage
        if stage == 0:
            return [remote(buf.at[1 - c], view(rcs, n), at, partner, send)]
        mode = SCATTER_MODES[n]
        _, step, others = axes(mode)[stage - 1]
        base, got = place_in(mode, stage - 1), got_refs[stage - 1][n]
        return [
            remote(buf.at[c, pl.ds(base + place * step, step)], got.at[pl.ds(i * step, step)], at, device, send)
            for i, (place, device) in enumerate(others)
        ]

    def scatter_all(n, stage):
        if stage == 0:
            return scatter_copies(n, stage)[0]
        got = got_refs[stage - 1][n]
        part = view(rss, n).at[c, pl.ds(0, got.shape[0])]
        return remote(part, got, SCATTER + n * SEMS + stage, partner, n * SEMS + stage)

    def scatter_step(n, stage, rows):
        if stage:
            scatter_all(n, stage - 1).wait_recv()
            buf, mode = view(rss, n), SCATTER_MODES[n]
            got = view(rcs, n) if stage == 1 else got_refs[stage - 2][n]
            count = 16 if stage == 1 else axes(mode)[stage - 2][1]
            first, terms = place_in(mode, stage - 1), got.shape[0] // count

            def summed(i):
                total = buf[c, first + i].astype(WIDE)
                for k in range(terms):
                    total = total + got[k * count + i].astype(WIDE)
                return total

            if stage <= len(mode[0]):
                def step(i, _):
                    buf[c, first + i] = low(summed(i))
                    return 0

                lax.fori_loop(0, count, step, 0)
            else:
                small_ref[pl.ds(sum(PIECE_ROWS[:n]), rows), :] = summed(0)
        else:
            gather_sent(n)
        if stage <= (len(SCATTER_MODES[n][0]) if stage else 1):
            start(scatter_copies(n, stage))

    SCATTER = 9 * SEMS
    STATE = SCATTER + 9 * SEMS
    BACK, OUT, GIN = STATE + 2, STATE + 4, STATE + 10

    ins_w = ins[3:]
    if linked:
        small_ref = outs[2]
        wq, wk, wv, wo, ws, wu, wd, ga1, ga2 = ins_w
        place = [place_in(mode) for mode in GATHER_MODES]
        for n, shard in ((QUERY, wq), (KEY, wk), (VALUE, wv), (OUT_W, wo)):
            for t in range(4):
                ags[n][c, place[n], pl.ds(t * 16, 16), :] = shard[:, t * 128 : t * 128 + 128]
        ags[SLOT][c, place[SLOT], pl.ds(0, 64), :] = ws[...]
        rows16 = iota2((16, 16), 0)
        both = jnp.where(
            rows16 == 0,
            jnp.broadcast_to(ga1[...].astype(WIDE), (16, 16)),
            jnp.where(rows16 == 1, jnp.broadcast_to(ga2[...].astype(WIDE), (16, 16)), 0.0),
        )
        lane_at = ((dp * 4 + slot) % 8) * 16
        spread = jnp.where(iota2((16, 128), 1) == iota2((16, 128), 0) + lane_at, 1.0, 0.0)
        ags[SLOT][c, place[SLOT], pl.ds(64, 16), :] = low(dot(low(both), low(spread)))
        for t in range(4):
            ags[TILE][t, c, place[TILE + t], pl.ds(0, 64), :] = wu[:, t * 128 : t * 128 + 128]
            ags[TILE][t, c, place[TILE + t], pl.ds(64, 64), :] = wd[:, t * 128 : t * 128 + 128]
        query_w, key_w, value_w, out_w = (
            functools.partial(square_of, ags[n], n) for n in (QUERY, KEY, VALUE, OUT_W)
        )

        def up_w(t):
            return tile_of(ags[TILE], t, 0)

        def down_w(t):
            return tile_of(ags[TILE], t, 64)
    else:
        square_v, up_v, down_v = rest
        fw_q, fw_k, fw_v, fw_o, fw_s, fw_u, fw_d, fg1, fg2 = ins_w
        copies = [
            pltpu.make_async_copy(src, dst, lsem.at[4 + i])
            for i, (src, dst) in enumerate((
                (fw_q, square_v.at[0]), (fw_k, square_v.at[1]), (fw_v, square_v.at[2]), (fw_o, square_v.at[3]),
                (fw_s, w_slot), (fw_u, up_v), (fw_d, down_v),
            ))
        ]
        start(copies)
        for copy in copies:
            copy.wait()
        gains[0:1, :] = fg1[...].astype(WIDE)
        gains[1:2, :] = fg2[...].astype(WIDE)
        query_w, key_w, value_w, out_w = (lambda n=n: square_v[n] for n in range(4))

        def up_w(t):
            return up_v[t]

        def down_w(t):
            return down_v[t]

    pl.semaphore_wait(barrier, len(peers))

    ol = pltpu.make_async_copy(outb, out_ref.at[row, own_rows], lsem.at[2])
    results = {OUT: (outb, out_ref), GIN: (ginb, gin_ref)}

    def spread(base, i):
        source, target = results[base]
        part = pl.ds(pl.multiple_of(half * tokens + i * CHUNK, CHUNK), CHUNK)
        mine, theirs = target.at[row, part], target.at[1 - row, part]
        chunk = source.at[pl.ds(i * CHUNK, CHUNK)]
        return (
            remote(chunk, mine, base + i, y_peer),
            remote(chunk, mine, base + chunks, partner),
            remote(theirs, theirs, base + chunks + 1, partner),
        )

    def spread_all(base, k):
        mine = results[base][1].at[row, own_rows]
        return remote(mine, mine, base + chunks + k, partner)

    def spread_steps(word):
        copies = spread(OUT if word[0] in "op" else GIN, int(word[1]))
        if word[0] in "oy":
            copies[0].start()
            copies[1].start()
        else:
            copies[0].wait_recv()
            copies[2].start()

    names = {"S": SLOT, "K": KEY, "V": VALUE, "Q": QUERY, "O": OUT_W}
    names.update({"T%d" % t: TILE + t for t in range(4)})

    def planned(block):
        for word in PLAN.get(block, ()):
            if word[0] in "opyf":
                spread_steps(word)
            elif linked:
                if "." in word:
                    piece, stage = word.split(".")
                    scatter_step(names[piece], int(stage), PIECE_ROWS[names[piece]])
                else:
                    gather_step(names[word[:-1]], int(word[-1]))

    def planned_at(block, i):
        for k in range(4):
            if PLAN.get(block % k):
                pl.when(i == k)(functools.partial(planned, block % k))

    if linked:
        for n in range(9):
            gather_step(n, 0)
    lane = iota2((CHUNK, LANES), 1)
    sub = iota2((CHUNK, LANES), 0)
    bd_lo[...] = low(jnp.where(lane < 64, 1.0, 0.0))
    bd_hi[...] = low(jnp.where(lane < 64, 0.0, 1.0))
    bdm[...] = jnp.where((lane < 64) == (sub < 64), 1.0, 0.0)
    upper = low(jnp.where(sub <= lane, 1.0, 0.0))
    lower = low(jnp.where(sub >= lane, 1.0, 0.0))
    ones = jnp.ones((CHUNK, LANES), NARROW)
    for n in range(chunks):
        begin = starts_ref[:, pl.ds(pl.multiple_of(half * tokens + n * CHUNK, CHUNK), CHUNK)].astype(WIDE)
        begin = jnp.where(row == 0, begin[0:1], begin[1:2])
        begin = low(jnp.broadcast_to(begin, (CHUNK, LANES)))
        by_lane = dot(begin, upper)
        by_row = dot_nt(lower, begin)
        total = dot(begin, ones)
        same = by_row == by_lane
        v = low(jnp.where(same & (sub >= lane), 1.0, 0.0))
        vt = low(jnp.where(same & (sub <= lane), 1.0, 0.0))
        vis[n, :, 0:128] = v
        vis[n, :, 128:256] = v
        vist[n, :, 0:128] = vt
        vist[n, :, 128:256] = vt
        carried = jnp.where(by_row == 0.0, 1.0, 0.0)
        ending = jnp.where(by_row == total, 1.0, 0.0)
        hcar[n] = carried
        tail[n] = ending
        hcar_n[n] = low(carried)
        tail_n[n] = low(ending)
        passf[n] = jnp.where(total == 0.0, 1.0, 0.0)

    def perm_rows(i, _):
        r = iota2((CHUNK, WIDTH), 0) + i * CHUNK
        n = iota2((CHUNK, WIDTH), 1)
        source = ((n >> 4) & 3) * 128 + (n & 15) * 8 + (n >> 6)
        perm[pl.ds(pl.multiple_of(i * CHUNK, CHUNK), CHUNK), :] = low(jnp.where(r == source, 1.0, 0.0))
        return 0

    lax.fori_loop(0, WIDTH // CHUNK, perm_rows, 0)
    x_copy.wait()

    def by_chunk(body):
        def step(i, _):
            body(pl.ds(pl.multiple_of(i * CHUNK, CHUNK), CHUNK), i)
            return 0

        lax.fori_loop(0, chunks, step, 0)

    def norm_one(rows, i):
        gtwo[rows, :], _ = norm_parts(x_v[rows, :])

    by_chunk(norm_one)

    if linked:
        planned("slot")
        for index, core, at, odp, oslot in owners(GATHER_MODES[SLOT]):
            w_slot[odp * 64 : odp * 64 + 64, oslot * 128 : oslot * 128 + 128] = ags[SLOT][core, at, 0:64, :]
        for window in range(4):
            total = jnp.zeros((16, 128), WIDE)
            for index, core, at, _, _ in owners(GATHER_MODES[SLOT]):
                if index // 8 == window:
                    total = total + ags[SLOT][core, at, 64:80, :].astype(WIDE)
            gains[0:8, window * 128 : window * 128 + 128] = total[0:8]
    w_slot[...] = low(dot(w_slot[...], perm[...]))

    gain_one = gains[0:1, :]
    gain_two = gains[1:2, :]

    n1[...] = low(gtwo[...] * gain_one)
    expo[...] = jnp.exp(dot(n1[...], w_slot[...]))
    proj[3] = low(expo[...])
    planned("key")
    proj[1] = low(dot(n1[...], key_w()))
    planned("val")
    proj[2] = low(dot(n1[...], value_w()))
    def two(v):
        return jnp.concatenate([v * bd_lo[...], v * bd_hi[...]], axis=0)

    every = range(PAIRS)
    pair_cols = [slice(p * 128, p * 128 + 128) for p in every]

    def local_states(rows, i):
        w_tail = proj[3, rows, :]
        tloc[i] = jnp.broadcast_to(
            dot(jnp.ones((8, CHUNK), NARROW), w_tail * jnp.concatenate([tail_n[i]] * PAIRS, axis=1)),
            (8, WIDTH),
        )
        w = [proj[3, rows, cols] for cols in pair_cols]
        k_tail = [proj[1, rows, cols] * tail_n[i] for cols in pair_cols]
        v = [proj[2, rows, cols] for cols in pair_cols]
        kw = [dot_tn(k_tail[p], w[p]) for p in every]
        wv = [dot_tn(w[p] * tail_n[i], v[p]) for p in every]
        for p in every:
            loc[0, i, p] = kw[p] * bdm[...]
            loc[1, i, p] = wv[p] * bdm[...]

    planned("loc")
    by_chunk(local_states)

    def scan_states(order, initial, t_initial, keep):
        def one(kind, p):
            state = initial(kind, p)
            for i in order:
                if keep:
                    sin[kind, i, p] = low(state)
                state = loc[kind, i, p] + passf[i] * state
            if not keep:
                xsend[kind, p] = state

        def step(k, _):
            one(k // PAIRS, k % PAIRS)
            return 0

        lax.fori_loop(0, 2 * PAIRS, step, 0)
        state = t_initial()
        for i in order:
            if keep:
                tin[i] = state
            state = tloc[i] + jnp.concatenate([passf[i, 0:8, :]] * PAIRS, axis=1) * state
        if not keep:
            tsend[...] = state

    def exchange(at):
        return [remote(xsend, xrecv.at[(at - STATE) // 2], at, partner), remote(tsend, trecv.at[(at - STATE) // 2], at + 1, partner)]

    def send_states(order, at):
        scan_states(order, lambda k, p: jnp.zeros((128, 128), WIDE), lambda: jnp.zeros((8, WIDTH), WIDE), False)
        start(exchange(at))

    def carry_states(order, at, takes):
        n = (at - STATE) // 2
        recv(exchange(at))
        scan_states(order, lambda k, p: xrecv[n, k, p] * takes, lambda: trecv[n] * takes, True)

    forward = list(range(chunks))
    takes_forward = half.astype(WIDE)
    send_states(forward, STATE)
    planned("qry")
    proj[0] = low(dot(n1[...], query_w()))
    n1t[...] = n1[...].T
    planned("scan")
    carry_states(forward, STATE, takes_forward)
    first_half = iota2((CHUNK, LANES), 1) < 64

    def over_heads(lo_part, hi_part):
        return jnp.where(first_half, lo_part, hi_part)

    def head_max(v):
        return over_heads(
            jnp.max(jnp.where(first_half, v, -jnp.inf), axis=-1, keepdims=True),
            jnp.max(jnp.where(first_half, -jnp.inf, v), axis=-1, keepdims=True),
        )

    def head_sum(v):
        return over_heads(
            jnp.sum(jnp.where(first_half, v, 0.0), axis=-1, keepdims=True),
            jnp.sum(jnp.where(first_half, 0.0, v), axis=-1, keepdims=True),
        )

    def attend(rows, i):
        planned_at("att%d", i)
        mask = vis[i]
        carried = hcar[i]
        totals = dot(mask[:, 0:128], proj[3, rows, :]) + jnp.concatenate([carried] * PAIRS, axis=1) * tin[i, 0:1, :]
        rtot[rows, :] = 1.0 / totals
        q, k, v, w = ([proj[n, rows, cols] for cols in pair_cols] for n in range(4))
        w2 = [two(w[p]) for p in every]
        cross = [low(dot_nt(q[p], two(k[p]))) * mask for p in every]
        from_state = [dot(q[p], sin[0, i, p]) for p in every]
        numer = [dot(cross[p], w2[p]) for p in every]
        r = [rtot[rows, cols] for cols in pair_cols]
        s = [(numer[p] + carried * from_state[p]) * r[p] for p in every]
        e = [jnp.exp(s[p] - head_max(s[p])) for p in every]
        pr = [e[p] / head_sum(e[p]) for p in every]
        sc = [low(pr[p] * r[p]) for p in every]
        for p in every:
            score[rows, pair_cols[p]] = s[p]
            prob[rows, pair_cols[p]] = pr[p]
            scaled[rows, pair_cols[p]] = sc[p]
        mix = [low(dot_nt(sc[p], w2[p])) * mask for p in every]
        from_state = [dot(sc[p], sin[1, i, p]) for p in every]
        near = [dot(mix[p], two(v[p])) for p in every]
        for p in every:
            att[rows, pair_cols[p]] = low(near[p] + carried * from_state[p])

    by_chunk(attend)

    planned("outp")
    mid[...] = x_v[...] + dot(att[...], out_w())
    acc[...] = mid[...]
    cot_copy.wait()

    def norm_two(rows, i):
        xhat, _ = norm_parts(mid[rows, :])
        n2[rows, :] = low(xhat * gain_two)
        gf[rows, :] = low(cot_v[rows, :])
        gtwo[rows, :] = jnp.zeros((CHUNK, WIDTH), WIDE)

    by_chunk(norm_two)
    n2t[...] = n2[...].T
    gft[...] = gf[...].T

    def feed(t, _):
        planned_at("ffn%da", t)
        hidden = dot(n2[...], up_w(t))
        cdf = 0.5 * (1.0 + lax.erf(hidden * 0.7071067811865476))
        active = low(hidden * cdf)
        slope = cdf + hidden * (jnp.exp(-0.5 * hidden * hidden) * 0.3989422804014327)
        grad_hidden = low(dot(gf[...], down_w(t)) * slope)
        planned_at("ffn%db", t)
        acc[...] += dot_nt(active, down_w(t))
        gtwo[...] += dot_nt(grad_hidden, up_w(t))
        g_up = low(dot(n2t[...], grad_hidden))
        g_down = low(dot(gft[...], active))
        if linked:
            for (_, core, at, odp, oslot), *later in zip(*(owners(mode) for mode in SCATTER_MODES[TILE:])):
                at = tile_place(t, [at] + [other[2] for other in later])
                rows, cols = slice(odp * 64, odp * 64 + 64), slice(oslot * 128, oslot * 128 + 128)
                rss[TILE][t, core, at, 0:64, :] = g_up[rows, cols]
                rss[TILE][t, core, at, 64:128, :] = g_down[rows, cols]
            for k in range(4):
                pl.when(t == k)(functools.partial(scatter_step, TILE + k, 0, 128))
        else:
            outs[7][t] = g_up
            outs[8][t] = g_down
        return 0

    lax.fori_loop(0, 4, feed, 0)

    def norm_two_back(rows, i):
        outb[rows, :] = low(acc[rows, :])
        xhat, inv = norm_parts(mid[rows, :])
        up = gtwo[rows, :]
        grad = cot_v[rows, :] + norm_back(xhat, inv, gain_two, up)
        cot_v[rows, :] = grad
        gf[rows, :] = low(grad)
        gains[3:4, :] = gains[3:4, :] + jnp.sum(up * xhat, axis=0, keepdims=True)

    planned("n2b")
    gains[2:8, :] = jnp.zeros((6, WIDTH), WIDE)
    by_chunk(norm_two_back)
    ol.start()
    planned("ga")
    ga[...] = low(dot_nt(gf[...], out_w()))
    planned("gout")
    g_out = low(dot_tn(att[...], gf[...]))

    def pack_square(n, grad):
        for index, core, at, _, _ in owners(SCATTER_MODES[n]):
            for t in range(4):
                rss[n][core, at, t * 16 : t * 16 + 16, :] = grad[
                    index * 16 : index * 16 + 16, t * 128 : t * 128 + 128
                ]

    if linked:
        pack_square(OUT_W, g_out)
    else:
        outs[5][...] = g_out

    def back_first(rows, i):
        planned_at("B1_%d", i)
        mask = vis[i]
        carried = hcar[i]
        carried_n = hcar_n[i]
        q, k, v, w = ([proj[n, rows, cols] for cols in pair_cols] for n in range(4))
        g = [ga[rows, cols] for cols in pair_cols]
        w2 = [two(w[p]) for p in every]
        gmix = [low(dot_nt(g[p], two(v[p]))) * mask for p in every]
        from_state = [dot_nt(g[p], sin[1, i, p]) for p in every]
        near = [dot(gmix[p], w2[p]) for p in every]
        r, pr, s = ([ref[rows, cols] for cols in pair_cols] for ref in (rtot, prob, score))
        gs = [low(near[p] + carried * from_state[p]).astype(WIDE) for p in every]
        gp = [gs[p] * r[p] for p in every]
        gscore = [pr[p] * (gp[p] - head_sum(pr[p] * gp[p])) for p in every]
        gn = [low(gscore[p] * r[p]) for p in every]
        gt = [low(-(gp[p] * pr[p] + gscore[p] * s[p]) * r[p]) for p in every]
        for p in every:
            gnum[rows, pair_cols[p]] = gn[p]
            gtot[rows, pair_cols[p]] = gt[p]
        gcross = [low(dot_nt(gn[p], w2[p])) * mask for p in every]
        from_state = [dot_nt(gn[p], sin[0, i, p]) for p in every]
        near = [dot(gcross[p], two(k[p])) for p in every]
        qn = [dot_tn(q[p] * carried_n, gn[p]) for p in every]
        gsc = [dot_tn(g[p] * carried_n, scaled[rows, pair_cols[p]]) for p in every]
        for p in every:
            gproj[0, rows, pair_cols[p]] = low(near[p] + carried * from_state[p])
            loc[0, i, p] = qn[p] * bdm[...]
            loc[1, i, p] = gsc[p] * bdm[...]
        tloc[i] = jnp.broadcast_to(
            dot(
                jnp.ones((8, CHUNK), NARROW),
                jnp.concatenate(gt, axis=1) * jnp.concatenate([carried_n] * PAIRS, axis=1),
            ),
            (8, WIDTH),
        )

    by_chunk(back_first)
    planned("send2")
    sent(exchange(STATE))
    send_states(forward[::-1], BACK)
    planned("qg")
    grad = low(dot(n1t[...], gproj[0]))
    if linked:
        pack_square(QUERY, grad)
    else:
        outs[2][...] = grad
    planned("scan2")
    carry_states(forward[::-1], BACK, 1.0 - takes_forward)
    def back_value(rows, i):
        planned_at("bv%d", i)
        mask = vist[i]
        ends = tail[i]
        w, g, sc = ([m[rows, cols] for cols in pair_cols] for m in (proj.at[3], ga, scaled))
        g2, sc2 = ([two(m[p]) for p in every] for m in (g, sc))
        mix = [low(dot_nt(w[p], sc2[p])) * mask for p in every]
        from_state = [dot_nt(w[p], sin[1, i, p]) for p in every]
        near = [dot(mix[p], g2[p]) for p in every]
        for p in every:
            gproj[2, rows, pair_cols[p]] = low(near[p] + ends * from_state[p])

    by_chunk(back_value)
    planned("wV")
    grad = low(dot(n1t[...], gproj[2]))
    if linked:
        pack_square(VALUE, grad)
    else:
        outs[4][...] = grad

    def back_second(rows, i):
        planned_at("B2_%d", i)
        mask = vist[i]
        ends = tail[i]
        wc = dot(mask[:, 0:128], gtot[rows, :]) + jnp.concatenate([ends] * PAIRS, axis=1) * tin[i, 0:1, :]
        q, k, v, w = ([proj[n, rows, cols] for cols in pair_cols] for n in range(4))
        g, sc, gn = ([ref[rows, cols] for cols in pair_cols] for ref in (ga, scaled, gnum))
        g2, sc2, gn2, q2 = ([two(m[p]) for p in every] for m in (g, sc, gn, q))
        s_query, s_grad = ([sin[n, i, p] for p in every] for n in range(2))
        gmix = [low(dot_nt(v[p], g2[p])) * mask for p in every]
        cross = [low(dot_nt(k[p], q2[p])) * mask for p in every]
        gcross = [low(dot_nt(w[p], gn2[p])) * mask for p in every]
        from_state = [dot_nt(w[p], s_query[p]) for p in every]
        near = [dot(gcross[p], q2[p]) for p in every]
        for p in every:
            gproj[1, rows, pair_cols[p]] = low(near[p] + ends * from_state[p])
        from_state = [dot(v[p], s_grad[p]) + dot(k[p], s_query[p]) for p in every]
        near = [dot(gmix[p], sc2[p]) + dot(cross[p], gn2[p]) for p in every]
        for p in every:
            gw = low(near[p] + ends * from_state[p] + wc[:, pair_cols[p]]).astype(WIDE)
            gproj[3, rows, pair_cols[p]] = low(gw * expo[rows, pair_cols[p]])
        planned_at("G%d", i)
        up = dot_nt(gproj[0, rows, :], query_w()) + dot_nt(gproj[1, rows, :], key_w())
        up = up + dot_nt(gproj[2, rows, :], value_w()) + dot_nt(gproj[3, rows, :], w_slot[...])
        xhat, inv = norm_parts(x_v[rows, :])
        ginb[rows, :] = low(cot_v[rows, :] + norm_back(xhat, inv, gain_one, up))
        gains[2:3, :] = gains[2:3, :] + jnp.sum(up * xhat, axis=0, keepdims=True)

    by_chunk(back_second)

    il = pltpu.make_async_copy(ginb, gin_ref.at[row, own_rows], lsem.at[3])
    il.start()
    planned("wK")
    for n, piece in ((1, KEY), (3, SLOT)):
        grad = low(dot(n1t[...], gproj[n]))
        if n == 3:
            grad = low(dot_nt(grad, perm[...]))
        if not linked:
            outs[2 + n if n < 3 else 6][...] = grad
        elif n < 3:
            pack_square(piece, grad)
        else:
            for index, core, at, odp, oslot in owners(SCATTER_MODES[SLOT]):
                rss[SLOT][core, at, 0:64, :] = grad[odp * 64 : odp * 64 + 64, oslot * 128 : oslot * 128 + 128]
                window = index // 8
                rss[SLOT][core, at, 64:80, :] = low(
                    jnp.concatenate(
                        [gains[2:4, window * 128 : window * 128 + 128], jnp.zeros((14, 128), WIDE)], axis=0
                    )
                )
        planned("wS" if n == 1 else "end")
    if not linked:
        outs[9][...] = gains[2:4, :]

    ol.wait()
    il.wait()
    for base in (OUT, GIN):
        for i in range(chunks):
            spread(base, i)[0].wait_send()
        spread_all(base, 0).wait()
        spread_all(base, 1).wait()
    sent(exchange(BACK))
    if linked:
        for n in range(9):
            sent([scatter_all(n, stage) for stage in range(len(SCATTER_MODES[n][0]) + 1)])


def finish_kernel(out_ref, gin_ref, small_ref, o, g, gq, gk, gv, go, gs, gu, gd, g1, g2):
    step = pl.program_id(0)
    per_row = out_ref.shape[1] // o.shape[1]
    rows = pl.ds(pl.multiple_of((step % per_row) * o.shape[1], o.shape[1]), o.shape[1])
    o[0] = out_ref[step // per_row, rows, :].astype(WIDE)
    g[0] = gin_ref[step // per_row, rows, :].astype(WIDE)

    @pl.when(pl.program_id(0) == 0)
    def _():
        base = 0
        bases = []
        for rows in PIECE_ROWS:
            bases.append(base)
            base += rows
        gs[...] = small_ref[0:64, :]
        mine = lax.axis_index("dp") * lax.axis_size("slot") + lax.axis_index("slot")
        window = small_ref[64:72, :]
        lanes = iota2((8, 128), 1)
        first = (mine % 8) * 16
        moved = jnp.concatenate(
            [
                jnp.sum(jnp.where(lanes == first + k, window, 0.0), axis=1, keepdims=True)
                for k in range(16)
            ],
            axis=1,
        )
        g1[...] = moved[0:1]
        g2[...] = moved[1:2]
        for t in range(4):
            cols = slice(t * 128, t * 128 + 128)
            for n, target in ((QUERY, gq), (KEY, gk), (VALUE, gv), (OUT_W, go)):
                target[:, cols] = small_ref[bases[n] + t * 16 : bases[n] + t * 16 + 16, :]
            gu[:, cols] = small_ref[bases[TILE + t] : bases[TILE + t] + 64, :]
            gd[:, cols] = small_ref[bases[TILE + t] + 64 : bases[TILE + t] + 128, :]


def finish(out, gin, small):
    rows, length, width = out.shape
    count = 512
    block = pl.BlockSpec((1, count, width), lambda i: (i // (length // count), i % (length // count), 0))
    here = pl.BlockSpec(memory_space=pltpu.VMEM)
    whole = lambda shape: pl.BlockSpec(shape, lambda i: (0,) * len(shape))
    shapes = [(16, width)] * 4 + [(64, 128), (64, width), (64, width), (1, 16), (1, 16)]
    shape = jax.ShapeDtypeStruct
    return pl.pallas_call(
        finish_kernel,
        grid=(rows * length // count,),
        out_shape=[shape(out.shape, WIDE)] * 2 + [shape(s, WIDE) for s in shapes],
        in_specs=[here] * 3,
        out_specs=[block, block] + [whole(s) for s in shapes],
        compiler_params=pltpu.CompilerParams(vmem_limit_bytes=32 * 1024 * 1024),
    )(*(pltpu.with_memory_space_constraint(v, pltpu.VMEM) for v in (out, gin, small)))


def run_block(linked, inputs, starts, cotangent, weights):
    rows, length, width = inputs.shape
    tokens = length // 2
    chunks = tokens // CHUNK
    vm = pltpu.VMEM
    scratch = [
        vm((tokens, width), WIDE), vm((tokens, width), WIDE),
        vm((width, width), NARROW), vm((width, width), NARROW), vm((8, width), WIDE),
        vm((tokens, width), NARROW), vm((width, tokens), NARROW),
        vm((4, tokens, width), NARROW), vm((tokens, width), WIDE),
        vm((tokens, width), WIDE), vm((tokens, width), WIDE), vm((tokens, width), WIDE),
        vm((tokens, width), NARROW), vm((tokens, width), NARROW),
        vm((tokens, width), WIDE), vm((tokens, width), WIDE),
        vm((tokens, width), NARROW), vm((width, tokens), NARROW),
        vm((tokens, width), NARROW), vm((width, tokens), NARROW), vm((tokens, width), WIDE),
        vm((tokens, width), NARROW), vm((4, tokens, width), NARROW),
        vm((tokens, width), NARROW), vm((tokens, width), NARROW),
        vm((tokens, width), NARROW), vm((tokens, width), NARROW),
        vm((chunks, CHUNK, 256), NARROW), vm((chunks, CHUNK, 256), NARROW),
        vm((chunks, CHUNK, LANES), WIDE), vm((chunks, CHUNK, LANES), WIDE), vm((chunks, CHUNK, LANES), WIDE),
        vm((chunks, CHUNK, LANES), NARROW), vm((chunks, CHUNK, LANES), NARROW),
        vm((2, chunks, PAIRS, 128, 128), WIDE), vm((2, chunks, PAIRS, 128, 128), NARROW),
        vm((chunks, 8, width), WIDE), vm((chunks, 8, width), WIDE),
        vm((CHUNK, LANES), NARROW), vm((CHUNK, LANES), NARROW), vm((CHUNK, LANES), WIDE),
        vm((2, PAIRS, 128, 128), WIDE), vm((2, 2, PAIRS, 128, 128), WIDE),
        vm((8, width), WIDE), vm((2, 8, width), WIDE),
        pltpu.SemaphoreType.DMA((52,)), pltpu.SemaphoreType.DMA((88,)), pltpu.SemaphoreType.DMA((4 if linked else 12,)),
    ]
    if linked:
        for lead in ((2, 16), (2, 16), (16,)):
            scratch += [vm((*lead, r, LANES), NARROW) for r in PIECE_ROWS[:TILE]]
            scratch += [vm((4, *lead, 128, LANES), NARROW)]
        for k in range(3):
            for r, mode in zip(PIECE_ROWS, SCATTER_MODES):
                sizes, steps = strides(mode)
                blocks = (sizes[k] - 1) * steps[k] if k < len(sizes) else 0
                scratch += [vm((blocks, r, LANES) if blocks else (1, 16, LANES), NARROW)]
    else:
        scratch += [vm((4, width, width), NARROW)] * 3
    anywhere = pl.BlockSpec(memory_space=pl.ANY)
    here = pl.BlockSpec(memory_space=pltpu.VMEM)
    shape = jax.ShapeDtypeStruct
    big = [pltpu.VMEM((rows, length, width), NARROW)] * 2
    square = (width, width)
    if linked:
        small = [pltpu.VMEM((SMALL_ROWS, LANES), WIDE)]
        weight_specs = [here] * 9
    else:
        small = [shape(square, NARROW)] * 5 + [shape((4, *square), NARROW)] * 2 + [shape((2, width), WIDE)]
        weight_specs = [anywhere] * 7 + [here] * 2
    return pl.pallas_call(
        functools.partial(block_kernel, linked, 12, 2 + len(small)),
        out_shape=big + small,
        in_specs=[anywhere, here, anywhere] + weight_specs,
        out_specs=[here] * (2 + len(small)),
        scratch_shapes=scratch,
        compiler_params=pltpu.CompilerParams(
            collective_id=0, has_side_effects=True, vmem_limit_bytes=57 * 1024 * 1024
        ),
    )(inputs, starts, cotangent, *weights)


def on_device(
    inputs, starts, w_query, w_key, w_value, w_out, w_slot, w_up, w_down, gain_attn, gain_ffn, cotangent
):
    n_dp, n_slot = lax.axis_size("dp"), lax.axis_size("slot")
    if n_dp == 8 and n_slot == 4:
        weights = (
            w_query, w_key, w_value, w_out, w_slot, w_up, w_down.T,
            gain_attn.reshape(1, -1), gain_ffn.reshape(1, -1),
        )
        out, gin, small = run_block(True, inputs, starts, cotangent, weights)
        out, gin, gq, gk, gv, go, gs, gu, gd, g1, g2 = finish(out, gin, small)
        return out, gin, gq, gk, gv, go, gs, gu, gd.T, g1.reshape(-1), g2.reshape(-1)

    def whole(v, names, axis):
        return lax.all_gather(v, names, axis=axis, tiled=True)

    both = ("dp", "slot")
    width = inputs.shape[-1]
    up = whole(whole(w_up, "dp", 0), "slot", 1).reshape(width, 4, 4, 128).transpose(2, 0, 1, 3)
    down = whole(whole(w_down, "dp", 1), "slot", 0).reshape(4, 4, 128, width).transpose(1, 3, 0, 2)
    up, down = up.reshape(4, width, width), down.reshape(4, width, width)
    weights = (
        whole(w_query, both, 0), whole(w_key, both, 0), whole(w_value, both, 0), whole(w_out, both, 0),
        whole(whole(w_slot, "dp", 0), "slot", 1), up, down,
        whole(gain_attn, both, 0).reshape(1, -1), whole(gain_ffn, both, 0).reshape(1, -1),
    )
    out, gin, gq, gk, gv, go, gs, gu, gd, gg = run_block(False, inputs, starts, cotangent, weights)

    def shared(v, names, axis):
        return lax.psum_scatter(v.astype(WIDE), names, scatter_dimension=axis, tiled=True)

    gu = gu.reshape(4, width, 4, 128).transpose(1, 2, 0, 3).reshape(width, -1)
    gd = gd.reshape(4, width, 4, 128).transpose(2, 0, 3, 1).reshape(-1, width)
    return (
        out.astype(WIDE), gin.astype(WIDE),
        shared(gq, both, 0), shared(gk, both, 0), shared(gv, both, 0), shared(go, both, 0),
        shared(shared(gs, "slot", 1), "dp", 0), shared(shared(gu, "slot", 1), "dp", 0),
        shared(shared(gd, "slot", 0), "dp", 1), shared(gg[0], both, 0), shared(gg[1], both, 0),
    )


def solution(mesh):
    every = ("dp", "slot")
    rows = P("dp", None, None)
    return jax.shard_map(
        on_device,
        mesh=mesh,
        in_specs=(
            rows, P("dp", None), P(every, None), P(every, None), P(every, None), P(every, None),
            P("dp", "slot"), P("dp", "slot"), P("slot", "dp"), P(every), P(every), rows,
        ),
        out_specs=(
            rows, rows, P(every, None), P(every, None), P(every, None), P(every, None),
            P("dp", "slot"), P("dp", "slot"), P("slot", "dp"), P(every), P(every),
        ),
        check_vma=False,
    )
```

```python
import functools

import jax
import jax.numpy as jnp
from jax import lax
from jax.experimental import pallas as pl
from jax.experimental.pallas import tpu as pltpu
from jax.sharding import PartitionSpec as P

HEADS = 8
EPSILON = 1e-05
NARROW = jnp.bfloat16
WIDE = jnp.float32
MESH = pl.DeviceIdType.MESH

WIDTH = 512
CHUNK = 128
PAIRS = 4
LANES = 128
PIECE_ROWS = (80, 64, 64, 64, 64, 128, 128, 128, 128)
SLOT, KEY, VALUE, QUERY, OUT_W, TILE = range(6)
SMALL_ROWS = sum(PIECE_ROWS)
GATHER_MODES = (
    ("ABZ", "m"), ("ABZ", "m"), ("ABZ", "m"), ("ABZ", "m"), ("ABZ", "m"),
    ("ABZ", "m"), ("AZB", "m"), ("ABZ", "m"), ("AZB", "m"),
)
SCATTER_MODES = (
    ("ABZ", "m"), ("AZB", "x"), ("ABZ", "x"), ("ABZ", "m"), ("ABZ", "m"),
    ("ABZ", "y"), ("ZAB", "x"), ("AZB", "x"), ("AZB", "x"),
)
PLAN = {
    "slot": (
        "S1", "K1", "T11", "V1", "S2", "Q1", "K2", "V2", "S3", "O1", "T01", "K3", "S4", "Q2",
        "V3", "K4", "T31", "T21",
    ),
    "val": ("O2", "V4", "T02",),
    "qry": ("Q3", "Q4", "T12",),
    "att0": ("O3",),
    "att1": ("T22",),
    "att3": ("T03",),
    "outp": ("O4",),
    "ffn0a": ("T04", "T32", "T13",),
    "ffn1a": ("T23", "T14",),
    "ffn2a": ("T24",),
    "ffn2b": ("T33", "T0.1",),
    "ffn3a": ("T1.1", "T34",),
    "ga": ("o1", "T2.1", "o0",),
    "B1_1": ("O.0", "T3.1",),
    "send2": ("o2",),
    "qg": ("o3", "p1",),
    "scan2": ("Q.0", "T2.2", "O.1",),
    "B2_0": ("V.0",),
    "B2_1": ("Q.1", "T0.2",),
    "B2_2": ("T3.2", "y1",),
    "B2_3": ("y2", "V.1",),
    "wS": ("O.2", "K.0",),
    "end": (
        "S.0", "p3", "Q.2", "T2.3", "T0.3", "K.1", "S.1", "V.2", "O.3", "Q.3", "T1.2", "y0", "K.2", "T3.3",
        "S.2", "T2.4", "V.3", "p0", "y3", "O.4", "f0", "p2", "S.3", "T1.3", "T3.4", "T0.4", "f2", "f1",
        "K.3", "f3", "V.4", "Q.4", "T1.4", "K.4", "S.4",
    ),
}
Z_ORDER = (2, 1, 3)
SEMS = 4


def dot(a, b):
    return lax.dot_general(a, b, (((1,), (0,)), ((), ())), preferred_element_type=WIDE)


def dot_nt(a, b):
    return lax.dot_general(a, b, (((1,), (1,)), ((), ())), preferred_element_type=WIDE)


def dot_tn(a, b):
    return lax.dot_general(a, b, (((0,), (0,)), ((), ())), preferred_element_type=WIDE)


def low(v):
    return v.astype(NARROW)


def iota2(shape, dim):
    return lax.broadcasted_iota(jnp.int32, shape, dim)


def row_mean(v):
    return jnp.sum(v, axis=-1, keepdims=True) * (1.0 / v.shape[-1])


def norm_parts(v):
    center = v - row_mean(v)
    inv = lax.rsqrt(row_mean(center * center) + EPSILON)
    return center * inv, inv


def norm_back(xhat, inv, gain, up):
    u = up * gain
    return (u - row_mean(u) - xhat * row_mean(u * xhat)) * inv


def strides(mode):
    sizes = [2 if axis in "AB" else 4 for axis in mode[0]]
    steps = [1]
    for size in sizes[:0:-1]:
        steps.insert(0, steps[0] * size)
    return sizes, steps


def owners(mode):
    out = []
    _, steps = strides(mode)
    for dp in range(8):
        for slot in range(4):
            z, x, y, c = dp // 2, dp % 2, slot // 2, slot % 2
            first_y = mode[1] == "y" or (mode[1] == "m" and c == 0)
            at = {"A": y if first_y else x, "B": x if first_y else y, "Z": z, "P": x * 2 + y}
            place = sum(at[axis] * step for axis, step in zip(mode[0], steps))
            out.append((dp * 4 + slot, c, place, dp, slot))
    return out


def square_of(buf, n):
    return jnp.concatenate(
        [
            jnp.concatenate([buf[core, at, t * 16 : t * 16 + 16, :] for t in range(4)], axis=1)
            for _, core, at, _, _ in owners(GATHER_MODES[n])
        ],
        axis=0,
    )


def tile_place(t, places):
    at = places[0]
    for k in range(1, 4):
        if places[k] != places[0]:
            at = jnp.where(t == k, places[k], at)
    return at


def tile_of(buf, n, first):
    spots = {}
    for each in zip(*(owners(mode) for mode in GATHER_MODES[TILE:])):
        _, core, _, dp, slot = each[0]
        spots[dp, slot] = core, tile_place(n, [at for _, _, at, _, _ in each])
    return jnp.concatenate(
        [
            jnp.concatenate(
                [buf[(n, *spots[dp, slot], slice(first, first + 64), slice(None))] for dp in range(8)], axis=0
            )
            for slot in range(4)
        ],
        axis=1,
    )


def block_kernel(linked, n_in, n_out, *refs):
    ins, outs, scr = refs[:n_in], refs[n_in : n_in + n_out], refs[n_in + n_out :]
    inputs_ref, starts_ref, cot_ref = ins[:3]
    out_ref, gin_ref = outs[:2]
    (x_v, cot_v, w_slot, perm, gains, n1, n1t, proj, expo, score, prob,
     rtot, scaled, att, mid, acc, n2, n2t, gf, gft, gtwo, ga, gproj, gnum, gtot, outb, ginb,
     vis, vist, hcar, tail, passf, hcar_n, tail_n, loc, sin, tloc, tin, bd_lo, bd_hi, bdm, xsend, xrecv, tsend, trecv,
     ssem, rsem, lsem) = scr[:48]
    rest = scr[48:]

    slot = lax.axis_index("slot")
    dp = lax.axis_index("dp")
    y, c = slot // 2, slot % 2
    row, half = y, c
    tokens = x_v.shape[0]
    chunks = tokens // CHUNK
    partner = (dp, y * 2 + (1 - c))
    y_peer = (dp, (1 - y) * 2 + c)
    if linked:
        ags, rss, rcs = (rest[6 * n : 6 * n + 6] for n in range(3))
        got_refs = [rest[18 + 9 * n : 27 + 9 * n] for n in range(3)]
        z, x = dp // 2, dp % 2
        x_peer = (z * 2 + 1 - x, slot)
        near = {
            "x": (x, y, x_peer, y_peer),
            "y": (y, x, y_peer, x_peer),
            "m": (
                y + c * (x - y),
                x + c * (y - x),
                (z * 2 + x + c * (1 - 2 * x), slot + (1 - c) * 2 * (1 - 2 * y)),
                (z * 2 + x + (1 - c) * (1 - 2 * x), slot + c * 2 * (1 - 2 * y)),
            ),
        }
        z_peers = [((((z + s) % 4) * 2 + x), slot) for s in Z_ORDER]
        diagonal = (z * 2 + 1 - x, (1 - y) * 2 + c)
        peers = [partner, x_peer, y_peer] + z_peers
    else:
        peers = [partner, y_peer]

    barrier = pltpu.get_barrier_semaphore()
    for peer in peers:
        pl.semaphore_signal(barrier, inc=1, device_id=peer, device_id_type=MESH)

    own_rows = pl.ds(pl.multiple_of(half * tokens, tokens), tokens)
    x_copy = pltpu.make_async_copy(inputs_ref.at[row, own_rows], x_v, lsem.at[0])
    cot_copy = pltpu.make_async_copy(cot_ref.at[row, own_rows], cot_v, lsem.at[1])
    x_copy.start()
    cot_copy.start()

    def remote(src, dst, at, device, send_at=None):
        return pltpu.make_async_remote_copy(
            src_ref=src, dst_ref=dst, recv_sem=rsem.at[at],
            send_sem=ssem.at[send_at if send_at is not None else at if at < SCATTER else at - SCATTER],
            device_id=device, device_id_type=MESH,
        )

    def start(copies):
        for copy in copies:
            copy.start()

    def recv(copies):
        for copy in copies:
            copy.wait_recv()

    def sent(copies):
        for copy in copies:
            copy.wait_send()

    def view(bufs, n):
        return bufs[n] if n < TILE else bufs[TILE].at[n - TILE]

    def axes(mode):
        pa, pb, dev_a, dev_b = near[mode[1]]
        known = {
            "A": (pa, [(1 - pa, dev_a)]),
            "B": (pb, [(1 - pb, dev_b)]),
            "Z": (z, [((z + s) % 4, peer) for s, peer in zip(Z_ORDER, z_peers)]),
            "P": (x * 2 + y, [((1 - x) * 2 + y, x_peer), (x * 2 + 1 - y, y_peer), ((1 - x) * 2 + 1 - y, diagonal)]),
        }
        return [(known[axis][0], step, known[axis][1]) for axis, step in zip(mode[0], strides(mode)[1])]

    def place_in(mode, upto=None):
        return sum(at * step for at, step, _ in axes(mode)[:upto])

    def gather_along(n, k):
        mode = GATHER_MODES[n]
        _, step, others = axes(mode)[k]
        part = view(ags, n).at[c, pl.ds(place_in(mode, k + 1), step)]
        return [remote(part, part, n * SEMS + k, device) for _, device in others]

    def gather_along_all(n, k):
        _, step, others = axes(GATHER_MODES[n])[k]
        part = view(ags, n).at[c, pl.ds(0, step * len(others))]
        return remote(part, part, n * SEMS + k, partner)

    def gather_across(n, k):
        mode = GATHER_MODES[n]
        _, step, others = axes(mode)[k]
        base = place_in(mode, k)
        if k == len(mode[0]) - 1:
            parts = [pl.ds(base, strides(mode)[0][k])]
        else:
            parts = [pl.ds(base + place * step, step) for place, _ in others]
        refs = [view(ags, n).at[c, part] for part in parts]
        return [remote(ref, ref, n * SEMS + 3, partner) for ref in refs]

    def gather_across_all(n):
        every_block = view(ags, n).at[c]
        return remote(every_block, every_block, n * SEMS + 3, partner)

    def gather_step(n, stage):
        count = len(GATHER_MODES[n][0])
        if stage > count:
            gather_across_all(n).wait_recv()
            return
        if stage:
            gather_along_all(n, count - stage).wait_recv()
        if stage < count:
            start(gather_along(n, count - 1 - stage))
        if stage:
            start(gather_across(n, count - stage))

    def gather_sent(n):
        sent([gather_along_all(n, k) for k in range(len(GATHER_MODES[n][0]))] + [gather_across_all(n)])

    def scatter_copies(n, stage):
        buf, at, send = view(rss, n), SCATTER + n * SEMS + stage, n * SEMS + stage
        if stage == 0:
            return [remote(buf.at[1 - c], view(rcs, n), at, partner, send)]
        mode = SCATTER_MODES[n]
        _, step, others = axes(mode)[stage - 1]
        base, got = place_in(mode, stage - 1), got_refs[stage - 1][n]
        return [
            remote(buf.at[c, pl.ds(base + place * step, step)], got.at[pl.ds(i * step, step)], at, device, send)
            for i, (place, device) in enumerate(others)
        ]

    def scatter_all(n, stage):
        if stage == 0:
            return scatter_copies(n, stage)[0]
        got = got_refs[stage - 1][n]
        part = view(rss, n).at[c, pl.ds(0, got.shape[0])]
        return remote(part, got, SCATTER + n * SEMS + stage, partner, n * SEMS + stage)

    def scatter_step(n, stage, rows):
        if stage:
            scatter_all(n, stage - 1).wait_recv()
            buf, mode = view(rss, n), SCATTER_MODES[n]
            got = view(rcs, n) if stage == 1 else got_refs[stage - 2][n]
            count = 16 if stage == 1 else axes(mode)[stage - 2][1]
            first, terms = place_in(mode, stage - 1), got.shape[0] // count

            def summed(i):
                total = buf[c, first + i].astype(WIDE)
                for k in range(terms):
                    total = total + got[k * count + i].astype(WIDE)
                return total

            if stage <= len(mode[0]):
                def step(i, _):
                    buf[c, first + i] = low(summed(i))
                    return 0

                lax.fori_loop(0, count, step, 0)
            else:
                small_ref[pl.ds(sum(PIECE_ROWS[:n]), rows), :] = summed(0)
        else:
            gather_sent(n)
        if stage <= (len(SCATTER_MODES[n][0]) if stage else 1):
            start(scatter_copies(n, stage))

    SCATTER = 9 * SEMS
    STATE = SCATTER + 9 * SEMS
    BACK, OUT, GIN = STATE + 2, STATE + 4, STATE + 10

    ins_w = ins[3:]
    if linked:
        small_ref = outs[2]
        wq, wk, wv, wo, ws, wu, wd, ga1, ga2 = ins_w
        place = [place_in(mode) for mode in GATHER_MODES]
        for n, shard in ((QUERY, wq), (KEY, wk), (VALUE, wv), (OUT_W, wo)):
            for t in range(4):
                ags[n][c, place[n], pl.ds(t * 16, 16), :] = shard[:, t * 128 : t * 128 + 128]
        ags[SLOT][c, place[SLOT], pl.ds(0, 64), :] = ws[...]
        rows16 = iota2((16, 16), 0)
        both = jnp.where(
            rows16 == 0,
            jnp.broadcast_to(ga1[...].astype(WIDE), (16, 16)),
            jnp.where(rows16 == 1, jnp.broadcast_to(ga2[...].astype(WIDE), (16, 16)), 0.0),
        )
        lane_at = ((dp * 4 + slot) % 8) * 16
        spread = jnp.where(iota2((16, 128), 1) == iota2((16, 128), 0) + lane_at, 1.0, 0.0)
        ags[SLOT][c, place[SLOT], pl.ds(64, 16), :] = low(dot(low(both), low(spread)))
        for t in range(4):
            ags[TILE][t, c, place[TILE + t], pl.ds(0, 64), :] = wu[:, t * 128 : t * 128 + 128]
            ags[TILE][t, c, place[TILE + t], pl.ds(64, 64), :] = wd[:, t * 128 : t * 128 + 128]
        query_w, key_w, value_w, out_w = (
            functools.partial(square_of, ags[n], n) for n in (QUERY, KEY, VALUE, OUT_W)
        )

        def up_w(t):
            return tile_of(ags[TILE], t, 0)

        def down_w(t):
            return tile_of(ags[TILE], t, 64)
    else:
        square_v, up_v, down_v = rest
        fw_q, fw_k, fw_v, fw_o, fw_s, fw_u, fw_d, fg1, fg2 = ins_w
        copies = [
            pltpu.make_async_copy(src, dst, lsem.at[4 + i])
            for i, (src, dst) in enumerate((
                (fw_q, square_v.at[0]), (fw_k, square_v.at[1]), (fw_v, square_v.at[2]), (fw_o, square_v.at[3]),
                (fw_s, w_slot), (fw_u, up_v), (fw_d, down_v),
            ))
        ]
        start(copies)
        for copy in copies:
            copy.wait()
        gains[0:1, :] = fg1[...].astype(WIDE)
        gains[1:2, :] = fg2[...].astype(WIDE)
        query_w, key_w, value_w, out_w = (lambda n=n: square_v[n] for n in range(4))

        def up_w(t):
            return up_v[t]

        def down_w(t):
            return down_v[t]

    pl.semaphore_wait(barrier, len(peers))

    ol = pltpu.make_async_copy(outb, out_ref.at[row, own_rows], lsem.at[2])
    results = {OUT: (outb, out_ref), GIN: (ginb, gin_ref)}

    def spread(base, i):
        source, target = results[base]
        part = pl.ds(pl.multiple_of(half * tokens + i * CHUNK, CHUNK), CHUNK)
        mine, theirs = target.at[row, part], target.at[1 - row, part]
        chunk = source.at[pl.ds(i * CHUNK, CHUNK)]
        return (
            remote(chunk, mine, base + i, y_peer),
            remote(chunk, mine, base + chunks, partner),
            remote(theirs, theirs, base + chunks + 1, partner),
        )

    def spread_all(base, k):
        mine = results[base][1].at[row, own_rows]
        return remote(mine, mine, base + chunks + k, partner)

    def spread_steps(word):
        copies = spread(OUT if word[0] in "op" else GIN, int(word[1]))
        if word[0] in "oy":
            copies[0].start()
            copies[1].start()
        else:
            copies[0].wait_recv()
            copies[2].start()

    names = {"S": SLOT, "K": KEY, "V": VALUE, "Q": QUERY, "O": OUT_W}
    names.update({"T%d" % t: TILE + t for t in range(4)})

    def planned(block):
        for word in PLAN.get(block, ()):
            if word[0] in "opyf":
                spread_steps(word)
            elif linked:
                if "." in word:
                    piece, stage = word.split(".")
                    scatter_step(names[piece], int(stage), PIECE_ROWS[names[piece]])
                else:
                    gather_step(names[word[:-1]], int(word[-1]))

    def planned_at(block, i):
        for k in range(4):
            if PLAN.get(block % k):
                pl.when(i == k)(functools.partial(planned, block % k))

    if linked:
        for n in range(9):
            gather_step(n, 0)
    lane = iota2((CHUNK, LANES), 1)
    sub = iota2((CHUNK, LANES), 0)
    bd_lo[...] = low(jnp.where(lane < 64, 1.0, 0.0))
    bd_hi[...] = low(jnp.where(lane < 64, 0.0, 1.0))
    bdm[...] = jnp.where((lane < 64) == (sub < 64), 1.0, 0.0)
    upper = low(jnp.where(sub <= lane, 1.0, 0.0))
    lower = low(jnp.where(sub >= lane, 1.0, 0.0))
    ones = jnp.ones((CHUNK, LANES), NARROW)
    for n in range(chunks):
        begin = starts_ref[:, pl.ds(pl.multiple_of(half * tokens + n * CHUNK, CHUNK), CHUNK)].astype(WIDE)
        begin = jnp.where(row == 0, begin[0:1], begin[1:2])
        begin = low(jnp.broadcast_to(begin, (CHUNK, LANES)))
        by_lane = dot(begin, upper)
        by_row = dot_nt(lower, begin)
        total = dot(begin, ones)
        same = by_row == by_lane
        v = low(jnp.where(same & (sub >= lane), 1.0, 0.0))
        vt = low(jnp.where(same & (sub <= lane), 1.0, 0.0))
        vis[n, :, 0:128] = v
        vis[n, :, 128:256] = v
        vist[n, :, 0:128] = vt
        vist[n, :, 128:256] = vt
        carried = jnp.where(by_row == 0.0, 1.0, 0.0)
        ending = jnp.where(by_row == total, 1.0, 0.0)
        hcar[n] = carried
        tail[n] = ending
        hcar_n[n] = low(carried)
        tail_n[n] = low(ending)
        passf[n] = jnp.where(total == 0.0, 1.0, 0.0)

    def perm_rows(i, _):
        r = iota2((CHUNK, WIDTH), 0) + i * CHUNK
        n = iota2((CHUNK, WIDTH), 1)
        source = ((n >> 4) & 3) * 128 + (n & 15) * 8 + (n >> 6)
        perm[pl.ds(pl.multiple_of(i * CHUNK, CHUNK), CHUNK), :] = low(jnp.where(r == source, 1.0, 0.0))
        return 0

    lax.fori_loop(0, WIDTH // CHUNK, perm_rows, 0)
    x_copy.wait()

    def by_chunk(body):
        def step(i, _):
            body(pl.ds(pl.multiple_of(i * CHUNK, CHUNK), CHUNK), i)
            return 0

        lax.fori_loop(0, chunks, step, 0)

    def norm_one(rows, i):
        gtwo[rows, :], _ = norm_parts(x_v[rows, :])

    by_chunk(norm_one)

    if linked:
        planned("slot")
        for index, core, at, odp, oslot in owners(GATHER_MODES[SLOT]):
            w_slot[odp * 64 : odp * 64 + 64, oslot * 128 : oslot * 128 + 128] = ags[SLOT][core, at, 0:64, :]
        for window in range(4):
            total = jnp.zeros((16, 128), WIDE)
            for index, core, at, _, _ in owners(GATHER_MODES[SLOT]):
                if index // 8 == window:
                    total = total + ags[SLOT][core, at, 64:80, :].astype(WIDE)
            gains[0:8, window * 128 : window * 128 + 128] = total[0:8]
    w_slot[...] = low(dot(w_slot[...], perm[...]))

    gain_one = gains[0:1, :]
    gain_two = gains[1:2, :]

    n1[...] = low(gtwo[...] * gain_one)
    expo[...] = jnp.exp(dot(n1[...], w_slot[...]))
    proj[3] = low(expo[...])
    planned("key")
    proj[1] = low(dot(n1[...], key_w()))
    planned("val")
    proj[2] = low(dot(n1[...], value_w()))
    def two(v):
        return jnp.concatenate([v * bd_lo[...], v * bd_hi[...]], axis=0)

    every = range(PAIRS)
    pair_cols = [slice(p * 128, p * 128 + 128) for p in every]

    def local_states(rows, i):
        w_tail = proj[3, rows, :]
        tloc[i] = jnp.broadcast_to(
            dot(jnp.ones((8, CHUNK), NARROW), w_tail * jnp.concatenate([tail_n[i]] * PAIRS, axis=1)),
            (8, WIDTH),
        )
        w = [proj[3, rows, cols] for cols in pair_cols]
        k_tail = [proj[1, rows, cols] * tail_n[i] for cols in pair_cols]
        v = [proj[2, rows, cols] for cols in pair_cols]
        kw = [dot_tn(k_tail[p], w[p]) for p in every]
        wv = [dot_tn(w[p] * tail_n[i], v[p]) for p in every]
        for p in every:
            loc[0, i, p] = kw[p] * bdm[...]
            loc[1, i, p] = wv[p] * bdm[...]

    planned("loc")
    by_chunk(local_states)

    def scan_states(order, initial, t_initial, keep):
        def one(kind, p):
            state = initial(kind, p)
            for i in order:
                if keep:
                    sin[kind, i, p] = low(state)
                state = loc[kind, i, p] + passf[i] * state
            if not keep:
                xsend[kind, p] = state

        def step(k, _):
            one(k // PAIRS, k % PAIRS)
            return 0

        lax.fori_loop(0, 2 * PAIRS, step, 0)
        state = t_initial()
        for i in order:
            if keep:
                tin[i] = state
            state = tloc[i] + jnp.concatenate([passf[i, 0:8, :]] * PAIRS, axis=1) * state
        if not keep:
            tsend[...] = state

    def exchange(at):
        return [remote(xsend, xrecv.at[(at - STATE) // 2], at, partner), remote(tsend, trecv.at[(at - STATE) // 2], at + 1, partner)]

    def send_states(order, at):
        scan_states(order, lambda k, p: jnp.zeros((128, 128), WIDE), lambda: jnp.zeros((8, WIDTH), WIDE), False)
        start(exchange(at))

    def carry_states(order, at, takes):
        n = (at - STATE) // 2
        recv(exchange(at))
        scan_states(order, lambda k, p: xrecv[n, k, p] * takes, lambda: trecv[n] * takes, True)

    forward = list(range(chunks))
    takes_forward = half.astype(WIDE)
    send_states(forward, STATE)
    planned("qry")
    proj[0] = low(dot(n1[...], query_w()))
    n1t[...] = n1[...].T
    planned("scan")
    carry_states(forward, STATE, takes_forward)
    first_half = iota2((CHUNK, LANES), 1) < 64

    def over_heads(lo_part, hi_part):
        return jnp.where(first_half, lo_part, hi_part)

    def head_max(v):
        return over_heads(
            jnp.max(jnp.where(first_half, v, -jnp.inf), axis=-1, keepdims=True),
            jnp.max(jnp.where(first_half, -jnp.inf, v), axis=-1, keepdims=True),
        )

    def head_sum(v):
        return over_heads(
            jnp.sum(jnp.where(first_half, v, 0.0), axis=-1, keepdims=True),
            jnp.sum(jnp.where(first_half, 0.0, v), axis=-1, keepdims=True),
        )

    def attend(rows, i):
        planned_at("att%d", i)
        mask = vis[i]
        carried = hcar[i]
        totals = dot(mask[:, 0:128], proj[3, rows, :]) + jnp.concatenate([carried] * PAIRS, axis=1) * tin[i, 0:1, :]
        rtot[rows, :] = 1.0 / totals
        q, k, v, w = ([proj[n, rows, cols] for cols in pair_cols] for n in range(4))
        w2 = [two(w[p]) for p in every]
        cross = [low(dot_nt(q[p], two(k[p]))) * mask for p in every]
        from_state = [dot(q[p], sin[0, i, p]) for p in every]
        numer = [dot(cross[p], w2[p]) for p in every]
        r = [rtot[rows, cols] for cols in pair_cols]
        s = [(numer[p] + carried * from_state[p]) * r[p] for p in every]
        e = [jnp.exp(s[p] - head_max(s[p])) for p in every]
        pr = [e[p] / head_sum(e[p]) for p in every]
        sc = [low(pr[p] * r[p]) for p in every]
        for p in every:
            score[rows, pair_cols[p]] = s[p]
            prob[rows, pair_cols[p]] = pr[p]
            scaled[rows, pair_cols[p]] = sc[p]
        mix = [low(dot_nt(sc[p], w2[p])) * mask for p in every]
        from_state = [dot(sc[p], sin[1, i, p]) for p in every]
        near = [dot(mix[p], two(v[p])) for p in every]
        for p in every:
            att[rows, pair_cols[p]] = low(near[p] + carried * from_state[p])

    by_chunk(attend)

    planned("outp")
    mid[...] = x_v[...] + dot(att[...], out_w())
    acc[...] = mid[...]
    cot_copy.wait()

    def norm_two(rows, i):
        xhat, _ = norm_parts(mid[rows, :])
        n2[rows, :] = low(xhat * gain_two)
        gf[rows, :] = low(cot_v[rows, :])
        gtwo[rows, :] = jnp.zeros((CHUNK, WIDTH), WIDE)

    by_chunk(norm_two)
    n2t[...] = n2[...].T
    gft[...] = gf[...].T

    def feed(t, _):
        planned_at("ffn%da", t)
        hidden = dot(n2[...], up_w(t))
        cdf = 0.5 * (1.0 + lax.erf(hidden * 0.7071067811865476))
        active = low(hidden * cdf)
        slope = cdf + hidden * (jnp.exp(-0.5 * hidden * hidden) * 0.3989422804014327)
        grad_hidden = low(dot(gf[...], down_w(t)) * slope)
        planned_at("ffn%db", t)
        acc[...] += dot_nt(active, down_w(t))
        gtwo[...] += dot_nt(grad_hidden, up_w(t))
        g_up = low(dot(n2t[...], grad_hidden))
        g_down = low(dot(gft[...], active))
        if linked:
            for (_, core, at, odp, oslot), *later in zip(*(owners(mode) for mode in SCATTER_MODES[TILE:])):
                at = tile_place(t, [at] + [other[2] for other in later])
                rows, cols = slice(odp * 64, odp * 64 + 64), slice(oslot * 128, oslot * 128 + 128)
                rss[TILE][t, core, at, 0:64, :] = g_up[rows, cols]
                rss[TILE][t, core, at, 64:128, :] = g_down[rows, cols]
            for k in range(4):
                pl.when(t == k)(functools.partial(scatter_step, TILE + k, 0, 128))
        else:
            outs[7][t] = g_up
            outs[8][t] = g_down
        return 0

    lax.fori_loop(0, 4, feed, 0)

    def norm_two_back(rows, i):
        outb[rows, :] = low(acc[rows, :])
        xhat, inv = norm_parts(mid[rows, :])
        up = gtwo[rows, :]
        grad = cot_v[rows, :] + norm_back(xhat, inv, gain_two, up)
        cot_v[rows, :] = grad
        gf[rows, :] = low(grad)
        gains[3:4, :] = gains[3:4, :] + jnp.sum(up * xhat, axis=0, keepdims=True)

    planned("n2b")
    gains[2:8, :] = jnp.zeros((6, WIDTH), WIDE)
    by_chunk(norm_two_back)
    ol.start()
    planned("ga")
    ga[...] = low(dot_nt(gf[...], out_w()))
    planned("gout")
    g_out = low(dot_tn(att[...], gf[...]))

    def pack_square(n, grad):
        for index, core, at, _, _ in owners(SCATTER_MODES[n]):
            for t in range(4):
                rss[n][core, at, t * 16 : t * 16 + 16, :] = grad[
                    index * 16 : index * 16 + 16, t * 128 : t * 128 + 128
                ]

    if linked:
        pack_square(OUT_W, g_out)
    else:
        outs[5][...] = g_out

    def back_first(rows, i):
        planned_at("B1_%d", i)
        mask = vis[i]
        carried = hcar[i]
        carried_n = hcar_n[i]
        q, k, v, w = ([proj[n, rows, cols] for cols in pair_cols] for n in range(4))
        g = [ga[rows, cols] for cols in pair_cols]
        w2 = [two(w[p]) for p in every]
        gmix = [low(dot_nt(g[p], two(v[p]))) * mask for p in every]
        from_state = [dot_nt(g[p], sin[1, i, p]) for p in every]
        near = [dot(gmix[p], w2[p]) for p in every]
        r, pr, s = ([ref[rows, cols] for cols in pair_cols] for ref in (rtot, prob, score))
        gs = [low(near[p] + carried * from_state[p]).astype(WIDE) for p in every]
        gp = [gs[p] * r[p] for p in every]
        gscore = [pr[p] * (gp[p] - head_sum(pr[p] * gp[p])) for p in every]
        gn = [low(gscore[p] * r[p]) for p in every]
        gt = [low(-(gp[p] * pr[p] + gscore[p] * s[p]) * r[p]) for p in every]
        for p in every:
            gnum[rows, pair_cols[p]] = gn[p]
            gtot[rows, pair_cols[p]] = gt[p]
        gcross = [low(dot_nt(gn[p], w2[p])) * mask for p in every]
        from_state = [dot_nt(gn[p], sin[0, i, p]) for p in every]
        near = [dot(gcross[p], two(k[p])) for p in every]
        qn = [dot_tn(q[p] * carried_n, gn[p]) for p in every]
        gsc = [dot_tn(g[p] * carried_n, scaled[rows, pair_cols[p]]) for p in every]
        for p in every:
            gproj[0, rows, pair_cols[p]] = low(near[p] + carried * from_state[p])
            loc[0, i, p] = qn[p] * bdm[...]
            loc[1, i, p] = gsc[p] * bdm[...]
        tloc[i] = jnp.broadcast_to(
            dot(
                jnp.ones((8, CHUNK), NARROW),
                jnp.concatenate(gt, axis=1) * jnp.concatenate([carried_n] * PAIRS, axis=1),
            ),
            (8, WIDTH),
        )

    by_chunk(back_first)
    planned("send2")
    sent(exchange(STATE))
    send_states(forward[::-1], BACK)
    planned("qg")
    grad = low(dot(n1t[...], gproj[0]))
    if linked:
        pack_square(QUERY, grad)
    else:
        outs[2][...] = grad
    planned("scan2")
    carry_states(forward[::-1], BACK, 1.0 - takes_forward)
    def back_value(rows, i):
        planned_at("bv%d", i)
        mask = vist[i]
        ends = tail[i]
        w, g, sc = ([m[rows, cols] for cols in pair_cols] for m in (proj.at[3], ga, scaled))
        g2, sc2 = ([two(m[p]) for p in every] for m in (g, sc))
        mix = [low(dot_nt(w[p], sc2[p])) * mask for p in every]
        from_state = [dot_nt(w[p], sin[1, i, p]) for p in every]
        near = [dot(mix[p], g2[p]) for p in every]
        for p in every:
            gproj[2, rows, pair_cols[p]] = low(near[p] + ends * from_state[p])

    by_chunk(back_value)
    planned("wV")
    grad = low(dot(n1t[...], gproj[2]))
    if linked:
        pack_square(VALUE, grad)
    else:
        outs[4][...] = grad

    def back_second(rows, i):
        planned_at("B2_%d", i)
        mask = vist[i]
        ends = tail[i]
        wc = dot(mask[:, 0:128], gtot[rows, :]) + jnp.concatenate([ends] * PAIRS, axis=1) * tin[i, 0:1, :]
        q, k, v, w = ([proj[n, rows, cols] for cols in pair_cols] for n in range(4))
        g, sc, gn = ([ref[rows, cols] for cols in pair_cols] for ref in (ga, scaled, gnum))
        g2, sc2, gn2, q2 = ([two(m[p]) for p in every] for m in (g, sc, gn, q))
        s_query, s_grad = ([sin[n, i, p] for p in every] for n in range(2))
        gmix = [low(dot_nt(v[p], g2[p])) * mask for p in every]
        cross = [low(dot_nt(k[p], q2[p])) * mask for p in every]
        gcross = [low(dot_nt(w[p], gn2[p])) * mask for p in every]
        from_state = [dot_nt(w[p], s_query[p]) for p in every]
        near = [dot(gcross[p], q2[p]) for p in every]
        for p in every:
            gproj[1, rows, pair_cols[p]] = low(near[p] + ends * from_state[p])
        from_state = [dot(v[p], s_grad[p]) + dot(k[p], s_query[p]) for p in every]
        near = [dot(gmix[p], sc2[p]) + dot(cross[p], gn2[p]) for p in every]
        for p in every:
            gw = low(near[p] + ends * from_state[p] + wc[:, pair_cols[p]]).astype(WIDE)
            gproj[3, rows, pair_cols[p]] = low(gw * expo[rows, pair_cols[p]])
        planned_at("G%d", i)
        up = dot_nt(gproj[0, rows, :], query_w()) + dot_nt(gproj[1, rows, :], key_w())
        up = up + dot_nt(gproj[2, rows, :], value_w()) + dot_nt(gproj[3, rows, :], w_slot[...])
        xhat, inv = norm_parts(x_v[rows, :])
        ginb[rows, :] = low(cot_v[rows, :] + norm_back(xhat, inv, gain_one, up))
        gains[2:3, :] = gains[2:3, :] + jnp.sum(up * xhat, axis=0, keepdims=True)

    by_chunk(back_second)

    il = pltpu.make_async_copy(ginb, gin_ref.at[row, own_rows], lsem.at[3])
    il.start()
    planned("wK")
    for n, piece in ((1, KEY), (3, SLOT)):
        grad = low(dot(n1t[...], gproj[n]))
        if n == 3:
            grad = low(dot_nt(grad, perm[...]))
        if not linked:
            outs[2 + n if n < 3 else 6][...] = grad
        elif n < 3:
            pack_square(piece, grad)
        else:
            for index, core, at, odp, oslot in owners(SCATTER_MODES[SLOT]):
                rss[SLOT][core, at, 0:64, :] = grad[odp * 64 : odp * 64 + 64, oslot * 128 : oslot * 128 + 128]
                window = index // 8
                rss[SLOT][core, at, 64:80, :] = low(
                    jnp.concatenate(
                        [gains[2:4, window * 128 : window * 128 + 128], jnp.zeros((14, 128), WIDE)], axis=0
                    )
                )
        planned("wS" if n == 1 else "end")
    if not linked:
        outs[9][...] = gains[2:4, :]

    ol.wait()
    il.wait()
    for base in (OUT, GIN):
        for i in range(chunks):
            spread(base, i)[0].wait_send()
        spread_all(base, 0).wait()
        spread_all(base, 1).wait()
    sent(exchange(BACK))
    if linked:
        for n in range(9):
            sent([scatter_all(n, stage) for stage in range(len(SCATTER_MODES[n][0]) + 1)])


def finish_kernel(out_ref, gin_ref, small_ref, o, g, gq, gk, gv, go, gs, gu, gd, g1, g2):
    step = pl.program_id(0)
    per_row = out_ref.shape[1] // o.shape[1]
    rows = pl.ds(pl.multiple_of((step % per_row) * o.shape[1], o.shape[1]), o.shape[1])
    o[0] = out_ref[step // per_row, rows, :].astype(WIDE)
    g[0] = gin_ref[step // per_row, rows, :].astype(WIDE)

    @pl.when(pl.program_id(0) == 0)
    def _():
        base = 0
        bases = []
        for rows in PIECE_ROWS:
            bases.append(base)
            base += rows
        gs[...] = small_ref[0:64, :]
        mine = lax.axis_index("dp") * lax.axis_size("slot") + lax.axis_index("slot")
        window = small_ref[64:72, :]
        lanes = iota2((8, 128), 1)
        first = (mine % 8) * 16
        moved = jnp.concatenate(
            [
                jnp.sum(jnp.where(lanes == first + k, window, 0.0), axis=1, keepdims=True)
                for k in range(16)
            ],
            axis=1,
        )
        g1[...] = moved[0:1]
        g2[...] = moved[1:2]
        for t in range(4):
            cols = slice(t * 128, t * 128 + 128)
            for n, target in ((QUERY, gq), (KEY, gk), (VALUE, gv), (OUT_W, go)):
                target[:, cols] = small_ref[bases[n] + t * 16 : bases[n] + t * 16 + 16, :]
            gu[:, cols] = small_ref[bases[TILE + t] : bases[TILE + t] + 64, :]
            gd[:, cols] = small_ref[bases[TILE + t] + 64 : bases[TILE + t] + 128, :]


def finish(out, gin, small):
    rows, length, width = out.shape
    count = 512
    block = pl.BlockSpec((1, count, width), lambda i: (i // (length // count), i % (length // count), 0))
    here = pl.BlockSpec(memory_space=pltpu.VMEM)
    whole = lambda shape: pl.BlockSpec(shape, lambda i: (0,) * len(shape))
    shapes = [(16, width)] * 4 + [(64, 128), (64, width), (64, width), (1, 16), (1, 16)]
    shape = jax.ShapeDtypeStruct
    return pl.pallas_call(
        finish_kernel,
        grid=(rows * length // count,),
        out_shape=[shape(out.shape, WIDE)] * 2 + [shape(s, WIDE) for s in shapes],
        in_specs=[here] * 3,
        out_specs=[block, block] + [whole(s) for s in shapes],
        compiler_params=pltpu.CompilerParams(vmem_limit_bytes=32 * 1024 * 1024),
    )(*(pltpu.with_memory_space_constraint(v, pltpu.VMEM) for v in (out, gin, small)))


def run_block(linked, inputs, starts, cotangent, weights):
    rows, length, width = inputs.shape
    tokens = length // 2
    chunks = tokens // CHUNK
    vm = pltpu.VMEM
    scratch = [
        vm((tokens, width), WIDE), vm((tokens, width), WIDE),
        vm((width, width), NARROW), vm((width, width), NARROW), vm((8, width), WIDE),
        vm((tokens, width), NARROW), vm((width, tokens), NARROW),
        vm((4, tokens, width), NARROW), vm((tokens, width), WIDE),
        vm((tokens, width), WIDE), vm((tokens, width), WIDE), vm((tokens, width), WIDE),
        vm((tokens, width), NARROW), vm((tokens, width), NARROW),
        vm((tokens, width), WIDE), vm((tokens, width), WIDE),
        vm((tokens, width), NARROW), vm((width, tokens), NARROW),
        vm((tokens, width), NARROW), vm((width, tokens), NARROW), vm((tokens, width), WIDE),
        vm((tokens, width), NARROW), vm((4, tokens, width), NARROW),
        vm((tokens, width), NARROW), vm((tokens, width), NARROW),
        vm((tokens, width), NARROW), vm((tokens, width), NARROW),
        vm((chunks, CHUNK, 256), NARROW), vm((chunks, CHUNK, 256), NARROW),
        vm((chunks, CHUNK, LANES), WIDE), vm((chunks, CHUNK, LANES), WIDE), vm((chunks, CHUNK, LANES), WIDE),
        vm((chunks, CHUNK, LANES), NARROW), vm((chunks, CHUNK, LANES), NARROW),
        vm((2, chunks, PAIRS, 128, 128), WIDE), vm((2, chunks, PAIRS, 128, 128), NARROW),
        vm((chunks, 8, width), WIDE), vm((chunks, 8, width), WIDE),
        vm((CHUNK, LANES), NARROW), vm((CHUNK, LANES), NARROW), vm((CHUNK, LANES), WIDE),
        vm((2, PAIRS, 128, 128), WIDE), vm((2, 2, PAIRS, 128, 128), WIDE),
        vm((8, width), WIDE), vm((2, 8, width), WIDE),
        pltpu.SemaphoreType.DMA((52,)), pltpu.SemaphoreType.DMA((88,)), pltpu.SemaphoreType.DMA((4 if linked else 12,)),
    ]
    if linked:
        for lead in ((2, 16), (2, 16), (16,)):
            scratch += [vm((*lead, r, LANES), NARROW) for r in PIECE_ROWS[:TILE]]
            scratch += [vm((4, *lead, 128, LANES), NARROW)]
        for k in range(3):
            for r, mode in zip(PIECE_ROWS, SCATTER_MODES):
                sizes, steps = strides(mode)
                blocks = (sizes[k] - 1) * steps[k] if k < len(sizes) else 0
                scratch += [vm((blocks, r, LANES) if blocks else (1, 16, LANES), NARROW)]
    else:
        scratch += [vm((4, width, width), NARROW)] * 3
    anywhere = pl.BlockSpec(memory_space=pl.ANY)
    here = pl.BlockSpec(memory_space=pltpu.VMEM)
    shape = jax.ShapeDtypeStruct
    big = [pltpu.VMEM((rows, length, width), NARROW)] * 2
    square = (width, width)
    if linked:
        small = [pltpu.VMEM((SMALL_ROWS, LANES), WIDE)]
        weight_specs = [here] * 9
    else:
        small = [shape(square, NARROW)] * 5 + [shape((4, *square), NARROW)] * 2 + [shape((2, width), WIDE)]
        weight_specs = [anywhere] * 7 + [here] * 2
    return pl.pallas_call(
        functools.partial(block_kernel, linked, 12, 2 + len(small)),
        out_shape=big + small,
        in_specs=[anywhere, here, anywhere] + weight_specs,
        out_specs=[here] * (2 + len(small)),
        scratch_shapes=scratch,
        compiler_params=pltpu.CompilerParams(
            collective_id=0, has_side_effects=True, vmem_limit_bytes=57 * 1024 * 1024
        ),
    )(inputs, starts, cotangent, *weights)


def on_device(
    inputs, starts, w_query, w_key, w_value, w_out, w_slot, w_up, w_down, gain_attn, gain_ffn, cotangent
):
    n_dp, n_slot = lax.axis_size("dp"), lax.axis_size("slot")
    if n_dp == 8 and n_slot == 4:
        weights = (
            w_query, w_key, w_value, w_out, w_slot, w_up, w_down.T,
            gain_attn.reshape(1, -1), gain_ffn.reshape(1, -1),
        )
        out, gin, small = run_block(True, inputs, starts, cotangent, weights)
        out, gin, gq, gk, gv, go, gs, gu, gd, g1, g2 = finish(out, gin, small)
        return out, gin, gq, gk, gv, go, gs, gu, gd.T, g1.reshape(-1), g2.reshape(-1)

    def whole(v, names, axis):
        return lax.all_gather(v, names, axis=axis, tiled=True)

    both = ("dp", "slot")
    width = inputs.shape[-1]
    up = whole(whole(w_up, "dp", 0), "slot", 1).reshape(width, 4, 4, 128).transpose(2, 0, 1, 3)
    down = whole(whole(w_down, "dp", 1), "slot", 0).reshape(4, 4, 128, width).transpose(1, 3, 0, 2)
    up, down = up.reshape(4, width, width), down.reshape(4, width, width)
    weights = (
        whole(w_query, both, 0), whole(w_key, both, 0), whole(w_value, both, 0), whole(w_out, both, 0),
        whole(whole(w_slot, "dp", 0), "slot", 1), up, down,
        whole(gain_attn, both, 0).reshape(1, -1), whole(gain_ffn, both, 0).reshape(1, -1),
    )
    out, gin, gq, gk, gv, go, gs, gu, gd, gg = run_block(False, inputs, starts, cotangent, weights)

    def shared(v, names, axis):
        return lax.psum_scatter(v.astype(WIDE), names, scatter_dimension=axis, tiled=True)

    gu = gu.reshape(4, width, 4, 128).transpose(1, 2, 0, 3).reshape(width, -1)
    gd = gd.reshape(4, width, 4, 128).transpose(2, 0, 3, 1).reshape(-1, width)
    return (
        out.astype(WIDE), gin.astype(WIDE),
        shared(gq, both, 0), shared(gk, both, 0), shared(gv, both, 0), shared(go, both, 0),
        shared(shared(gs, "slot", 1), "dp", 0), shared(shared(gu, "slot", 1), "dp", 0),
        shared(shared(gd, "slot", 0), "dp", 1), shared(gg[0], both, 0), shared(gg[1], both, 0),
    )


def solution(mesh):
    every = ("dp", "slot")
    rows = P("dp", None, None)
    return jax.shard_map(
        on_device,
        mesh=mesh,
        in_specs=(
            rows, P("dp", None), P(every, None), P(every, None), P(every, None), P(every, None),
            P("dp", "slot"), P("dp", "slot"), P("slot", "dp"), P(every), P(every), rows,
        ),
        out_specs=(
            rows, rows, P(every, None), P(every, None), P(every, None), P(every, None),
            P("dp", "slot"), P("dp", "slot"), P("slot", "dp"), P(every), P(every),
        ),
        check_vma=False,
    )
```
